32 devices in a mesh: feat: 4 (over y, core), ex: 8 (over z, x).
Axes of the slice: x: 2, y: 2, z: 4, core: 2. Of those that a mesh axis runs over, the one named last changes fastest.
Arguments:
- gradients: bfloat16 [8, 67108864], P('ex', 'feat'), may hold values from -6 to 6
- sign_words: int32 [4194304], P('feat'), may hold values from 0 to 65535
- sub_index: int32 [8192], replicated, may hold values from 0 to 67108863, as said below
- test_sketch: bfloat16 [1024, 8192], P('ex'), may hold values from -6 to 6
Outputs:
- scores: float32 [8, 1024], P('ex')
The draws below stay inside these ranges and needn't reach their ends.
Inputs may be any that keep to these rules, and one draw needn't show every extreme that they name: `sub_index`: strictly increasing; entry k lies in [k * 8192, (k + 1) * 8192); the first entry is 0 and the last is 67108863.
All inputs are finite; a program needn't handle non-finite values.
Results may differ from the reference program's by a relative error of at most 0.0051.
Values may be sent and summed in bfloat16 or wider, within the bound.
No kernel may reach another device: no remote copies, remote signals or barrier semaphores. Data moves between devices by JAX's collectives and lax.ppermute only.
A program may use at most 832 MiB of HBM per device.

```python
import jax
import jax.numpy as jnp
from jax import lax

NHIGH = 1024
NMID = 256
NLOW = 256
K = 8192
TESTS = 1024
F = 67108864
EXAMPLES = 8


def draw_sub_index(key, part):
    stride = NHIGH * NMID * NLOW // K
    offsets = jax.random.randint(key, (K,), 0, stride, dtype=jnp.int32)
    offsets = offsets.at[0].set(0)
    offsets = offsets.at[K - 1].set(stride - 1)
    return jnp.arange(K, dtype=jnp.int32) * stride + offsets


def place_ends(drawn, key, least, largest):
    dims = drawn.shape
    spot = [jax.random.randint(jax.random.fold_in(key, axis), (), 0, dims[axis]) for axis in range(len(dims))]
    drawn = drawn.at[tuple(spot)].set(least)
    longest = dims.index(max(dims))
    spot[longest] = (spot[longest] + 1) % dims[longest]
    return drawn.at[tuple(spot)].set(largest)


def steps_of(own_key, shape, shards, low, top_value):
    level, own = 1.0, jax.random.fold_in(own_key, 6)
    for dim, shards_of in shards:
        draws = jnp.exp(jax.random.uniform(jax.random.fold_in(own, dim), (shards_of,), jnp.float32, low / len(shards), top_value / len(shards)))
        level = level * jnp.repeat(draws, shape[dim] // shards_of).reshape([-1 if axis == dim else 1 for axis in range(len(shape))])
    return level


def centred(own_key, extent, width, most, shards=(), kind=jnp.bfloat16):
    gain = steps_of(own_key, extent, shards, -0.22, 0.18) if shards else 1.0
    drawn = jax.random.normal(own_key, extent, jnp.float32) * width * gain
    return jnp.minimum(jnp.maximum(drawn, -most), most).astype(kind)


def setup_inputs(seed: int = 0) -> dict:
    key_list = jax.random.split(jax.random.key(seed), 5)
    return {
        "gradients": centred(key_list[0], (EXAMPLES, F), 1.0, 6.0, ((0, 8), (1, 4))),
        "sign_words": place_ends(jax.random.randint(key_list[1], (F // 16,), 0, 65536), jax.random.fold_in(key_list[1], 1), 0, 65535).astype(jnp.int32),
        "sub_index": draw_sub_index(jax.random.fold_in(key_list[4], 71), 0),
        "test_sketch": centred(key_list[3], (TESTS, K), 1.0, 6.0, ((0, 8),)),
    }


def parity_sign(left, right, nbits):
    common = jnp.bitwise_and(left, right)
    total = jnp.zeros_like(common)
    for position in range(nbits):
        total = total + jnp.bitwise_and(jnp.right_shift(common, position), 1)
    return (1 - 2 * (total % 2)).astype(jnp.float32)


def hadamard_table(order):
    places = jnp.arange(order, dtype=jnp.int32)
    return parity_sign(places[:, None], places[None, :], order.bit_length() - 1)


def reference(gradients, sign_words, sub_index, test_sketch):
    total_features = NHIGH * NMID * NLOW
    shifts = jnp.arange(16, dtype=jnp.int32)
    flags = jnp.bitwise_and(jnp.right_shift(sign_words.astype(jnp.int32)[:, None], shifts[None, :]), 1).reshape(total_features)
    signs = (2 * flags - 1).astype(jnp.bfloat16)
    low_table = hadamard_table(NLOW)
    mid_table = hadamard_table(NMID)
    high_of = (sub_index // (NMID * NLOW)).astype(jnp.int32)
    col_of = (sub_index % (NMID * NLOW)).astype(jnp.int32)
    rows = jnp.arange(NHIGH, dtype=jnp.int32)
    select = parity_sign(rows[:, None], high_of[None, :], NHIGH.bit_length() - 1)
    feature_scale = float(total_features) ** -0.5

    def one_example(grad):
        signed = (grad * signs).reshape(NHIGH, NMID, NLOW)
        first = jnp.einsum("hml,pl->hmp", signed.astype(jnp.float32), low_table).astype(jnp.bfloat16)
        second = jnp.einsum("hml,qm->hql", first.astype(jnp.float32), mid_table).astype(jnp.bfloat16)
        second = second.reshape(NHIGH, NMID * NLOW)
        picked = jnp.take(second, col_of, axis=1).astype(jnp.float32)
        return jnp.sum(select * picked, axis=0) * feature_scale

    sketch = lax.map(one_example, gradients)
    sketch_rounded = sketch.astype(jnp.bfloat16)
    scores = jnp.einsum("ek,tk->et", sketch_rounded.astype(jnp.float32), test_sketch.astype(jnp.float32))
    return scores * (float(K) ** -0.5)
```

```python
import functools

import jax
import jax.numpy as jnp
from jax import lax
from jax.experimental import pallas as pl
from jax.experimental.pallas import tpu as pltpu
from jax.sharding import PartitionSpec as P

NMID = 256
NLOW = 256
TOP = 8
GROUP = 8
STEP = 4
SLOTS = 3
LANES = 128


def odd_common_bits(left, right):
    return jnp.bitwise_and(lax.population_count(jnp.bitwise_and(left, right)), 1) == 1


def iota(shape, axis):
    return lax.broadcasted_iota(jnp.int32, shape, axis)


def sketch_kernel(
    place_ref, grads, words, sub_ref, out_ref,
    xbuf, wbuf, wpair, table, ybuf, tbuf, picks, acc, sems, wsem,
    *, high_dev, scale,
):
    high_parts = out_ref.shape[0] * LANES // TOP // high_dev
    rest = NMID // TOP
    chunks = rest // GROUP
    steps = rest // STEP
    low_group = high_dev // 8
    points = high_parts * low_group
    depth = GROUP * low_group
    blocks = high_dev // 16 // 8
    copies = high_dev // (STEP * 8)
    half = LANES // 16

    def grad_copy(step, h):
        return pltpu.make_async_copy(
            grads.at[h, :, pl.ds(step * (2 * STEP), 2 * STEP)],
            xbuf.at[lax.rem(step, SLOTS), :, :, :, pl.ds(pl.multiple_of(h * LANES, LANES), LANES)],
            sems.at[lax.rem(step, SLOTS)],
        )

    def wait_step(step):
        slot = lax.rem(step, SLOTS)
        pltpu.make_async_copy(xbuf.at[slot], xbuf.at[slot], sems.at[slot]).wait()

    word_copy = pltpu.make_async_copy(words, wbuf, wsem)
    word_copy.start()

    @pl.loop(0, 2 * high_dev // 8)
    def _(n):
        for i in range(8):
            h = n * 8 + i
            step = h // high_dev
            grad_copy(step, h - step * high_dev).start()

    table[...] = jnp.where(
        odd_common_bits(iota(table.shape, 0), iota(table.shape, 1)), -1.0, 1.0
    ).astype(jnp.bfloat16)
    out_ref[...] = jnp.zeros_like(out_ref)
    lane8 = iota((8, LANES), 1)
    sub8 = iota((8, LANES), 0)

    def entry_columns(j, g):
        columns = []
        for hi in range(high_parts):
            for v in range(low_group // 8):
                row = (hi * high_dev + g * low_group) // 16 + v // 2
                line = jnp.broadcast_to(sub_ref[pl.ds(row, 1), :], (8, LANES))
                spot = ((v % 2) * 8 + sub8) * TOP + j
                columns.append((row, spot, jnp.take_along_axis(line, spot, axis=1, mode="promise_in_bounds")))
        return columns

    @pl.loop(0, TOP * 8)
    def _(e):
        j, g = e // 8, e % 8
        lane = iota((8, depth), 1)
        for n, (_, _, entry) in enumerate(entry_columns(j, g)):
            own = (n % (low_group // 8)) * 8 + iota((8, depth), 0)
            entry = jnp.concatenate([entry] * (depth // LANES), axis=1)
            odd = odd_common_bits(jnp.right_shift(entry, 8), lane // low_group)
            signs = jnp.where(lane % low_group == own, jnp.where(odd, -1.0, 1.0), 0.0)
            picks[e, n * 8 : n * 8 + 8, :] = signs

    word_copy.wait()
    per_high = NMID * NLOW // 16 // LANES

    @pl.loop(0, high_dev // 8)
    def _(n):
        for c in range(chunks):
            for pair in range(TOP // 2):
                one = wbuf[pl.ds(n * 8 * per_high + (2 * pair) * chunks + c, 8, per_high), :]
                two = wbuf[pl.ds(n * 8 * per_high + (2 * pair + 1) * chunks + c, 8, per_high), :]
                wpair[c, pair, pl.ds(pl.multiple_of(n * 8, 8), 8), :] = jnp.bitwise_or(
                    one, jnp.left_shift(two, 16)
                )

    def prepare(mid, u):
        slot = lax.rem(mid // STEP, SLOTS)
        chunk = mid // GROUP
        lane16 = iota((16, LANES), 1)
        bit_one = jnp.left_shift(1, lane16 % 16)
        bit_two = jnp.left_shift(1, lane16 % 16 + 16)
        for b in range(blocks):
            block = u * blocks + b
            rows = pl.ds(pl.multiple_of(block * 16, 16), 16)
            columns = pl.ds(pl.multiple_of(block * (16 * LANES), 16 * LANES), 16 * LANES)
            pairs = [wpair[chunk, pair, rows, :] for pair in range(TOP // 2)]
            for l_hi in range(2):
                spot = (mid % GROUP) * 16 + l_hi * half + lane16 // 16
                values = []
                for pair in range(TOP // 2):
                    word = jnp.take_along_axis(pairs[pair], spot, axis=1, mode="promise_in_bounds")
                    for which, bit in ((0, bit_one), (1, bit_two)):
                        value = xbuf[slot, 2 * pair + which, (mid % STEP) * 2 + l_hi, :, columns]
                        value = value.reshape(16, LANES).astype(jnp.float32)
                        values.append(jnp.where(jnp.bitwise_and(word, bit) != 0, value, -value))
                reach = 1
                while reach < TOP:
                    nxt = list(values)
                    for at in range(TOP):
                        if not at & reach:
                            nxt[at] = values[at] + values[at + reach]
                            nxt[at + reach] = values[at] - values[at + reach]
                    values, reach = nxt, reach * 2
                for j in range(TOP):
                    ybuf[lax.rem(mid, 2), j, rows, l_hi * LANES : (l_hi + 1) * LANES] = values[j].astype(
                        jnp.bfloat16
                    )

    def transform_high(mid, j):
        result = jnp.dot(table[...], ybuf[lax.rem(mid, 2), j], preferred_element_type=jnp.float32)
        return result.astype(jnp.bfloat16)

    def evaluate(chunk, e):
        j, g = e // 8, e % 8
        block = tbuf[chunk % 2, j, :, pl.ds(pl.multiple_of(g * low_group, low_group), low_group), :]
        found = jnp.dot(
            picks[e].astype(jnp.bfloat16), block.reshape(depth, NLOW), preferred_element_type=jnp.float32
        )
        for n, (row, spot, entry) in enumerate(entry_columns(j, g)):
            rows = slice(n * 8, n * 8 + 8)
            flip = jnp.bitwise_and(entry, 128) != 0
            total = found[rows, LANES:]
            total = found[rows, :LANES] + jnp.where(flip, -total, total)
            if chunk:
                odd = odd_common_bits(entry, chunk * GROUP * 256)
                total = acc[e, rows, :] + jnp.where(odd, -total, total)
            if chunk < chunks - 1:
                acc[e, rows, :] = total
            else:
                total = jnp.where(odd_common_bits(entry, lane8), -total, total)
                value = jnp.sum(total, axis=1, keepdims=True)
                value = jnp.sum(jnp.where(lane8 == spot, value, 0.0), axis=0, keepdims=True)
                out_ref[pl.ds(row, 1), :] += value

    def stretch(first, last, chunk, with_prepare, with_copies):
        @pl.loop(first, last)
        def _(i):
            mid = chunk * GROUP + i
            if with_prepare:

                @pl.when(lax.rem(mid + 1, STEP) == 0)
                def _():
                    wait_step((mid + 1) // STEP)

            @pl.loop(0, TOP)
            def _(u):
                high = transform_high(mid, u)
                if chunk:
                    evaluate(chunk - 1, i * 8 + u)
                if with_prepare:
                    prepare(mid + 1, u)
                if with_copies:
                    for n in range(copies):
                        ahead = (mid + 1) // STEP + 2
                        h = (((mid + 1) % STEP) * 8 + u) * copies + n
                        grad_copy(ahead, h).start()
                tbuf[chunk % 2, u, i] = high

    wait_step(0)

    @pl.loop(0, TOP)
    def _(u):
        prepare(0, u)
        for n in range(copies):
            grad_copy(2, u * copies + n).start()

    end_copies = (steps - 2) * STEP - 1
    for chunk in range(chunks):
        base = chunk * GROUP
        cuts = sorted({0, GROUP, min(max(end_copies - base, 0), GROUP), min(max(rest - 1 - base, 0), GROUP)})
        for first, last in zip(cuts[:-1], cuts[1:]):
            stretch(first, last, chunk, base + first < rest - 1, base + first < end_copies)

    @pl.loop(0, TOP * 8)
    def _(e):
        evaluate(chunks - 1, e)

    place = place_ref[0]
    rows = high_dev * TOP // LANES
    for hi in range(high_parts):
        common = jnp.bitwise_and(place, hi)
        odd = jnp.bitwise_and(common ^ (common >> 1) ^ (common >> 2) ^ (common >> 3), 1)
        sign = jnp.where(odd == 1, -scale, scale)
        out_ref[hi * rows : (hi + 1) * rows, :] = out_ref[hi * rows : (hi + 1) * rows, :] * sign


def partial_sketch(gradients, sign_words, sub_index, place, high_dev, scale):
    kept = sub_index.shape[0]
    rest = NMID // TOP
    low_group = high_dev // 8
    points = kept // (TOP * 8)
    grads = gradients.reshape(high_dev, TOP, rest * 2, 1, LANES)
    words = sign_words.reshape(-1, LANES)
    return pl.pallas_call(
        functools.partial(sketch_kernel, high_dev=high_dev, scale=scale),
        out_shape=jax.ShapeDtypeStruct((kept // LANES, LANES), jnp.float32),
        in_specs=[
            pl.BlockSpec(memory_space=pltpu.SMEM),
            pl.BlockSpec(memory_space=pl.ANY),
            pl.BlockSpec(memory_space=pl.ANY),
            pl.BlockSpec(memory_space=pltpu.VMEM),
        ],
        out_specs=pl.BlockSpec(memory_space=pltpu.VMEM),
        scratch_shapes=[
            pltpu.VMEM((SLOTS, TOP, 2 * STEP, 1, high_dev * LANES), jnp.bfloat16),
            pltpu.VMEM(words.shape, jnp.int32),
            pltpu.VMEM((rest // GROUP, TOP // 2, high_dev, LANES), jnp.int32),
            pltpu.VMEM((high_dev, high_dev), jnp.bfloat16),
            pltpu.VMEM((2, TOP, high_dev, NLOW), jnp.bfloat16),
            pltpu.VMEM((2, TOP, GROUP, high_dev, NLOW), jnp.bfloat16),
            pltpu.VMEM((TOP * 8, points, GROUP * low_group), jnp.float32),
            pltpu.VMEM((TOP * 8, points, LANES), jnp.float32),
            pltpu.SemaphoreType.DMA((SLOTS,)),
            pltpu.SemaphoreType.DMA,
        ],
        compiler_params=pltpu.CompilerParams(vmem_limit_bytes=62 * 1024 * 1024),
        name="sketch",
    )(place, grads, words, sub_index.reshape(kept // LANES, LANES))


def on_device(gradients, sign_words, sub_index, test_sketch, *, feat_size):
    local_features = gradients.shape[1]
    kept = sub_index.shape[0]
    high_dev = local_features // (NMID * NLOW)
    feature_scale = float(local_features * feat_size) ** (-0.5)
    score_scale = float(kept) ** (-0.5)
    place = lax.axis_index("feat").astype(jnp.int32).reshape(1)
    share = partial_sketch(gradients, sign_words, sub_index, place, high_dev, feature_scale)
    sketch = lax.psum(share, "feat").astype(jnp.bfloat16).reshape(1, kept)
    sketches = lax.all_gather(sketch, "ex", axis=0, tiled=True)
    scores = jnp.einsum("ek,tk->et", sketches, test_sketch, preferred_element_type=jnp.float32)
    scores = lax.all_to_all(scores, "ex", split_axis=0, concat_axis=1, tiled=True)
    return scores * score_scale


def solution(mesh):
    return jax.shard_map(
        functools.partial(on_device, feat_size=mesh.shape["feat"]),
        mesh=mesh,
        in_specs=(P("ex", "feat"), P("feat"), P(), P("ex", None)),
        out_specs=P("ex", None),
        check_vma=False,
    )
```

```python
import functools

import jax
import jax.numpy as jnp
from jax import lax
from jax.experimental import pallas as pl
from jax.experimental.pallas import tpu as pltpu
from jax.sharding import PartitionSpec as P

NMID = 256
NLOW = 256
TOP = 8
GROUP = 8
STEP = 4
SLOTS = 3
HALVED = TOP // 2
LANES = 128
PACK = 16


def odd_common_bits(left, right):
    return jnp.bitwise_and(lax.population_count(jnp.bitwise_and(left, right)), 1) == 1


def iota(shape, axis):
    return lax.broadcasted_iota(jnp.int32, shape, axis)


def sketch_kernel(
    place_ref, grads, words, sub_ref, out_ref,
    xbuf, wbuf, wpair, table, ybuf, tbuf, entries, weights, signs, acc, found_rows, sems, wsem,
    *, high_dev, scale,
):
    high_parts = out_ref.shape[0] * LANES // TOP // high_dev
    rest = NMID // TOP
    chunks = rest // GROUP
    steps = rest // STEP
    groups = high_dev // PACK
    points = entries.shape[2]
    pairs = HALVED * groups
    rounds = GROUP * TOP
    blocks = high_dev // PACK // TOP
    copies = high_dev // (STEP * TOP)
    half = LANES // 16

    def grad_copy(step, h):
        return pltpu.make_async_copy(
            grads.at[h, :, pl.ds(step * (2 * STEP), 2 * STEP)],
            xbuf.at[lax.rem(step, SLOTS), :, :, :, pl.ds(pl.multiple_of(h * LANES, LANES), LANES)],
            sems.at[lax.rem(step, SLOTS)],
        )

    def wait_step(step):
        slot = lax.rem(step, SLOTS)
        pltpu.make_async_copy(xbuf.at[slot], xbuf.at[slot], sems.at[slot]).wait()

    word_copy = pltpu.make_async_copy(words, wbuf, wsem)
    word_copy.start()

    @pl.loop(0, 2 * high_dev // 8)
    def _(n):
        for i in range(8):
            h = n * 8 + i
            step = h // high_dev
            grad_copy(step, h - step * high_dev).start()

    table[...] = jnp.where(
        odd_common_bits(iota(table.shape, 0), iota(table.shape, 1)), -1.0, 1.0
    ).astype(jnp.bfloat16)
    acc[...] = jnp.zeros_like(acc)
    lane = iota((groups, LANES), 1)
    for j in range(HALVED):
        spot = (lane // 2 % PACK) * TOP + 2 * j + lane % 2
        for part in range(points // LANES):
            line = jnp.zeros((groups, LANES), jnp.int32)
            for n in range(LANES // (2 * PACK)):
                hi = part * (LANES // (2 * PACK)) + n
                rows = sub_ref[hi * groups : (hi + 1) * groups, :]
                taken = jnp.take_along_axis(rows, spot, axis=1, mode="promise_in_bounds")
                line = jnp.where(lane // (2 * PACK) == n, taken, line)
            entries[j, :, part * LANES : (part + 1) * LANES] = line

    @pl.loop(0, pairs)
    def _(e):
        entry = entries[e // groups, pl.ds(e % groups, 1), :]
        row = iota((24, points), 0)
        mask = jnp.where(
            row < 2 * GROUP,
            jnp.bitwise_or(jnp.left_shift(row % GROUP, 8), jnp.left_shift(row // GROUP, 13)),
            jnp.left_shift(row - 2 * GROUP, 11),
        )
        signs[e] = jnp.where(odd_common_bits(entry, mask), -1.0, 1.0)
        weights[e] = jnp.where(
            odd_common_bits(entry, iota((NLOW, points), 0)), -1.0, 1.0
        ).astype(jnp.bfloat16)

    word_copy.wait()
    per_high = NMID * NLOW // 16 // LANES

    @pl.loop(0, high_dev // 8)
    def _(n):
        for c in range(chunks):
            for pair in range(TOP // 2):
                one = wbuf[pl.ds(n * 8 * per_high + (2 * pair) * chunks + c, 8, per_high), :]
                two = wbuf[pl.ds(n * 8 * per_high + (2 * pair + 1) * chunks + c, 8, per_high), :]
                wpair[c, pair, pl.ds(pl.multiple_of(n * 8, 8), 8), :] = jnp.bitwise_or(
                    one, jnp.left_shift(two, 16)
                )

    def prepare(mid, u):
        slot = lax.rem(mid // STEP, SLOTS)
        chunk = mid // GROUP
        lane16 = iota((PACK, LANES), 1)
        bit_one = jnp.left_shift(1, lane16 % 16)
        bit_two = jnp.left_shift(1, lane16 % 16 + 16)
        for b in range(blocks):
            block = u * blocks + b
            rows = pl.ds(pl.multiple_of(block * PACK, PACK), PACK)
            columns = pl.ds(pl.multiple_of(block * (PACK * LANES), PACK * LANES), PACK * LANES)
            both = [wpair[chunk, pair, rows, :] for pair in range(TOP // 2)]
            for l_hi in range(2):
                spot = (mid % GROUP) * 16 + l_hi * half + lane16 // 16
                values = []
                for pair in range(TOP // 2):
                    word = jnp.take_along_axis(both[pair], spot, axis=1, mode="promise_in_bounds")
                    for which, bit in ((0, bit_one), (1, bit_two)):
                        value = xbuf[slot, 2 * pair + which, (mid % STEP) * 2 + l_hi, :, columns]
                        value = value.reshape(PACK, LANES).astype(jnp.float32)
                        values.append(jnp.where(jnp.bitwise_and(word, bit) != 0, value, -value))
                for reach in (2, 4):
                    nxt = list(values)
                    for at in range(TOP):
                        if not at & reach:
                            nxt[at] = values[at] + values[at + reach]
                            nxt[at + reach] = values[at] - values[at + reach]
                    values = nxt
                for j in range(TOP):
                    ybuf[lax.rem(mid, 2), j, rows, l_hi * LANES : (l_hi + 1) * LANES] = values[j].astype(
                        jnp.bfloat16
                    )

    def transform_high(chunk, i, u):
        result = jnp.dot(table[...], ybuf[i % 2, u], preferred_element_type=jnp.float32)
        tbuf[chunk % 2, u // 2, (u % 2) * GROUP + i] = result.astype(jnp.bfloat16)

    def evaluate(chunk, e):
        j, g = e // groups, e % groups
        block = tbuf[chunk % 2, j, :, pl.ds(pl.multiple_of(g * PACK, PACK), PACK), :]
        found = jnp.dot(
            block.reshape(2 * GROUP * PACK, NLOW), weights[e], preferred_element_type=jnp.float32
        )
        total = found[:PACK] * signs[e, 0:1, :]
        for n in range(1, 2 * GROUP):
            total += found[n * PACK : (n + 1) * PACK] * signs[e, n : n + 1, :]
        acc[e] += total * signs[e, 2 * GROUP + chunk : 2 * GROUP + chunk + 1, :]

    def evaluate_round(chunk, n):
        if pairs >= rounds:
            for m in range(pairs // rounds):
                evaluate(chunk, n * (pairs // rounds) + m)
        else:
            pl.when(n < pairs)(lambda: evaluate(chunk, n))

    def stretch(first, last, chunk, with_prepare, with_copies):
        @pl.loop(first, last)
        def _(i):
            mid = chunk * GROUP + i
            if with_prepare:

                @pl.when(lax.rem(mid + 1, STEP) == 0)
                def _():
                    wait_step((mid + 1) // STEP)

            @pl.loop(0, TOP)
            def _(u):
                if with_copies:
                    for n in range(copies):
                        ahead = (mid + 1) // STEP + 2
                        h = (((mid + 1) % STEP) * TOP + u) * copies + n
                        grad_copy(ahead, h).start()
                if chunk:
                    evaluate_round(chunk - 1, i * TOP + u)
                transform_high(chunk, i, u)
                if with_prepare:
                    prepare(mid + 1, u)

    wait_step(0)

    @pl.loop(0, TOP)
    def _(u):
        prepare(0, u)
        for n in range(copies):
            grad_copy(2, u * copies + n).start()

    end_copies = (steps - 2) * STEP - 1
    for chunk in range(chunks):
        base = chunk * GROUP
        cuts = sorted({0, GROUP, min(max(end_copies - base, 0), GROUP), min(max(rest - 1 - base, 0), GROUP)})
        for first, last in zip(cuts[:-1], cuts[1:]):
            stretch(first, last, chunk, base + first < rest - 1, base + first < end_copies)

    @pl.loop(0, pairs)
    def _(e):
        evaluate(chunks - 1, e)
        own = iota((PACK, points), 1) // 2 % PACK == iota((PACK, points), 0)
        found_rows[e // groups, pl.ds(e % groups, 1), :] = jnp.sum(
            jnp.where(own, acc[e], 0.0), axis=0, keepdims=True
        )

    place = place_ref[0]
    shares = []
    for hi in range(high_parts):
        common = jnp.bitwise_and(place, hi)
        odd = jnp.bitwise_and(common ^ (common >> 1) ^ (common >> 2) ^ (common >> 3), 1)
        sign = jnp.where(odd == 1, -scale, scale)
        part, first = divmod(hi * 2 * PACK, LANES)
        spot = first + lane // TOP * 2 + lane % 2
        line = jnp.zeros((groups, LANES), jnp.float32)
        for j in range(HALVED):
            rows = found_rows[j, :, part * LANES : (part + 1) * LANES]
            taken = jnp.take_along_axis(rows, spot, axis=1, mode="promise_in_bounds")
            line = jnp.where(lane % TOP // 2 == j, taken, line)
        shares.append(line * sign)
    out_ref[...] = jnp.concatenate(shares, axis=0).astype(out_ref.dtype)


def partial_sketch(gradients, sign_words, sub_index, place, high_dev, scale):
    kept = sub_index.shape[0]
    rest = NMID // TOP
    groups = high_dev // PACK
    points = kept // (HALVED * groups)
    grads = gradients.reshape(high_dev, TOP, rest * 2, 1, LANES)
    words = sign_words.reshape(-1, LANES)
    return pl.pallas_call(
        functools.partial(sketch_kernel, high_dev=high_dev, scale=scale),
        out_shape=jax.ShapeDtypeStruct((kept // LANES, LANES), jnp.bfloat16),
        in_specs=[
            pl.BlockSpec(memory_space=pltpu.SMEM),
            pl.BlockSpec(memory_space=pl.ANY),
            pl.BlockSpec(memory_space=pl.ANY),
            pl.BlockSpec(memory_space=pltpu.VMEM),
        ],
        out_specs=pl.BlockSpec(memory_space=pltpu.VMEM),
        scratch_shapes=[
            pltpu.VMEM((SLOTS, TOP, 2 * STEP, 1, high_dev * LANES), jnp.bfloat16),
            pltpu.VMEM(words.shape, jnp.int32),
            pltpu.VMEM((rest // GROUP, TOP // 2, high_dev, LANES), jnp.int32),
            pltpu.VMEM((high_dev, high_dev), jnp.bfloat16),
            pltpu.VMEM((2, TOP, high_dev, NLOW), jnp.bfloat16),
            pltpu.VMEM((2, HALVED, 2 * GROUP, high_dev, NLOW), jnp.bfloat16),
            pltpu.VMEM((HALVED, groups, points), jnp.int32),
            pltpu.VMEM((HALVED * groups, NLOW, points), jnp.bfloat16),
            pltpu.VMEM((HALVED * groups, 24, points), jnp.float32),
            pltpu.VMEM((HALVED * groups, PACK, points), jnp.float32),
            pltpu.VMEM((HALVED, groups, points), jnp.float32),
            pltpu.SemaphoreType.DMA((SLOTS,)),
            pltpu.SemaphoreType.DMA,
        ],
        compiler_params=pltpu.CompilerParams(vmem_limit_bytes=62 * 1024 * 1024),
        name="sketch",
    )(place, grads, words, sub_index.reshape(kept // LANES, LANES))


def shifted(value, axis, size, shift):
    return lax.ppermute(value, axis, [(i, (i + shift) % size) for i in range(size)])


def on_device(gradients, sign_words, sub_index, test_sketch, *, feat_size, ex_size):
    local_features = gradients.shape[1]
    kept = sub_index.shape[0]
    high_dev = local_features // (NMID * NLOW)
    feature_scale = float(local_features * feat_size) ** (-0.5)
    score_scale = float(kept) ** (-0.5)
    place = lax.axis_index("feat").astype(jnp.int32).reshape(1)
    share = partial_sketch(gradients, sign_words, sub_index, place, high_dev, feature_scale)
    shares = [share] + [shifted(share, "ex", ex_size, s) for s in range(1, ex_size)]
    shares = jnp.stack(shares).reshape(ex_size, kept)
    scores = jnp.einsum("ek,tk->et", shares, test_sketch, preferred_element_type=jnp.float32)
    scores = jnp.stack(
        [scores[0]] + [shifted(scores[s], "ex", ex_size, -s) for s in range(1, ex_size)]
    )
    total = scores
    for s in range(1, feat_size):
        total = total + shifted(scores, "feat", feat_size, s)
    total = jnp.roll(total * score_scale, lax.axis_index("ex"), axis=0)
    return total.reshape(1, -1)


def solution(mesh):
    return jax.shard_map(
        functools.partial(on_device, feat_size=mesh.shape["feat"], ex_size=mesh.shape["ex"]),
        mesh=mesh,
        in_specs=(P("ex", "feat"), P("feat"), P(), P("ex", None)),
        out_specs=P("ex", None),
        check_vma=False,
    )
```

```python
import functools

import jax
import jax.numpy as jnp
from jax import lax
from jax.experimental import pallas as pl
from jax.experimental.pallas import tpu as pltpu
from jax.sharding import PartitionSpec as P

NMID = 256
NLOW = 256
TOP = 8
GROUP = 8
STEP = 4
SLOTS = 2
ROWS = 2 * STEP
HALVED = TOP // 2
LANES = 128
PACK = 16


def odd_common_bits(left, right):
    return jnp.bitwise_and(lax.population_count(jnp.bitwise_and(left, right)), 1) == 1


def iota(shape, axis):
    return lax.broadcasted_iota(jnp.int32, shape, axis)


def sketch_kernel(
    place_ref, grads, words, sub_ref, out_ref,
    xbuf, wbuf, wpair, table, ybuf, tbuf, entries, weights, signs, acc, found_rows, sems, wsem,
    *, high_dev, scale,
):
    high_parts = out_ref.shape[0] * LANES // TOP // high_dev
    rest = NMID // TOP
    chunks = rest // GROUP
    steps = rest // STEP
    groups = high_dev // PACK
    points = entries.shape[2]
    pairs = HALVED * groups
    rounds = GROUP * TOP
    highs = high_dev // (STEP * TOP)
    half = LANES // 16
    stride = high_dev + 1

    def grad_copies(step, then):
        slot = lax.rem(step, SLOTS)
        for top in range(TOP):
            copy = pltpu.make_async_copy(
                grads.at[:, top, step],
                xbuf.at[slot, :, :, top * ROWS * LANES : (top + 1) * ROWS * LANES],
                sems.at[slot, top],
            )
            then(copy)

    word_copy = pltpu.make_async_copy(words, wbuf, wsem)
    word_copy.start()
    for step in range(SLOTS):
        grad_copies(step, lambda copy: copy.start())

    table[...] = jnp.where(
        odd_common_bits(iota(table.shape, 0), iota(table.shape, 1)), -1.0, 1.0
    ).astype(jnp.bfloat16)
    acc[...] = jnp.zeros_like(acc)
    lane = iota((groups, LANES), 1)
    for j in range(HALVED):
        spot = (lane // 2 % PACK) * TOP + 2 * j + lane % 2
        for part in range(points // LANES):
            line = jnp.zeros((groups, LANES), jnp.int32)
            for n in range(LANES // (2 * PACK)):
                hi = part * (LANES // (2 * PACK)) + n
                rows = sub_ref[hi * groups : (hi + 1) * groups, :]
                taken = jnp.take_along_axis(rows, spot, axis=1, mode="promise_in_bounds")
                line = jnp.where(lane // (2 * PACK) == n, taken, line)
            entries[j, :, part * LANES : (part + 1) * LANES] = line

    @pl.loop(0, pairs)
    def _(e):
        entry = entries[e // groups, pl.ds(e % groups, 1), :]
        row = iota((24, points), 0)
        mask = jnp.where(
            row < 2 * GROUP,
            jnp.bitwise_or(jnp.left_shift(row % GROUP, 8), jnp.left_shift(row // GROUP, 13)),
            jnp.left_shift(row - 2 * GROUP, 11),
        )
        signs[e] = jnp.where(odd_common_bits(entry, mask), -1.0, 1.0)
        weights[e] = jnp.where(
            odd_common_bits(entry, iota((NLOW, points), 0)), -1.0, 1.0
        ).astype(jnp.bfloat16)

    word_copy.wait()
    per_high = NMID * NLOW // 16 // LANES

    @pl.loop(0, high_dev // 8)
    def _(n):
        for c in range(chunks):
            for pair in range(TOP // 2):
                one = wbuf[pl.ds(n * 8 * per_high + (2 * pair) * chunks + c, 8, per_high), :]
                two = wbuf[pl.ds(n * 8 * per_high + (2 * pair + 1) * chunks + c, 8, per_high), :]
                wpair[c, pair, pl.ds(pl.multiple_of(n * 8, 8), 8), :] = jnp.bitwise_or(
                    one, jnp.left_shift(two, 16)
                )

    def prepare(step, u):
        slot = lax.rem(step, SLOTS)
        chunk = step * STEP // GROUP
        lane8 = iota((ROWS, LANES), 1)
        bits = [jnp.left_shift(1, lane8 % 16), jnp.left_shift(1, lane8 % 16 + 16)]
        spot = lax.rem(step, GROUP // STEP) * (16 * STEP) + iota((ROWS, LANES), 0) * half + lane8 // 16
        for n in range(highs):
            h = u * highs + n
            values = []
            for pair in range(TOP // 2):
                word = jnp.broadcast_to(wpair[chunk, pair, pl.ds(h, 1), :], (ROWS, LANES))
                word = jnp.take_along_axis(word, spot, axis=1, mode="promise_in_bounds")
                two = xbuf[slot, h, :, 2 * pair * ROWS * LANES : 2 * (pair + 1) * ROWS * LANES]
                two = two.reshape(2 * ROWS, LANES).astype(jnp.float32)
                for which in range(2):
                    value = two[which * ROWS : (which + 1) * ROWS]
                    values.append(jnp.where(jnp.bitwise_and(word, bits[which]) != 0, value, -value))
            for reach in (2, 4):
                nxt = list(values)
                for at in range(TOP):
                    if not at & reach:
                        nxt[at] = values[at] + values[at + reach]
                        nxt[at + reach] = values[at] - values[at + reach]
                values = nxt
            for top in range(TOP):
                ybuf[lax.rem(step, 2), top, pl.ds(h, ROWS, stride), :] = values[top]

    def transform_high(step, u):
        top, i = u % TOP, u // TOP
        columns = [
            ybuf[lax.rem(step, 2), top, pl.ds((2 * i + l_hi) * stride, high_dev), :].astype(jnp.bfloat16)
            for l_hi in range(2)
        ]
        result = jnp.dot(
            table[...], jnp.concatenate(columns, axis=1), preferred_element_type=jnp.float32
        )
        chunk = step * STEP // GROUP
        row = (top % 2) * GROUP + lax.rem(step, GROUP // STEP) * STEP + i
        tbuf[lax.rem(chunk, 2), top // 2, row] = result.astype(jnp.bfloat16)

    def evaluate(chunk, e):
        j, g = e // groups, e % groups
        block = tbuf[chunk % 2, j, :, pl.ds(pl.multiple_of(g * PACK, PACK), PACK), :]
        found = jnp.dot(
            block.reshape(2 * GROUP * PACK, NLOW), weights[e], preferred_element_type=jnp.float32
        )
        total = found[:PACK] * signs[e, 0:1, :]
        for n in range(1, 2 * GROUP):
            total += found[n * PACK : (n + 1) * PACK] * signs[e, n : n + 1, :]
        acc[e] += total * signs[e, 2 * GROUP + chunk : 2 * GROUP + chunk + 1, :]

    def evaluate_round(chunk, n):
        if pairs >= rounds:
            for m in range(pairs // rounds):
                evaluate(chunk, n * (pairs // rounds) + m)
        else:
            pl.when(n < pairs)(lambda: evaluate(chunk, n))

    turns = STEP * TOP
    per_chunk = GROUP // STEP

    grad_copies(0, lambda copy: copy.wait())

    @pl.loop(0, turns)
    def _(u):
        prepare(0, u)

    for step in range(steps):
        if step + SLOTS < steps:
            grad_copies(step + SLOTS, lambda copy: copy.start())
        if step + 1 < steps:
            grad_copies(step + 1, lambda copy: copy.wait())

        @pl.loop(0, turns)
        def _(u):
            if step >= per_chunk:
                evaluate_round(step // per_chunk - 1, step % per_chunk * turns + u)
            transform_high(step, u)
            if step + 1 < steps:
                prepare(step + 1, u)

    @pl.loop(0, pairs)
    def _(e):
        evaluate(chunks - 1, e)
        own = iota((PACK, points), 1) // 2 % PACK == iota((PACK, points), 0)
        found_rows[e // groups, pl.ds(e % groups, 1), :] = jnp.sum(
            jnp.where(own, acc[e], 0.0), axis=0, keepdims=True
        )

    place = place_ref[0]
    shares = []
    for hi in range(high_parts):
        common = jnp.bitwise_and(place, hi)
        odd = jnp.bitwise_and(common ^ (common >> 1) ^ (common >> 2) ^ (common >> 3), 1)
        sign = jnp.where(odd == 1, -scale, scale)
        part, first = divmod(hi * 2 * PACK, LANES)
        spot = first + lane // TOP * 2 + lane % 2
        line = jnp.zeros((groups, LANES), jnp.float32)
        for j in range(HALVED):
            rows = found_rows[j, :, part * LANES : (part + 1) * LANES]
            taken = jnp.take_along_axis(rows, spot, axis=1, mode="promise_in_bounds")
            line = jnp.where(lane % TOP // 2 == j, taken, line)
        shares.append(line * sign)
    out_ref[...] = jnp.concatenate(shares, axis=0).astype(out_ref.dtype)


def partial_sketch(gradients, sign_words, sub_index, place, high_dev, scale):
    kept = sub_index.shape[0]
    rest = NMID // TOP
    groups = high_dev // PACK
    points = kept // (HALVED * groups)
    grads = gradients.reshape(high_dev, TOP, rest // STEP, 1, ROWS * LANES)
    words = sign_words.reshape(-1, LANES)
    return pl.pallas_call(
        functools.partial(sketch_kernel, high_dev=high_dev, scale=scale),
        out_shape=jax.ShapeDtypeStruct((kept // LANES, LANES), jnp.bfloat16),
        in_specs=[
            pl.BlockSpec(memory_space=pltpu.SMEM),
            pl.BlockSpec(memory_space=pl.ANY),
            pl.BlockSpec(memory_space=pl.ANY),
            pl.BlockSpec(memory_space=pltpu.VMEM),
        ],
        out_specs=pl.BlockSpec(memory_space=pltpu.VMEM),
        scratch_shapes=[
            pltpu.VMEM((SLOTS, high_dev, 1, TOP * ROWS * LANES), jnp.bfloat16),
            pltpu.VMEM(words.shape, jnp.int32),
            pltpu.VMEM((rest // GROUP, TOP // 2, high_dev, LANES), jnp.int32),
            pltpu.VMEM((high_dev, high_dev), jnp.bfloat16),
            pltpu.VMEM((2, TOP, ROWS * (high_dev + 1), LANES), jnp.float32),
            pltpu.VMEM((2, HALVED, 2 * GROUP, high_dev, NLOW), jnp.bfloat16),
            pltpu.VMEM((HALVED, groups, points), jnp.int32),
            pltpu.VMEM((HALVED * groups, NLOW, points), jnp.bfloat16),
            pltpu.VMEM((HALVED * groups, 24, points), jnp.float32),
            pltpu.VMEM((HALVED * groups, PACK, points), jnp.float32),
            pltpu.VMEM((HALVED, groups, points), jnp.float32),
            pltpu.SemaphoreType.DMA((SLOTS, TOP)),
            pltpu.SemaphoreType.DMA,
        ],
        compiler_params=pltpu.CompilerParams(vmem_limit_bytes=62 * 1024 * 1024),
        name="sketch",
    )(place, grads, words, sub_index.reshape(kept // LANES, LANES))


def swapped(value, axis, size, bit):
    return lax.ppermute(value, axis, [(i, i ^ bit) for i in range(size)])


def on_device(gradients, sign_words, sub_index, test_sketch, *, feat_size, ex_size):
    local_features = gradients.shape[1]
    kept = sub_index.shape[0]
    tests = test_sketch.shape[0]
    high_dev = local_features // (NMID * NLOW)
    feature_scale = float(local_features * feat_size) ** (-0.5)
    score_scale = float(kept) ** (-0.5)
    ex_bits = [1 << b for b in range(ex_size.bit_length() - 1)]
    place = lax.axis_index("feat").astype(jnp.int32).reshape(1)
    shares = partial_sketch(gradients, sign_words, sub_index, place, high_dev, feature_scale)
    for bit in ex_bits:
        shares = jnp.concatenate([shares, swapped(shares, "ex", ex_size, bit)], axis=0)
    shares = shares.reshape(ex_size, kept)
    scores = jnp.einsum("ek,tk->et", shares, test_sketch, preferred_element_type=jnp.float32)
    for bit in ex_bits:
        split = scores.reshape(-1, 2, bit, tests)
        scores = jnp.stack([split[:, 0], swapped(split[:, 1], "ex", ex_size, bit)], axis=1)
    scores = scores.reshape(ex_size, tests)
    for b in range(feat_size.bit_length() - 1):
        scores = scores + swapped(scores, "feat", feat_size, 1 << b)
    scores = scores * score_scale
    own = lax.axis_index("ex")
    for bit in ex_bits:
        split = scores.reshape(-1, 2, bit, tests)
        scores = jnp.where(jnp.bitwise_and(own, bit) != 0, split[:, ::-1], split)
    return scores.reshape(1, ex_size * tests)


def solution(mesh):
    return jax.shard_map(
        functools.partial(on_device, feat_size=mesh.shape["feat"], ex_size=mesh.shape["ex"]),
        mesh=mesh,
        in_specs=(P("ex", "feat"), P("feat"), P(), P("ex", None)),
        out_specs=P("ex", None),
        check_vma=False,
    )
```

```python
import functools

import jax
import jax.numpy as jnp
from jax import lax
from jax.experimental import pallas as pl
from jax.experimental.pallas import tpu as pltpu
from jax.sharding import PartitionSpec as P

NMID = 256
NLOW = 256
TOP = 8
GROUP = 8
STEP = 4
SLOTS = 2
ROWS = 2 * STEP
HALVED = TOP // 2
LANES = 128
PACK = 16
PAIR = 2


def odd_common_bits(left, right):
    return jnp.bitwise_and(lax.population_count(jnp.bitwise_and(left, right)), 1) == 1


def iota(shape, axis):
    return lax.broadcasted_iota(jnp.int32, shape, axis)


def sketch_kernel(
    place_ref, grads, words, sub_ref, out_ref,
    xbuf, wbuf, wpair, table, ybuf0, ybuf1, tbuf0, tbuf1, entries, weights, signs, acc, found_rows, sems, wsem,
    *, high_dev, scale,
):
    high_parts = out_ref.shape[0] * LANES // TOP // high_dev
    rest = NMID // TOP
    chunks = rest // GROUP
    steps = rest // STEP
    groups = high_dev // PACK
    points = entries.shape[2]
    pairs = HALVED * groups
    rounds = GROUP * TOP // PAIR
    highs = high_dev * PAIR // (STEP * TOP)
    half = LANES // 16
    stride = high_dev + 1
    ybuf = (ybuf0, ybuf1)
    tbuf = (tbuf0, tbuf1)

    def grad_copies(step, then):
        slot = step % SLOTS
        for top in range(TOP):
            copy = pltpu.make_async_copy(
                grads.at[:, top, step],
                xbuf.at[slot, :, :, top * ROWS * LANES : (top + 1) * ROWS * LANES],
                sems.at[slot, top],
            )
            then(copy)

    word_copy = pltpu.make_async_copy(words, wbuf, wsem)
    word_copy.start()
    for step in range(SLOTS):
        grad_copies(step, lambda copy: copy.start())

    table[...] = jnp.where(
        odd_common_bits(iota(table.shape, 0), iota(table.shape, 1)), -1.0, 1.0
    ).astype(jnp.bfloat16)
    acc[...] = jnp.zeros_like(acc)
    lane = iota((groups, LANES), 1)
    for j in range(HALVED):
        spot = (lane // 2 % PACK) * TOP + 2 * j + lane % 2
        for part in range(points // LANES):
            line = jnp.zeros((groups, LANES), jnp.int32)
            for n in range(LANES // (2 * PACK)):
                hi = part * (LANES // (2 * PACK)) + n
                rows = sub_ref[hi * groups : (hi + 1) * groups, :]
                taken = jnp.take_along_axis(rows, spot, axis=1, mode="promise_in_bounds")
                line = jnp.where(lane // (2 * PACK) == n, taken, line)
            entries[j, :, part * LANES : (part + 1) * LANES] = line

    @pl.loop(0, pairs)
    def _(e):
        entry = entries[e // groups, pl.ds(e % groups, 1), :]
        row = iota((24, points), 0)
        mask = jnp.where(
            row < 2 * GROUP,
            jnp.bitwise_or(jnp.left_shift(row % GROUP, 8), jnp.left_shift(row // GROUP, 13)),
            jnp.left_shift(row - 2 * GROUP, 11),
        )
        signs[e] = jnp.where(odd_common_bits(entry, mask), -1.0, 1.0)
        weights[e] = jnp.where(
            odd_common_bits(entry, iota((NLOW, points), 0)), -1.0, 1.0
        ).astype(jnp.bfloat16)

    word_copy.wait()
    per_high = NMID * NLOW // 16 // LANES

    @pl.loop(0, high_dev // 8)
    def _(n):
        for c in range(chunks):
            for pair in range(TOP // 2):
                one = wbuf[pl.ds(n * 8 * per_high + (2 * pair) * chunks + c, 8, per_high), :]
                two = wbuf[pl.ds(n * 8 * per_high + (2 * pair + 1) * chunks + c, 8, per_high), :]
                wpair[c, pair, pl.ds(pl.multiple_of(n * 8, 8), 8), :] = jnp.bitwise_or(
                    one, jnp.left_shift(two, 16)
                )

    def prepare(step, u):
        slot = step % SLOTS
        chunk = step * STEP // GROUP
        lane8 = iota((ROWS, LANES), 1)
        bits = [jnp.left_shift(1, lane8 % 16), jnp.left_shift(1, lane8 % 16 + 16)]
        spot = step % (GROUP // STEP) * (16 * STEP) + iota((ROWS, LANES), 0) * half + lane8 // 16
        for n in range(highs):
            h = u * highs + n
            values = []
            for pair in range(TOP // 2):
                word = jnp.broadcast_to(wpair[chunk, pair, pl.ds(h, 1), :], (ROWS, LANES))
                word = jnp.take_along_axis(word, spot, axis=1, mode="promise_in_bounds")
                two = xbuf[slot, h, :, 2 * pair * ROWS * LANES : 2 * (pair + 1) * ROWS * LANES]
                two = two.reshape(2 * ROWS, LANES).astype(jnp.float32)
                for which in range(2):
                    value = two[which * ROWS : (which + 1) * ROWS]
                    values.append(jnp.where(jnp.bitwise_and(word, bits[which]) != 0, value, -value))
            for reach in (2, 4):
                nxt = list(values)
                for at in range(TOP):
                    if not at & reach:
                        nxt[at] = values[at] + values[at + reach]
                        nxt[at + reach] = values[at] - values[at + reach]
                values = nxt
            for top in range(TOP):
                ybuf[step % 2][top, pl.ds(h, ROWS, stride), :] = values[top]

    def transform_high(step, u):
        first, i = u * PAIR % TOP, u * PAIR // TOP
        columns = [
            ybuf[step % 2][first + n, pl.ds((2 * i + l_hi) * stride, high_dev), :].astype(jnp.bfloat16)
            for n in range(PAIR)
            for l_hi in range(2)
        ]
        result = jnp.dot(
            table[...], jnp.concatenate(columns, axis=1), preferred_element_type=jnp.float32
        ).astype(jnp.bfloat16)
        chunk = step * STEP // GROUP
        row = step % (GROUP // STEP) * STEP + i
        for n in range(PAIR):
            top = first + n
            tbuf[chunk % 2][top // 2, n % 2 * GROUP + row] = result[:, n * NLOW : (n + 1) * NLOW]

    def evaluate(chunk, e):
        j, g = e // groups, e % groups
        block = tbuf[chunk % 2][j, :, pl.ds(pl.multiple_of(g * PACK, PACK), PACK), :]
        found = jnp.dot(
            block.reshape(2 * GROUP * PACK, NLOW), weights[e], preferred_element_type=jnp.float32
        )
        total = found[:PACK] * signs[e, 0:1, :]
        for n in range(1, 2 * GROUP):
            total += found[n * PACK : (n + 1) * PACK] * signs[e, n : n + 1, :]
        acc[e] += total * signs[e, 2 * GROUP + chunk : 2 * GROUP + chunk + 1, :]

    def evaluate_round(chunk, n):
        if pairs >= rounds:
            for m in range(pairs // rounds):
                evaluate(chunk, n * (pairs // rounds) + m)
        else:
            pl.when(n < pairs)(lambda: evaluate(chunk, n))

    turns = STEP * TOP // PAIR
    per_chunk = GROUP // STEP

    grad_copies(0, lambda copy: copy.wait())

    @pl.loop(0, turns)
    def _(u):
        prepare(0, u)

    for step in range(steps):
        if step + SLOTS < steps:
            grad_copies(step + SLOTS, lambda copy: copy.start())
        if step + 1 < steps:
            grad_copies(step + 1, lambda copy: copy.wait())

        @pl.loop(0, turns)
        def _(u):
            if step >= per_chunk:
                evaluate_round(step // per_chunk - 1, step % per_chunk * turns + u)
            transform_high(step, u)
            if step + 1 < steps:
                prepare(step + 1, u)

    @pl.loop(0, pairs)
    def _(e):
        evaluate(chunks - 1, e)
        own = iota((PACK, points), 1) // 2 % PACK == iota((PACK, points), 0)
        found_rows[e // groups, pl.ds(e % groups, 1), :] = jnp.sum(
            jnp.where(own, acc[e], 0.0), axis=0, keepdims=True
        )

    place = place_ref[0]
    shares = []
    for hi in range(high_parts):
        common = jnp.bitwise_and(place, hi)
        odd = jnp.bitwise_and(common ^ (common >> 1) ^ (common >> 2) ^ (common >> 3), 1)
        sign = jnp.where(odd == 1, -scale, scale)
        part, first = divmod(hi * 2 * PACK, LANES)
        spot = first + lane // TOP * 2 + lane % 2
        line = jnp.zeros((groups, LANES), jnp.float32)
        for j in range(HALVED):
            rows = found_rows[j, :, part * LANES : (part + 1) * LANES]
            taken = jnp.take_along_axis(rows, spot, axis=1, mode="promise_in_bounds")
            line = jnp.where(lane % TOP // 2 == j, taken, line)
        shares.append(line * sign)
    out_ref[...] = jnp.concatenate(shares, axis=0).astype(out_ref.dtype)


def partial_sketch(gradients, sign_words, sub_index, place, high_dev, scale):
    kept = sub_index.shape[0]
    rest = NMID // TOP
    groups = high_dev // PACK
    points = kept // (HALVED * groups)
    grads = gradients.reshape(high_dev, TOP, rest // STEP, 1, ROWS * LANES)
    words = sign_words.reshape(-1, LANES)
    return pl.pallas_call(
        functools.partial(sketch_kernel, high_dev=high_dev, scale=scale),
        out_shape=jax.ShapeDtypeStruct((kept // LANES, LANES), jnp.bfloat16),
        in_specs=[
            pl.BlockSpec(memory_space=pltpu.SMEM),
            pl.BlockSpec(memory_space=pl.ANY),
            pl.BlockSpec(memory_space=pl.ANY),
            pl.BlockSpec(memory_space=pltpu.VMEM),
        ],
        out_specs=pl.BlockSpec(memory_space=pltpu.VMEM),
        scratch_shapes=[
            pltpu.VMEM((SLOTS, high_dev, 1, TOP * ROWS * LANES), jnp.bfloat16),
            pltpu.VMEM(words.shape, jnp.int32),
            pltpu.VMEM((rest // GROUP, TOP // 2, high_dev, LANES), jnp.int32),
            pltpu.VMEM((high_dev, high_dev), jnp.bfloat16),
            pltpu.VMEM((TOP, ROWS * (high_dev + 1), LANES), jnp.float32),
            pltpu.VMEM((TOP, ROWS * (high_dev + 1), LANES), jnp.float32),
            pltpu.VMEM((HALVED, 2 * GROUP, high_dev, NLOW), jnp.bfloat16),
            pltpu.VMEM((HALVED, 2 * GROUP, high_dev, NLOW), jnp.bfloat16),
            pltpu.VMEM((HALVED, groups, points), jnp.int32),
            pltpu.VMEM((HALVED * groups, NLOW, points), jnp.bfloat16),
            pltpu.VMEM((HALVED * groups, 24, points), jnp.float32),
            pltpu.VMEM((HALVED * groups, PACK, points), jnp.float32),
            pltpu.VMEM((HALVED, groups, points), jnp.float32),
            pltpu.SemaphoreType.DMA((SLOTS, TOP)),
            pltpu.SemaphoreType.DMA,
        ],
        compiler_params=pltpu.CompilerParams(vmem_limit_bytes=62 * 1024 * 1024),
        name="sketch",
    )(place, grads, words, sub_index.reshape(kept // LANES, LANES))


def swapped(value, axis, size, bit):
    return lax.ppermute(value, axis, [(i, i ^ bit) for i in range(size)])


def on_device(gradients, sign_words, sub_index, test_sketch, *, feat_size, ex_size):
    local_features = gradients.shape[1]
    kept = sub_index.shape[0]
    tests = test_sketch.shape[0]
    high_dev = local_features // (NMID * NLOW)
    feature_scale = float(local_features * feat_size) ** (-0.5)
    score_scale = float(kept) ** (-0.5)
    ex_bits = [1 << b for b in range(ex_size.bit_length() - 1)]
    place = lax.axis_index("feat").astype(jnp.int32).reshape(1)
    shares = partial_sketch(gradients, sign_words, sub_index, place, high_dev, feature_scale)
    for bit in ex_bits:
        shares = jnp.concatenate([shares, swapped(shares, "ex", ex_size, bit)], axis=0)
    shares = shares.reshape(ex_size, kept)
    scores = jnp.einsum("ek,tk->et", shares, test_sketch, preferred_element_type=jnp.float32)
    for bit in ex_bits:
        split = scores.reshape(-1, 2, bit, tests)
        scores = jnp.stack([split[:, 0], swapped(split[:, 1], "ex", ex_size, bit)], axis=1)
    scores = scores.reshape(ex_size, tests)
    for b in range(feat_size.bit_length() - 1):
        scores = scores + swapped(scores, "feat", feat_size, 1 << b)
    scores = scores * score_scale
    own = lax.axis_index("ex")
    for bit in ex_bits:
        split = scores.reshape(-1, 2, bit, tests)
        scores = jnp.where(jnp.bitwise_and(own, bit) != 0, split[:, ::-1], split)
    return scores.reshape(1, ex_size * tests)


def solution(mesh):
    return jax.shard_map(
        functools.partial(on_device, feat_size=mesh.shape["feat"], ex_size=mesh.shape["ex"]),
        mesh=mesh,
        in_specs=(P("ex", "feat"), P("feat"), P(), P("ex", None)),
        out_specs=P("ex", None),
        check_vma=False,
    )
```

```python
import functools

import jax
import jax.numpy as jnp
from jax import lax
from jax.experimental import pallas as pl
from jax.experimental.pallas import tpu as pltpu
from jax.sharding import Mesh, PartitionSpec as P

NMID = 256
NLOW = 256
TOP = 8
GROUP = 8
STEP = 4
SLOTS = 2
ROWS = 2 * STEP
HALVED = TOP // 2
LANES = 128
PACK = 16
PAIR = 4


def odd_common_bits(left, right):
    return jnp.bitwise_and(lax.population_count(jnp.bitwise_and(left, right)), 1) == 1


def iota(shape, axis):
    return lax.broadcasted_iota(jnp.int32, shape, axis)


def sketch_kernel(
    place_ref, grads, words, sub_ref, out_ref,
    xbuf, wbuf, wpair, table, ybuf0, ybuf1, tbuf0, tbuf1, entries, weights, signs, acc, found_rows, sems, wsem,
    *, high_dev, scale,
):
    high_parts = out_ref.shape[0]
    rest = NMID // TOP
    chunks = rest // GROUP
    steps = rest // STEP
    groups = high_dev // PACK
    points = entries.shape[2]
    pairs = HALVED * groups
    rounds = GROUP * TOP // PAIR
    highs = high_dev * PAIR // (STEP * TOP)
    half = LANES // 16
    stride = high_dev + 1
    ybuf = (ybuf0, ybuf1)
    tbuf = (tbuf0, tbuf1)

    def grad_copies(step, then):
        slot = step % SLOTS
        for top in range(TOP):
            copy = pltpu.make_async_copy(
                grads.at[:, top, step],
                xbuf.at[slot, :, :, top * ROWS * LANES : (top + 1) * ROWS * LANES],
                sems.at[slot, top],
            )
            then(copy)

    word_copy = pltpu.make_async_copy(words, wbuf, wsem)
    word_copy.start()
    for step in range(SLOTS):
        grad_copies(step, lambda copy: copy.start())

    table[...] = jnp.where(
        odd_common_bits(iota(table.shape, 0), iota(table.shape, 1)), -1.0, 1.0
    ).astype(jnp.bfloat16)
    acc[...] = jnp.zeros_like(acc)
    lane = iota((groups, LANES), 1)
    for j in range(HALVED):
        spot = (lane // 2 % PACK) * TOP + 2 * j + lane % 2
        for part in range(points // LANES):
            line = jnp.zeros((groups, LANES), jnp.int32)
            for n in range(LANES // (2 * PACK)):
                hi = part * (LANES // (2 * PACK)) + n
                rows = sub_ref[hi * groups : (hi + 1) * groups, :]
                taken = jnp.take_along_axis(rows, spot, axis=1, mode="promise_in_bounds")
                line = jnp.where(lane // (2 * PACK) == n, taken, line)
            entries[j, :, part * LANES : (part + 1) * LANES] = line

    def build(e):
        entry = entries[e // groups, pl.ds(e % groups, 1), :]
        row = iota((24, points), 0)
        mask = jnp.where(
            row < 2 * GROUP,
            jnp.bitwise_or(jnp.left_shift(row % GROUP, 8), jnp.left_shift(row // GROUP, 13)),
            jnp.left_shift(row - 2 * GROUP, 11),
        )
        signs[e] = jnp.where(odd_common_bits(entry, mask), -1.0, 1.0)
        weights[e] = jnp.where(
            odd_common_bits(entry, iota((NLOW, points), 0)), -1.0, 1.0
        ).astype(jnp.bfloat16)

    word_copy.wait()
    per_high = NMID * NLOW // 16 // LANES

    @pl.loop(0, high_dev // 8)
    def _(n):
        for c in range(chunks):
            for pair in range(TOP // 2):
                one = wbuf[pl.ds(n * 8 * per_high + (2 * pair) * chunks + c, 8, per_high), :]
                two = wbuf[pl.ds(n * 8 * per_high + (2 * pair + 1) * chunks + c, 8, per_high), :]
                wpair[c, pair, pl.ds(pl.multiple_of(n * 8, 8), 8), :] = jnp.bitwise_or(
                    one, jnp.left_shift(two, 16)
                )

    def prepare(step, u):
        slot = step % SLOTS
        chunk = step * STEP // GROUP
        lane8 = iota((ROWS, LANES), 1)
        bits = [jnp.left_shift(1, lane8 % 16), jnp.left_shift(1, lane8 % 16 + 16)]
        spot = step % (GROUP // STEP) * (16 * STEP) + iota((ROWS, LANES), 0) * half + lane8 // 16
        for n in range(highs):
            h = u * highs + n
            values = []
            for pair in range(TOP // 2):
                word = jnp.broadcast_to(wpair[chunk, pair, pl.ds(h, 1), :], (ROWS, LANES))
                word = jnp.take_along_axis(word, spot, axis=1, mode="promise_in_bounds")
                two = xbuf[slot, h, :, 2 * pair * ROWS * LANES : 2 * (pair + 1) * ROWS * LANES]
                two = two.reshape(2 * ROWS, LANES).astype(jnp.float32)
                for which in range(2):
                    value = two[which * ROWS : (which + 1) * ROWS]
                    values.append(jnp.where(jnp.bitwise_and(word, bits[which]) != 0, value, -value))
            for reach in (2, 4):
                nxt = list(values)
                for at in range(TOP):
                    if not at & reach:
                        nxt[at] = values[at] + values[at + reach]
                        nxt[at + reach] = values[at] - values[at + reach]
                values = nxt
            for top in range(TOP):
                ybuf[step % 2][top, pl.ds(h, ROWS, stride), :] = values[top]

    def transform_high(step, u):
        first, i = u * PAIR % TOP, u * PAIR // TOP
        columns = [
            ybuf[step % 2][first + n, pl.ds((2 * i + l_hi) * stride, high_dev), :].astype(jnp.bfloat16)
            for n in range(PAIR)
            for l_hi in range(2)
        ]
        result = jnp.dot(
            table[...], jnp.concatenate(columns, axis=1), preferred_element_type=jnp.float32
        ).astype(jnp.bfloat16)
        chunk = step * STEP // GROUP
        row = step % (GROUP // STEP) * STEP + i
        for n in range(PAIR):
            top = first + n
            tbuf[chunk % 2][top // 2, n % 2 * GROUP + row] = result[:, n * NLOW : (n + 1) * NLOW]

    def evaluate(chunk, e):
        j, g = e // groups, e % groups
        block = tbuf[chunk % 2][j, :, pl.ds(pl.multiple_of(g * PACK, PACK), PACK), :]
        found = jnp.dot(
            block.reshape(2 * GROUP * PACK, NLOW), weights[e], preferred_element_type=jnp.float32
        )
        total = found[:PACK] * signs[e, 0:1, :]
        for n in range(1, 2 * GROUP):
            total += found[n * PACK : (n + 1) * PACK] * signs[e, n : n + 1, :]
        acc[e] += total * signs[e, 2 * GROUP + chunk : 2 * GROUP + chunk + 1, :]

    def some_pairs(n, do):
        if pairs >= rounds:
            for m in range(pairs // rounds):
                do(n * (pairs // rounds) + m)
        else:
            pl.when(n < pairs)(lambda: do(n))

    turns = STEP * TOP // PAIR
    per_chunk = GROUP // STEP

    grad_copies(0, lambda copy: copy.wait())

    @pl.loop(0, turns)
    def _(u):
        prepare(0, u)

    for step in range(steps):
        if step + SLOTS < steps:
            grad_copies(step + SLOTS, lambda copy: copy.start())
        if step + 1 < steps:
            grad_copies(step + 1, lambda copy: copy.wait())

        @pl.loop(0, turns)
        def _(u):
            if step >= per_chunk:
                some_pairs(step % per_chunk * turns + u, functools.partial(evaluate, step // per_chunk - 1))
            else:
                some_pairs(step * turns + u, build)
            transform_high(step, u)
            if step + 1 < steps:
                prepare(step + 1, u)

    @pl.loop(0, pairs)
    def _(e):
        evaluate(chunks - 1, e)
        own = iota((PACK, points), 1) // 2 % PACK == iota((PACK, points), 0)
        found_rows[e // groups, pl.ds(e % groups, 1), :] = jnp.sum(
            jnp.where(own, acc[e], 0.0), axis=0, keepdims=True
        )

    place = place_ref[0]
    for hi in range(high_parts):
        common = jnp.bitwise_and(place, hi)
        odd = jnp.bitwise_and(common ^ (common >> 1) ^ (common >> 2) ^ (common >> 3), 1)
        sign = jnp.where(odd == 1, -scale, scale)
        part, first = divmod(hi * 2 * PACK, LANES)
        spot = first + lane // TOP * 2 + lane % 2
        line = jnp.zeros((groups, LANES), jnp.float32)
        for j in range(HALVED):
            rows = found_rows[j, :, part * LANES : (part + 1) * LANES]
            taken = jnp.take_along_axis(rows, spot, axis=1, mode="promise_in_bounds")
            line = jnp.where(lane % TOP // 2 == j, taken, line)
        out_ref[jnp.bitwise_xor(hi, place)] = line * sign


def partial_sketch(gradients, sign_words, sub_index, place, high_dev, scale):
    kept = sub_index.shape[0]
    rest = NMID // TOP
    groups = high_dev // PACK
    points = kept // (HALVED * groups)
    grads = gradients.reshape(high_dev, TOP, rest // STEP, 1, ROWS * LANES)
    words = sign_words.reshape(-1, LANES)
    return pl.pallas_call(
        functools.partial(sketch_kernel, high_dev=high_dev, scale=scale),
        out_shape=jax.ShapeDtypeStruct((kept // TOP // high_dev, groups, LANES), jnp.float32),
        in_specs=[
            pl.BlockSpec(memory_space=pltpu.SMEM),
            pl.BlockSpec(memory_space=pl.ANY),
            pl.BlockSpec(memory_space=pl.ANY),
            pl.BlockSpec(memory_space=pltpu.VMEM),
        ],
        out_specs=pl.BlockSpec(memory_space=pltpu.VMEM),
        scratch_shapes=[
            pltpu.VMEM((SLOTS, high_dev, 1, TOP * ROWS * LANES), jnp.bfloat16),
            pltpu.VMEM(words.shape, jnp.int32),
            pltpu.VMEM((rest // GROUP, TOP // 2, high_dev, LANES), jnp.int32),
            pltpu.VMEM((high_dev, high_dev), jnp.bfloat16),
            pltpu.VMEM((TOP, ROWS * (high_dev + 1), LANES), jnp.float32),
            pltpu.VMEM((TOP, ROWS * (high_dev + 1), LANES), jnp.float32),
            pltpu.VMEM((HALVED, 2 * GROUP, high_dev, NLOW), jnp.bfloat16),
            pltpu.VMEM((HALVED, 2 * GROUP, high_dev, NLOW), jnp.bfloat16),
            pltpu.VMEM((HALVED, groups, points), jnp.int32),
            pltpu.VMEM((HALVED * groups, NLOW, points), jnp.bfloat16),
            pltpu.VMEM((HALVED * groups, 24, points), jnp.float32),
            pltpu.VMEM((HALVED * groups, PACK, points), jnp.float32),
            pltpu.VMEM((HALVED, groups, points), jnp.float32),
            pltpu.SemaphoreType.DMA((SLOTS, TOP)),
            pltpu.SemaphoreType.DMA,
        ],
        compiler_params=pltpu.CompilerParams(vmem_limit_bytes=62 * 1024 * 1024),
        name="sketch",
    )(place, grads, words, sub_index.reshape(kept // LANES, LANES))


def swapped(value, axis, size, bits):
    return lax.ppermute(value, axis, [(i, i ^ bits) for i in range(size)])


def on_device(gradients, sign_words, sub_index, test_sketch, *, mesh):
    feat_size, far_size, near_size = (mesh.shape[axis] for axis in ("feat", "far", "near"))
    local_features = gradients.shape[1]
    kept = sub_index.shape[0]
    tests = test_sketch.shape[0]
    high_dev = local_features // (NMID * NLOW)
    feature_scale = float(local_features * feat_size) ** (-0.5)
    score_scale = float(kept) ** (-0.5)
    place = lax.axis_index("feat").astype(jnp.int32)
    own_kept = kept // feat_size
    own_tests = lax.dynamic_slice_in_dim(test_sketch, place * own_kept, own_kept, axis=1)
    own_tests = lax.all_gather(own_tests, "far", axis=0, tiled=True)
    shares = partial_sketch(gradients, sign_words, sub_index, place.reshape(1), high_dev, feature_scale)
    sketch = shares[0]
    for s in range(1, feat_size):
        sketch = sketch + swapped(shares[s], "feat", feat_size, s)
    sketch = sketch.astype(jnp.bfloat16).reshape(1, own_kept)
    sketches = [sketch] + [swapped(sketch, "near", near_size, s) for s in range(1, near_size)]
    scores = jnp.einsum(
        "ek,tk->et", jnp.concatenate(sketches, axis=0), own_tests, preferred_element_type=jnp.float32
    )
    scores = jnp.stack(
        [scores[0]] + [swapped(scores[s], "near", near_size, s) for s in range(1, near_size)]
    )
    total = scores
    for s in range(1, feat_size):
        total = total + swapped(scores, "feat", feat_size, s)
    total = (total * score_scale).reshape(near_size, far_size, tests)
    own = lax.axis_index("near")
    for b in range(near_size.bit_length() - 1):
        split = total.reshape(-1, 2, 1 << b, far_size, tests)
        total = jnp.where(jnp.bitwise_and(own, 1 << b) != 0, split[:, ::-1], split)
    total = total.reshape(near_size, far_size, tests)
    return jnp.swapaxes(total, 0, 1).reshape(1, -1)


def solution(mesh):
    feat_size, ex_size = mesh.shape["feat"], mesh.shape["ex"]
    far_size = min(4, ex_size)
    mesh = Mesh(mesh.devices.reshape(feat_size, far_size, ex_size // far_size), ("feat", "far", "near"))
    ex = ("far", "near")
    return jax.shard_map(
        functools.partial(on_device, mesh=mesh),
        mesh=mesh,
        in_specs=(P(ex, "feat"), P("feat"), P(), P(ex, None)),
        out_specs=P(ex, None),
        check_vma=False,
    )
```

```python
import functools

import jax
import jax.numpy as jnp
from jax import lax
from jax.experimental import pallas as pl
from jax.experimental.pallas import tpu as pltpu
from jax.sharding import Mesh, PartitionSpec as P

NMID = 256
NLOW = 256
TOP = 8
GROUP = 8
STEP = 4
SLOTS = 3
ROWS = 2 * STEP
HALVED = TOP // 2
LANES = 128
PACK = 16
PAIR = 4


def odd_common_bits(left, right):
    return jnp.bitwise_and(lax.population_count(jnp.bitwise_and(left, right)), 1) == 1


def iota(shape, axis):
    return lax.broadcasted_iota(jnp.int32, shape, axis)


def sketch_kernel(
    place_ref, grads, words, sub_ref, out_ref,
    xbuf, wbuf, wpair, table, ybuf0, ybuf1, tbuf0, tbuf1, entries, weights, signs, acc, found_rows, sems, wsem,
    *, high_dev, scale,
):
    high_parts = out_ref.shape[0] * LANES // TOP // high_dev
    rest = NMID // TOP
    chunks = rest // GROUP
    steps = rest // STEP
    groups = high_dev // PACK
    points = entries.shape[2]
    pairs = HALVED * groups
    rounds = GROUP * TOP // PAIR
    turns = STEP * TOP // PAIR
    per_chunk = GROUP // STEP
    blocks = STEP * high_dev // PACK // turns
    half = LANES // 16
    ybuf = (ybuf0, ybuf1)
    tbuf = (tbuf0, tbuf1)

    def grad_copy(step, h):
        return pltpu.make_async_copy(
            grads.at[h, :, pl.ds(step * ROWS, ROWS)],
            xbuf.at[step % SLOTS, :, :, :, pl.ds(pl.multiple_of(h * LANES, LANES), LANES)],
            sems.at[step % SLOTS],
        )

    def start_copies(step):
        @pl.loop(0, high_dev // 8)
        def _(n):
            for i in range(8):
                grad_copy(step, n * 8 + i).start()

    def wait_copies(step):
        slot = step % SLOTS
        pltpu.make_async_copy(xbuf.at[slot], xbuf.at[slot], sems.at[slot]).wait()

    word_copy = pltpu.make_async_copy(words, wbuf, wsem)
    word_copy.start()
    start_copies(0)
    start_copies(1)

    table[...] = jnp.where(
        odd_common_bits(iota(table.shape, 0), iota(table.shape, 1)), -1.0, 1.0
    ).astype(jnp.bfloat16)
    acc[...] = jnp.zeros_like(acc)
    lane = iota((groups, LANES), 1)
    for j in range(HALVED):
        spot = (lane // 2 % PACK) * TOP + 2 * j + lane % 2
        for part in range(points // LANES):
            line = jnp.zeros((groups, LANES), jnp.int32)
            for n in range(LANES // (2 * PACK)):
                hi = part * (LANES // (2 * PACK)) + n
                rows = sub_ref[hi * groups : (hi + 1) * groups, :]
                taken = jnp.take_along_axis(rows, spot, axis=1, mode="promise_in_bounds")
                line = jnp.where(lane // (2 * PACK) == n, taken, line)
            entries[j, :, part * LANES : (part + 1) * LANES] = line

    def build(e):
        entry = entries[e // groups, pl.ds(e % groups, 1), :]
        row = iota((24, points), 0)
        mask = jnp.where(
            row < 2 * GROUP,
            jnp.bitwise_or(jnp.left_shift(row % GROUP, 8), jnp.left_shift(row // GROUP, 13)),
            jnp.left_shift(row - 2 * GROUP, 11),
        )
        signs[e] = jnp.where(odd_common_bits(entry, mask), -1.0, 1.0)
        weights[e] = jnp.where(
            odd_common_bits(entry, iota((NLOW, points), 0)), -1.0, 1.0
        ).astype(jnp.bfloat16)

    word_copy.wait()
    per_high = NMID * NLOW // 16 // LANES

    @pl.loop(0, high_dev // 8)
    def _(n):
        for c in range(chunks):
            for pair in range(TOP // 2):
                one = wbuf[pl.ds(n * 8 * per_high + (2 * pair) * chunks + c, 8, per_high), :]
                two = wbuf[pl.ds(n * 8 * per_high + (2 * pair + 1) * chunks + c, 8, per_high), :]
                wpair[c, pair, pl.ds(pl.multiple_of(n * 8, 8), 8), :] = jnp.bitwise_or(
                    one, jnp.left_shift(two, 16)
                )

    def prepare(step, u):
        slot = step % SLOTS
        chunk = step * STEP // GROUP
        lane16 = iota((PACK, LANES), 1)
        bits = [jnp.left_shift(1, lane16 % 16), jnp.left_shift(1, lane16 % 16 + 16)]
        i = u * STEP // turns
        for n in range(blocks):
            block = (u * blocks + n) % (high_dev // PACK)
            rows = pl.ds(pl.multiple_of(block * PACK, PACK), PACK)
            columns = pl.ds(pl.multiple_of(block * (PACK * LANES), PACK * LANES), PACK * LANES)
            packed = [wpair[chunk, pair, rows, :] for pair in range(TOP // 2)]
            for l_hi in range(2):
                spot = (step % (GROUP // STEP) * STEP + i) * 16 + l_hi * half + lane16 // 16
                values = []
                for pair in range(TOP // 2):
                    word = jnp.take_along_axis(packed[pair], spot, axis=1, mode="promise_in_bounds")
                    for which in range(2):
                        value = xbuf[slot, 2 * pair + which, 2 * i + l_hi, :, columns]
                        value = value.reshape(PACK, LANES).astype(jnp.float32)
                        values.append(jnp.where(jnp.bitwise_and(word, bits[which]) != 0, value, -value))
                for reach in (2, 4):
                    nxt = list(values)
                    for at in range(TOP):
                        if not at & reach:
                            nxt[at] = values[at] + values[at + reach]
                            nxt[at + reach] = values[at] - values[at + reach]
                    values = nxt
                for top in range(TOP):
                    ybuf[step % 2][top, i, rows, l_hi * LANES : (l_hi + 1) * LANES] = values[top].astype(
                        jnp.bfloat16
                    )

    def transform_high(step, u):
        first, i = u * PAIR % TOP, u * PAIR // TOP
        columns = [ybuf[step % 2][first + n, i] for n in range(PAIR)]
        result = jnp.dot(
            table[...], jnp.concatenate(columns, axis=1), preferred_element_type=jnp.float32
        ).astype(jnp.bfloat16)
        chunk = step * STEP // GROUP
        row = step % (GROUP // STEP) * STEP + i
        for n in range(PAIR):
            top = first + n
            tbuf[chunk % 2][top // 2, n % 2 * GROUP + row] = result[:, n * NLOW : (n + 1) * NLOW]

    def evaluate(chunk, e):
        j, g = e // groups, e % groups
        block = tbuf[chunk % 2][j, :, pl.ds(pl.multiple_of(g * PACK, PACK), PACK), :]
        found = jnp.dot(
            block.reshape(2 * GROUP * PACK, NLOW), weights[e], preferred_element_type=jnp.float32
        )
        total = found[:PACK] * signs[e, 0:1, :]
        for n in range(1, 2 * GROUP):
            total += found[n * PACK : (n + 1) * PACK] * signs[e, n : n + 1, :]
        acc[e] += total * signs[e, 2 * GROUP + chunk : 2 * GROUP + chunk + 1, :]

    def some_pairs(n, do):
        if pairs >= rounds:
            for m in range(pairs // rounds):
                do(n * (pairs // rounds) + m)
        else:
            pl.when(n < pairs)(lambda: do(n))


    wait_copies(0)
    start_copies(2)

    @pl.loop(0, turns)
    def _(u):
        prepare(0, u)

    for step in range(steps):
        if step + 1 < steps:
            wait_copies(step + 1)

        @pl.loop(0, turns)
        def _(u):
            if step + SLOTS < steps:
                for n in range(high_dev // turns):
                    grad_copy(step + SLOTS, u * (high_dev // turns) + n).start()
            if step >= per_chunk:
                some_pairs(step % per_chunk * turns + u, functools.partial(evaluate, step // per_chunk - 1))
            else:
                some_pairs(step * turns + u, build)
            transform_high(step, u)
            if step + 1 < steps:
                prepare(step + 1, u)

    @pl.loop(0, pairs)
    def _(e):
        evaluate(chunks - 1, e)
        own = iota((PACK, points), 1) // 2 % PACK == iota((PACK, points), 0)
        found_rows[e // groups, pl.ds(e % groups, 1), :] = jnp.sum(
            jnp.where(own, acc[e], 0.0), axis=0, keepdims=True
        )

    place = place_ref[0]
    for hi in range(high_parts):
        common = jnp.bitwise_and(place, hi)
        odd = jnp.bitwise_and(common ^ (common >> 1) ^ (common >> 2) ^ (common >> 3), 1)
        sign = jnp.where(odd == 1, -scale, scale)
        part, first = divmod(hi * 2 * PACK, LANES)
        spot = first + lane // TOP * 2 + lane % 2
        line = jnp.zeros((groups, LANES), jnp.float32)
        for j in range(HALVED):
            rows = found_rows[j, :, part * LANES : (part + 1) * LANES]
            taken = jnp.take_along_axis(rows, spot, axis=1, mode="promise_in_bounds")
            line = jnp.where(lane % TOP // 2 == j, taken, line)
        out_ref[hi * groups : (hi + 1) * groups, :] = line * sign


def partial_sketch(gradients, sign_words, sub_index, place, high_dev, scale):
    kept = sub_index.shape[0]
    rest = NMID // TOP
    groups = high_dev // PACK
    points = kept // (HALVED * groups)
    grads = gradients.reshape(high_dev, TOP, 2 * rest, 1, LANES)
    words = sign_words.reshape(-1, LANES)
    return pl.pallas_call(
        functools.partial(sketch_kernel, high_dev=high_dev, scale=scale),
        out_shape=jax.ShapeDtypeStruct((kept // LANES, LANES), jnp.float32),
        in_specs=[
            pl.BlockSpec(memory_space=pltpu.SMEM),
            pl.BlockSpec(memory_space=pl.ANY),
            pl.BlockSpec(memory_space=pl.ANY),
            pl.BlockSpec(memory_space=pltpu.VMEM),
        ],
        out_specs=pl.BlockSpec(memory_space=pltpu.VMEM),
        scratch_shapes=[
            pltpu.VMEM((SLOTS, TOP, ROWS, 1, high_dev * LANES), jnp.bfloat16),
            pltpu.VMEM(words.shape, jnp.int32),
            pltpu.VMEM((rest // GROUP, TOP // 2, high_dev, LANES), jnp.int32),
            pltpu.VMEM((high_dev, high_dev), jnp.bfloat16),
            pltpu.VMEM((TOP, STEP, high_dev, NLOW), jnp.bfloat16),
            pltpu.VMEM((TOP, STEP, high_dev, NLOW), jnp.bfloat16),
            pltpu.VMEM((HALVED, 2 * GROUP, high_dev, NLOW), jnp.bfloat16),
            pltpu.VMEM((HALVED, 2 * GROUP, high_dev, NLOW), jnp.bfloat16),
            pltpu.VMEM((HALVED, groups, points), jnp.int32),
            pltpu.VMEM((HALVED * groups, NLOW, points), jnp.bfloat16),
            pltpu.VMEM((HALVED * groups, 24, points), jnp.float32),
            pltpu.VMEM((HALVED * groups, PACK, points), jnp.float32),
            pltpu.VMEM((HALVED, groups, points), jnp.float32),
            pltpu.SemaphoreType.DMA((SLOTS,)),
            pltpu.SemaphoreType.DMA,
        ],
        compiler_params=pltpu.CompilerParams(vmem_limit_bytes=62 * 1024 * 1024),
        cost_estimate=pl.CostEstimate(
            flops=4 * NLOW * high_dev * NMID * NLOW, bytes_accessed=4 * gradients.size, transcendentals=0
        ),
        name="sketch",
    )(place, grads, words, sub_index.reshape(kept // LANES, LANES))


def swapped(value, axis, size, bits):
    return lax.ppermute(value, axis, [(i, i ^ bits) for i in range(size)])


def score_kernel(*refs, scale):
    *sketches, own_tests, near_tests, out_ref, lines = refs
    for n, sketch in enumerate(sketches):
        whole = sketch[...].astype(jnp.float32)
        for row in range(whole.shape[0]):
            lines[n : n + 1, row * LANES : (row + 1) * LANES] = whole[row : row + 1, :]
    left = lines[...].astype(jnp.bfloat16)
    for n, tests in enumerate([own_tests] + [near_tests.at[s] for s in range(near_tests.shape[0])]):
        found = lax.dot_general(
            left, tests[...], (((1,), (1,)), ((), ())), preferred_element_type=jnp.float32
        )
        found = found[: len(sketches)] * scale
        out_ref[:, n * tests.shape[0] : (n + 1) * tests.shape[0]] = found


def scores_of(sketches, own_tests, near_tests, scale):
    tests, kept = own_tests.shape
    count = len(sketches)
    return pl.pallas_call(
        functools.partial(score_kernel, scale=scale),
        out_shape=jax.ShapeDtypeStruct((count, tests * (1 + near_tests.shape[0])), jnp.float32),
        scratch_shapes=[pltpu.VMEM((16, kept), jnp.float32)],
        compiler_params=pltpu.CompilerParams(vmem_limit_bytes=32 * 1024 * 1024),
        name="scores",
    )(*sketches, own_tests, near_tests)


def on_device(gradients, sign_words, sub_index, test_sketch, *, mesh):
    feat_size, far_size, near_size = (mesh.shape[axis] for axis in ("feat", "far", "near"))
    local_features = gradients.shape[1]
    kept = sub_index.shape[0]
    tests = test_sketch.shape[0]
    high_dev = local_features // (NMID * NLOW)
    feature_scale = float(local_features * feat_size) ** (-0.5)
    score_scale = float(kept) ** (-0.5)
    place = lax.axis_index("feat").astype(jnp.int32).reshape(1)
    near_tests = jnp.stack([swapped(test_sketch, "near", near_size, s) for s in range(1, near_size)])
    shares = partial_sketch(gradients, sign_words, sub_index, place, high_dev, feature_scale)
    sketch = shares
    for s in range(1, feat_size):
        sketch = sketch + swapped(shares, "feat", feat_size, s)
    sketch = sketch.astype(jnp.bfloat16)
    sketches = [sketch] + [swapped(sketch, "far", far_size, s) for s in range(1, far_size)]
    scores = scores_of(sketches, test_sketch, near_tests, score_scale)
    scores = jnp.stack(
        [scores[:1]] + [swapped(scores[s : s + 1], "far", far_size, s) for s in range(1, far_size)]
    )
    scores = scores.reshape(far_size, near_size, tests)
    far, near = lax.axis_index("far"), lax.axis_index("near")
    for b in range(near_size.bit_length() - 1):
        split = scores.reshape(far_size, -1, 2, 1 << b, tests)
        scores = jnp.where(jnp.bitwise_and(near, 1 << b) != 0, split[:, :, ::-1], split)
    for b in range(far_size.bit_length() - 1):
        split = scores.reshape(-1, 2, 1 << b, near_size, tests)
        scores = jnp.where(jnp.bitwise_and(far, 1 << b) != 0, split[:, ::-1], split)
    return scores.reshape(1, -1)


def solution(mesh):
    feat_size, ex_size = mesh.shape["feat"], mesh.shape["ex"]
    far_size = min(4, ex_size)
    mesh = Mesh(mesh.devices.reshape(feat_size, far_size, ex_size // far_size), ("feat", "far", "near"))
    ex = ("far", "near")
    return jax.shard_map(
        functools.partial(on_device, mesh=mesh),
        mesh=mesh,
        in_specs=(P(ex, "feat"), P("feat"), P(), P(ex, None)),
        out_specs=P(ex, None),
        check_vma=False,
    )
```

```python
import functools

import jax
import jax.numpy as jnp
from jax import lax
from jax.experimental import pallas as pl
from jax.experimental.pallas import tpu as pltpu
from jax.sharding import Mesh, PartitionSpec as P

NMID = 256
NLOW = 256
TOP = 8
GROUP = 8
STEP = 4
SLOTS = 3
ROWS = 2 * STEP
HALVED = TOP // 2
LANES = 128
PACK = 16
PAIR = 4


def odd_common_bits(left, right):
    return jnp.bitwise_and(lax.population_count(jnp.bitwise_and(left, right)), 1) == 1


def iota(shape, axis):
    return lax.broadcasted_iota(jnp.int32, shape, axis)


def sketch_kernel(
    place_ref, grads, words, sub_ref, out_ref,
    xbuf, wbuf, wpair, table, ybuf0, ybuf1, tbuf0, tbuf1, entries, weights, signs, acc, found_rows, sems, wsem,
    *, high_dev, scale,
):
    high_parts = out_ref.shape[0] * LANES // TOP // high_dev
    rest = NMID // TOP
    chunks = rest // GROUP
    steps = rest // STEP
    groups = high_dev // PACK
    points = entries.shape[2]
    pairs = HALVED * groups
    rounds = GROUP * TOP // PAIR
    turns = STEP * TOP // PAIR
    per_chunk = GROUP // STEP
    blocks = STEP * high_dev // PACK // turns
    half = LANES // 16
    ybuf = (ybuf0, ybuf1)
    tbuf = (tbuf0, tbuf1)

    def grad_copy(step, h):
        return pltpu.make_async_copy(
            grads.at[h, :, pl.ds(step * ROWS, ROWS)],
            xbuf.at[step % SLOTS, :, :, :, pl.ds(pl.multiple_of(h * LANES, LANES), LANES)],
            sems.at[step % SLOTS],
        )

    def start_copies(step):
        @pl.loop(0, high_dev // 8)
        def _(n):
            for i in range(8):
                grad_copy(step, n * 8 + i).start(priority=i % 2)

    def wait_copies(step):
        slot = step % SLOTS
        pltpu.make_async_copy(xbuf.at[slot], xbuf.at[slot], sems.at[slot]).wait()

    per_high = NMID * NLOW // 16 // LANES
    word_copy = pltpu.make_async_copy(words, wbuf.at[:, :per_high], wsem)
    word_copy.start()
    start_copies(0)
    start_copies(1)

    table[...] = jnp.where(
        odd_common_bits(iota(table.shape, 0), iota(table.shape, 1)), -1.0, 1.0
    ).astype(jnp.bfloat16)
    acc[...] = jnp.zeros_like(acc)
    lane = iota((groups, LANES), 1)
    for j in range(HALVED):
        spot = (lane // 2 % PACK) * TOP + 2 * j + lane % 2
        for part in range(points // LANES):
            line = jnp.zeros((groups, LANES), jnp.int32)
            for n in range(LANES // (2 * PACK)):
                hi = part * (LANES // (2 * PACK)) + n
                rows = sub_ref[hi * groups : (hi + 1) * groups, :]
                taken = jnp.take_along_axis(rows, spot, axis=1, mode="promise_in_bounds")
                line = jnp.where(lane // (2 * PACK) == n, taken, line)
            entries[j, :, part * LANES : (part + 1) * LANES] = line

    def build(e):
        entry = entries[e // groups, pl.ds(e % groups, 1), :]
        row = iota((24, points), 0)
        mask = jnp.where(
            row < 2 * GROUP,
            jnp.bitwise_or(jnp.left_shift(row % GROUP, 8), jnp.left_shift(row // GROUP, 13)),
            jnp.left_shift(row - 2 * GROUP, 11),
        )
        signs[e] = jnp.where(odd_common_bits(entry, mask), -1.0, 1.0)
        weights[e] = jnp.where(
            odd_common_bits(entry, iota((NLOW, points), 0)), -1.0, 1.0
        ).astype(jnp.bfloat16)

    word_copy.wait()
    lines = wbuf.reshape(high_dev * (per_high + 1), 1, LANES)

    @pl.loop(0, high_dev // 8)
    def _(n):
        for c in range(chunks):
            for pair in range(TOP // 2):
                one, two = (
                    lines[
                        pl.ds(n * 8 * (per_high + 1) + (2 * pair + which) * chunks + c, 8, per_high + 1), 0, :
                    ]
                    for which in range(2)
                )
                wpair[c, pair, pl.ds(pl.multiple_of(n * 8, 8), 8), :] = jnp.bitwise_or(
                    one, jnp.left_shift(two, 16)
                )

    def prepare(step, u):
        slot = step % SLOTS
        chunk = step * STEP // GROUP
        lane16 = iota((PACK, LANES), 1)
        bits = [jnp.left_shift(1, lane16 % 16), jnp.left_shift(1, lane16 % 16 + 16)]
        i = u * STEP // turns
        for n in range(blocks):
            block = (u * blocks + n) % (high_dev // PACK)
            rows = pl.ds(pl.multiple_of(block * PACK, PACK), PACK)
            columns = pl.ds(pl.multiple_of(block * (PACK * LANES), PACK * LANES), PACK * LANES)
            packed = [wpair[chunk, pair, rows, :] for pair in range(TOP // 2)]
            for l_hi in range(2):
                spot = (step % (GROUP // STEP) * STEP + i) * 16 + l_hi * half + lane16 // 16
                values = []
                for pair in range(TOP // 2):
                    word = jnp.take_along_axis(packed[pair], spot, axis=1, mode="promise_in_bounds")
                    for which in range(2):
                        value = xbuf[slot, 2 * pair + which, 2 * i + l_hi, :, columns]
                        value = value.reshape(PACK, LANES).astype(jnp.float32)
                        values.append(jnp.where(jnp.bitwise_and(word, bits[which]) != 0, value, -value))
                for reach in (2, 4):
                    nxt = list(values)
                    for at in range(TOP):
                        if not at & reach:
                            nxt[at] = values[at] + values[at + reach]
                            nxt[at + reach] = values[at] - values[at + reach]
                    values = nxt
                for top in range(TOP):
                    ybuf[step % 2][top, i, rows, l_hi * LANES : (l_hi + 1) * LANES] = values[top].astype(
                        jnp.bfloat16
                    )

    def transform_high(step, u):
        first, i = u * PAIR % TOP, u * PAIR // TOP
        columns = [ybuf[step % 2][first + n, i] for n in range(PAIR)]
        result = jnp.dot(
            table[...], jnp.concatenate(columns, axis=1), preferred_element_type=jnp.float32
        ).astype(jnp.bfloat16)
        chunk = step * STEP // GROUP
        row = step % (GROUP // STEP) * STEP + i
        for n in range(PAIR):
            top = first + n
            tbuf[chunk % 2][top // 2, n % 2 * GROUP + row] = result[:, n * NLOW : (n + 1) * NLOW]

    def evaluate(chunk, e):
        j, g = e // groups, e % groups
        block = tbuf[chunk % 2][j, :, pl.ds(pl.multiple_of(g * PACK, PACK), PACK), :]
        found = jnp.dot(
            block.reshape(2 * GROUP * PACK, NLOW), weights[e], preferred_element_type=jnp.float32
        )
        total = found[:PACK] * signs[e, 0:1, :]
        for n in range(1, 2 * GROUP):
            total += found[n * PACK : (n + 1) * PACK] * signs[e, n : n + 1, :]
        acc[e] += total * signs[e, 2 * GROUP + chunk : 2 * GROUP + chunk + 1, :]

    def some_pairs(n, do):
        if pairs >= rounds:
            for m in range(pairs // rounds):
                do(n * (pairs // rounds) + m)
        else:
            pl.when(n < pairs)(lambda: do(n))


    wait_copies(0)
    start_copies(2)

    @pl.loop(0, turns)
    def _(u):
        prepare(0, u)

    for step in range(steps):
        if step + 1 < steps:
            wait_copies(step + 1)

        @pl.loop(0, turns)
        def _(u):
            if step + SLOTS < steps:
                for n in range(high_dev // turns):
                    grad_copy(step + SLOTS, u * (high_dev // turns) + n).start(priority=n % 2)
            if step >= per_chunk:
                some_pairs(step % per_chunk * turns + u, functools.partial(evaluate, step // per_chunk - 1))
            else:
                some_pairs(step * turns + u, build)
            transform_high(step, u)
            if step + 1 < steps:
                prepare(step + 1, u)

    @pl.loop(0, pairs)
    def _(e):
        evaluate(chunks - 1, e)
        own = iota((PACK, points), 1) // 2 % PACK == iota((PACK, points), 0)
        found_rows[e // groups, pl.ds(e % groups, 1), :] = jnp.sum(
            jnp.where(own, acc[e], 0.0), axis=0, keepdims=True
        )

    place = place_ref[0]
    for hi in range(high_parts):
        common = jnp.bitwise_and(place, hi)
        odd = jnp.bitwise_and(common ^ (common >> 1) ^ (common >> 2) ^ (common >> 3), 1)
        sign = jnp.where(odd == 1, -scale, scale)
        part, first = divmod(hi * 2 * PACK, LANES)
        spot = first + lane // TOP * 2 + lane % 2
        line = jnp.zeros((groups, LANES), jnp.float32)
        for j in range(HALVED):
            rows = found_rows[j, :, part * LANES : (part + 1) * LANES]
            taken = jnp.take_along_axis(rows, spot, axis=1, mode="promise_in_bounds")
            line = jnp.where(lane % TOP // 2 == j, taken, line)
        out_ref[hi * groups : (hi + 1) * groups, :] = line * sign


def partial_sketch(gradients, sign_words, sub_index, place, high_dev, scale):
    kept = sub_index.shape[0]
    rest = NMID // TOP
    groups = high_dev // PACK
    points = kept // (HALVED * groups)
    grads = gradients.reshape(high_dev, TOP, 2 * rest, 1, LANES)
    words = sign_words.reshape(high_dev, -1, 1, LANES)
    return pl.pallas_call(
        functools.partial(sketch_kernel, high_dev=high_dev, scale=scale),
        out_shape=jax.ShapeDtypeStruct((kept // LANES, LANES), jnp.float32),
        in_specs=[
            pl.BlockSpec(memory_space=pltpu.SMEM),
            pl.BlockSpec(memory_space=pl.ANY),
            pl.BlockSpec(memory_space=pl.ANY),
            pl.BlockSpec(memory_space=pltpu.VMEM),
        ],
        out_specs=pl.BlockSpec(memory_space=pltpu.VMEM),
        scratch_shapes=[
            pltpu.VMEM((SLOTS, TOP, ROWS, 1, high_dev * LANES), jnp.bfloat16),
            pltpu.VMEM((high_dev, words.shape[1] + 1, 1, LANES), jnp.int32),
            pltpu.VMEM((rest // GROUP, TOP // 2, high_dev, LANES), jnp.int32),
            pltpu.VMEM((high_dev, high_dev), jnp.bfloat16),
            pltpu.VMEM((TOP, STEP, high_dev, NLOW), jnp.bfloat16),
            pltpu.VMEM((TOP, STEP, high_dev, NLOW), jnp.bfloat16),
            pltpu.VMEM((HALVED, 2 * GROUP, high_dev, NLOW), jnp.bfloat16),
            pltpu.VMEM((HALVED, 2 * GROUP, high_dev, NLOW), jnp.bfloat16),
            pltpu.VMEM((HALVED, groups, points), jnp.int32),
            pltpu.VMEM((HALVED * groups, NLOW, points), jnp.bfloat16),
            pltpu.VMEM((HALVED * groups, 24, points), jnp.float32),
            pltpu.VMEM((HALVED * groups, PACK, points), jnp.float32),
            pltpu.VMEM((HALVED, groups, points), jnp.float32),
            pltpu.SemaphoreType.DMA((SLOTS,)),
            pltpu.SemaphoreType.DMA,
        ],
        compiler_params=pltpu.CompilerParams(vmem_limit_bytes=62 * 1024 * 1024),
        cost_estimate=pl.CostEstimate(
            flops=4 * NLOW * high_dev * NMID * NLOW, bytes_accessed=4 * gradients.size, transcendentals=0
        ),
        name="sketch",
    )(place, grads, words, sub_index.reshape(kept // LANES, LANES))


def swapped(value, axis, size, bits):
    return lax.ppermute(value, axis, [(i, i ^ bits) for i in range(size)])


def score_kernel(*refs, scale):
    *sketches, own_tests, near_tests, out_ref, lines = refs

    @pl.when(pl.program_id(0) == 0)
    def _():
        out_ref[...] = jnp.zeros_like(out_ref)

    for n, sketch in enumerate(sketches):
        whole = sketch[...].astype(jnp.float32)
        for row in range(whole.shape[0]):
            lines[n : n + 1, row * LANES : (row + 1) * LANES] = whole[row : row + 1, :]
    left = lines[...].astype(jnp.bfloat16)
    for n, tests in enumerate([own_tests] + [near_tests.at[s] for s in range(near_tests.shape[0])]):
        found = lax.dot_general(
            left, tests[...], (((1,), (1,)), ((), ())), preferred_element_type=jnp.float32
        )
        out_ref[:, n * tests.shape[0] : (n + 1) * tests.shape[0]] += found[: len(sketches)] * scale


def scores_of(sketches, own_tests, near_tests, scale):
    tests, kept = own_tests.shape
    count, near = len(sketches), near_tests.shape[0]
    step = PACK * LANES
    return pl.pallas_call(
        functools.partial(score_kernel, scale=scale),
        grid=(kept // step,),
        out_shape=jax.ShapeDtypeStruct((count, tests * (1 + near)), jnp.float32),
        in_specs=[pl.BlockSpec((PACK, LANES), lambda n: (n, 0))] * count
        + [
            pl.BlockSpec((tests, step), lambda n: (0, n)),
            pl.BlockSpec((near, tests, step), lambda n: (0, 0, n)),
        ],
        out_specs=pl.BlockSpec((count, tests * (1 + near)), lambda n: (0, 0)),
        scratch_shapes=[pltpu.VMEM((16, step), jnp.float32)],
        compiler_params=pltpu.CompilerParams(vmem_limit_bytes=62 * 1024 * 1024),
        name="scores",
    )(*sketches, own_tests, near_tests)


def on_device(gradients, sign_words, sub_index, test_sketch, *, mesh):
    feat_size, far_size, near_size = (mesh.shape[axis] for axis in ("feat", "far", "near"))
    local_features = gradients.shape[1]
    kept = sub_index.shape[0]
    tests = test_sketch.shape[0]
    high_dev = local_features // (NMID * NLOW)
    feature_scale = float(local_features * feat_size) ** (-0.5)
    score_scale = float(kept) ** (-0.5)
    place = lax.axis_index("feat").astype(jnp.int32).reshape(1)
    near_tests = jnp.stack([swapped(test_sketch, "near", near_size, s) for s in range(1, near_size)])
    shares = partial_sketch(gradients, sign_words, sub_index, place, high_dev, feature_scale)
    sketch = shares
    for s in range(1, feat_size):
        sketch = sketch + swapped(shares, "feat", feat_size, s)
    sketch = sketch.astype(jnp.bfloat16)
    sketches = [sketch] + [swapped(sketch, "far", far_size, s) for s in range(1, far_size)]
    scores = scores_of(sketches, test_sketch, near_tests, score_scale)
    scores = jnp.stack(
        [scores[:1]] + [swapped(scores[s : s + 1], "far", far_size, s) for s in range(1, far_size)]
    )
    scores = scores.reshape(far_size, near_size, tests)
    far, near = lax.axis_index("far"), lax.axis_index("near")
    for b in range(near_size.bit_length() - 1):
        split = scores.reshape(far_size, -1, 2, 1 << b, tests)
        scores = jnp.where(jnp.bitwise_and(near, 1 << b) != 0, split[:, :, ::-1], split)
    for b in range(far_size.bit_length() - 1):
        split = scores.reshape(-1, 2, 1 << b, near_size, tests)
        scores = jnp.where(jnp.bitwise_and(far, 1 << b) != 0, split[:, ::-1], split)
    return scores.reshape(1, -1)


def solution(mesh):
    feat_size, ex_size = mesh.shape["feat"], mesh.shape["ex"]
    far_size = min(4, ex_size)
    mesh = Mesh(mesh.devices.reshape(feat_size, far_size, ex_size // far_size), ("feat", "far", "near"))
    ex = ("far", "near")
    return jax.shard_map(
        functools.partial(on_device, mesh=mesh),
        mesh=mesh,
        in_specs=(P(ex, "feat"), P("feat"), P(), P(ex, None)),
        out_specs=P(ex, None),
        check_vma=False,
    )
```

```python
import functools

import jax
import jax.numpy as jnp
from jax import lax
from jax.experimental import pallas as pl
from jax.experimental.pallas import tpu as pltpu
from jax.sharding import Mesh, PartitionSpec as P

NMID = 256
NLOW = 256
TOP = 8
GROUP = 8
STEP = 4
SLOTS = 3
HALVED = TOP // 2
LANES = 128
PACK = 16
PAIR = 4


def odd_common_bits(left, right):
    return jnp.bitwise_and(lax.population_count(jnp.bitwise_and(left, right)), 1) == 1


def iota(shape, axis):
    return lax.broadcasted_iota(jnp.int32, shape, axis)


def sketch_kernel(
    place_ref, grads, words, sub_ref, out_ref,
    xbuf, wbuf, wpair, table, ybuf0, ybuf1, tbuf0, tbuf1, entries, weights, signs, acc, found_rows, sems, wsem,
    *, high_dev, scale,
):
    high_parts = out_ref.shape[0] * LANES // TOP // high_dev
    rest = NMID // TOP
    chunks = rest // GROUP
    steps = rest // STEP
    groups = high_dev // PACK
    points = entries.shape[2]
    pairs = HALVED * groups
    rounds = GROUP * TOP // PAIR
    turns = STEP * TOP // PAIR
    per_chunk = GROUP // STEP
    blocks = STEP * high_dev // PACK // turns
    half = LANES // 16
    ybuf = (ybuf0, ybuf1)
    tbuf = (tbuf0, tbuf1)

    def grad_copy(step, h):
        return pltpu.make_async_copy(
            grads.at[h, :, pl.ds(step * STEP, STEP)],
            xbuf.at[step % SLOTS, :, :, :, pl.ds(pl.multiple_of(h * NLOW, NLOW), NLOW)],
            sems.at[step % SLOTS],
        )

    def start_copies(step):
        @pl.loop(0, high_dev // 8)
        def _(n):
            for i in range(8):
                grad_copy(step, n * 8 + i).start()

    def wait_copies(step):
        slot = step % SLOTS
        pltpu.make_async_copy(xbuf.at[slot], xbuf.at[slot], sems.at[slot]).wait()

    per_high = NMID * NLOW // 16 // LANES
    word_copy = pltpu.make_async_copy(words, wbuf.at[:, :per_high], wsem)
    word_copy.start()
    start_copies(0)
    start_copies(1)

    out, given = iota(table.shape, 0), iota(table.shape, 1)
    table[...] = jnp.where(
        out // (high_dev // 2) == given % 2,
        jnp.where(odd_common_bits(out % (high_dev // 2), given // 2), -1.0, 1.0),
        0.0,
    ).astype(jnp.bfloat16)
    acc[...] = jnp.zeros_like(acc)
    lane = iota((groups, LANES), 1)
    for j in range(HALVED):
        spot = (lane // 2 % PACK) * TOP + 2 * j + lane % 2
        for part in range(points // LANES):
            line = jnp.zeros((groups, LANES), jnp.int32)
            for n in range(LANES // (2 * PACK)):
                hi = part * (LANES // (2 * PACK)) + n
                rows = sub_ref[hi * groups : (hi + 1) * groups, :]
                taken = jnp.take_along_axis(rows, spot, axis=1, mode="promise_in_bounds")
                line = jnp.where(lane // (2 * PACK) == n, taken, line)
            entries[j, :, part * LANES : (part + 1) * LANES] = line

    def build(e):
        entry = entries[e // groups, pl.ds(e % groups, 1), :]
        row = iota((24, points), 0)
        mask = jnp.where(
            row < 2 * GROUP,
            jnp.bitwise_or(jnp.left_shift(row % GROUP, 8), jnp.left_shift(row // GROUP, 13)),
            jnp.left_shift(row - 2 * GROUP, 11),
        )
        signs[e] = jnp.where(odd_common_bits(entry, mask), -1.0, 1.0)
        weights[e] = jnp.where(
            odd_common_bits(entry, iota((NLOW, points), 0)), -1.0, 1.0
        ).astype(jnp.bfloat16)

    word_copy.wait()
    lines = wbuf.reshape(high_dev * (per_high + 1), 1, LANES)

    @pl.loop(0, high_dev // 8)
    def _(n):
        for c in range(chunks):
            for pair in range(TOP // 2):
                one, two = (
                    lines[
                        pl.ds(n * 8 * (per_high + 1) + (2 * pair + which) * chunks + c, 8, per_high + 1), 0, :
                    ]
                    for which in range(2)
                )
                both = jnp.bitwise_or(one, jnp.left_shift(two, 16))
                for l_hi in range(2):
                    wpair[c, pair, pl.ds(n * 16 + l_hi, 8, 2), :] = both

    def prepare(step, u):
        slot = step % SLOTS
        chunk = step * STEP // GROUP
        lane16 = iota((PACK, LANES), 1)
        bits = [jnp.left_shift(1, lane16 % 16), jnp.left_shift(1, lane16 % 16 + 16)]
        i = u * STEP // turns
        spot = (step % (GROUP // STEP) * STEP + i) * 16 + iota((PACK, LANES), 0) % 2 * half + lane16 // 16
        for n in range(blocks):
            block = (u * blocks + n) % (high_dev // PACK)
            values = [[None, None] for _ in range(TOP)]
            for t in range(2):
                row = pl.multiple_of(t * high_dev + block * PACK, PACK)
                for pair in range(TOP // 2):
                    word = wpair[chunk, pair, pl.ds(row, PACK), :]
                    word = jnp.take_along_axis(word, spot, axis=1, mode="promise_in_bounds")
                    for which in range(2):
                        columns = pl.ds(pl.multiple_of(row * LANES, PACK * LANES), PACK * LANES)
                        value = xbuf[slot, 2 * pair + which, i, :, columns]
                        value = value.reshape(PACK, LANES).astype(jnp.float32)
                        values[2 * pair + which][t] = jnp.where(
                            jnp.bitwise_and(word, bits[which]) != 0, value, -value
                        )
            values = [[one + two, one - two] for one, two in values]
            for reach in (2, 4):
                nxt = list(values)
                for at in range(TOP):
                    if not at & reach:
                        nxt[at] = [values[at][t] + values[at + reach][t] for t in range(2)]
                        nxt[at + reach] = [values[at][t] - values[at + reach][t] for t in range(2)]
                values = nxt
            rows = pl.ds(pl.multiple_of(block * PACK, PACK), PACK)
            for top in range(TOP):
                for t in range(2):
                    ybuf[step % 2][top, i, rows, t * LANES : (t + 1) * LANES] = values[top][t].astype(
                        jnp.bfloat16
                    )

    def transform_high(step, u):
        first, i = u * PAIR % TOP, u * PAIR // TOP
        columns = [ybuf[step % 2][first + n, i] for n in range(PAIR)]
        result = jnp.dot(
            table[...], jnp.concatenate(columns, axis=1), preferred_element_type=jnp.float32
        ).astype(jnp.bfloat16)
        chunk = step * STEP // GROUP
        row = step % (GROUP // STEP) * STEP + i
        lower = high_dev // 2
        for n in range(PAIR):
            top = first + n
            for t in range(2):
                for l_hi in range(2):
                    tbuf[chunk % 2][
                        top // 2,
                        n % 2 * GROUP + row,
                        t * lower : (t + 1) * lower,
                        l_hi * LANES : (l_hi + 1) * LANES,
                    ] = result[l_hi * lower : (l_hi + 1) * lower, (2 * n + t) * LANES : (2 * n + t + 1) * LANES]

    def evaluate(chunk, e):
        j, g = e // groups, e % groups
        block = tbuf[chunk % 2][j, :, pl.ds(pl.multiple_of(g * PACK, PACK), PACK), :]
        found = jnp.dot(
            block.reshape(2 * GROUP * PACK, NLOW), weights[e], preferred_element_type=jnp.float32
        )
        total = found[:PACK] * signs[e, 0:1, :]
        for n in range(1, 2 * GROUP):
            total += found[n * PACK : (n + 1) * PACK] * signs[e, n : n + 1, :]
        acc[e] += total * signs[e, 2 * GROUP + chunk : 2 * GROUP + chunk + 1, :]

    def some_pairs(n, do):
        if pairs >= rounds:
            for m in range(pairs // rounds):
                do(n * (pairs // rounds) + m)
        else:
            pl.when(n < pairs)(lambda: do(n))


    wait_copies(0)
    start_copies(2)

    @pl.loop(0, turns)
    def _(u):
        prepare(0, u)

    for step in range(steps):
        if step + 1 < steps:
            wait_copies(step + 1)

        @pl.loop(0, turns)
        def _(u):
            if step + SLOTS < steps:
                for n in range(high_dev // turns):
                    grad_copy(step + SLOTS, u * (high_dev // turns) + n).start()
            if step >= per_chunk:
                some_pairs(step % per_chunk * turns + u, functools.partial(evaluate, step // per_chunk - 1))
            else:
                some_pairs(step * turns + u, build)
            transform_high(step, u)
            if step + 1 < steps:
                prepare(step + 1, u)

    @pl.loop(0, pairs)
    def _(e):
        evaluate(chunks - 1, e)
        own = iota((PACK, points), 1) // 2 % PACK == iota((PACK, points), 0)
        found_rows[e // groups, pl.ds(e % groups, 1), :] = jnp.sum(
            jnp.where(own, acc[e], 0.0), axis=0, keepdims=True
        )

    place = place_ref[0]
    for hi in range(high_parts):
        common = jnp.bitwise_and(place, hi)
        odd = jnp.bitwise_and(common ^ (common >> 1) ^ (common >> 2) ^ (common >> 3), 1)
        sign = jnp.where(odd == 1, -scale, scale)
        part, first = divmod(hi * 2 * PACK, LANES)
        spot = first + lane // TOP * 2 + lane % 2
        line = jnp.zeros((groups, LANES), jnp.float32)
        for j in range(HALVED):
            rows = found_rows[j, :, part * LANES : (part + 1) * LANES]
            taken = jnp.take_along_axis(rows, spot, axis=1, mode="promise_in_bounds")
            line = jnp.where(lane % TOP // 2 == j, taken, line)
        out_ref[hi * groups : (hi + 1) * groups, :] = line * sign


def partial_sketch(gradients, sign_words, sub_index, place, high_dev, scale):
    kept = sub_index.shape[0]
    rest = NMID // TOP
    groups = high_dev // PACK
    points = kept // (HALVED * groups)
    grads = gradients.reshape(high_dev, TOP, rest, 1, NLOW)
    words = sign_words.reshape(high_dev, -1, 1, LANES)
    return pl.pallas_call(
        functools.partial(sketch_kernel, high_dev=high_dev, scale=scale),
        out_shape=jax.ShapeDtypeStruct((kept // LANES, LANES), jnp.float32),
        in_specs=[
            pl.BlockSpec(memory_space=pltpu.SMEM),
            pl.BlockSpec(memory_space=pl.ANY),
            pl.BlockSpec(memory_space=pl.ANY),
            pl.BlockSpec(memory_space=pltpu.VMEM),
        ],
        out_specs=pl.BlockSpec(memory_space=pltpu.VMEM),
        scratch_shapes=[
            pltpu.VMEM((SLOTS, TOP, STEP, 1, high_dev * NLOW), jnp.bfloat16),
            pltpu.VMEM((high_dev, words.shape[1] + 1, 1, LANES), jnp.int32),
            pltpu.VMEM((rest // GROUP, TOP // 2, 2 * high_dev, LANES), jnp.int32),
            pltpu.VMEM((high_dev, high_dev), jnp.bfloat16),
            pltpu.VMEM((TOP, STEP, high_dev, NLOW), jnp.bfloat16),
            pltpu.VMEM((TOP, STEP, high_dev, NLOW), jnp.bfloat16),
            pltpu.VMEM((HALVED, 2 * GROUP, high_dev, NLOW), jnp.bfloat16),
            pltpu.VMEM((HALVED, 2 * GROUP, high_dev, NLOW), jnp.bfloat16),
            pltpu.VMEM((HALVED, groups, points), jnp.int32),
            pltpu.VMEM((HALVED * groups, NLOW, points), jnp.bfloat16),
            pltpu.VMEM((HALVED * groups, 24, points), jnp.float32),
            pltpu.VMEM((HALVED * groups, PACK, points), jnp.float32),
            pltpu.VMEM((HALVED, groups, points), jnp.float32),
            pltpu.SemaphoreType.DMA((SLOTS,)),
            pltpu.SemaphoreType.DMA,
        ],
        compiler_params=pltpu.CompilerParams(vmem_limit_bytes=65000 * 1024),
        cost_estimate=pl.CostEstimate(
            flops=4 * NLOW * high_dev * NMID * NLOW, bytes_accessed=4 * gradients.size, transcendentals=0
        ),
        name="sketch",
    )(place, grads, words, sub_index.reshape(kept // LANES, LANES))


def swapped(value, axis, size, bits):
    return lax.ppermute(value, axis, [(i, i ^ bits) for i in range(size)])


def score_kernel(*refs, scale):
    *sketches, own_tests, near_tests, out_ref, lines = refs
    for n, sketch in enumerate(sketches):
        whole = sketch[...].astype(jnp.float32)
        for row in range(whole.shape[0]):
            lines[n : n + 1, row * LANES : (row + 1) * LANES] = whole[row : row + 1, :]
    left = lines[...].astype(jnp.bfloat16)
    for n, tests in enumerate([own_tests] + [near_tests.at[s] for s in range(near_tests.shape[0])]):
        found = lax.dot_general(
            left, tests[...], (((1,), (1,)), ((), ())), preferred_element_type=jnp.float32
        )
        found = found[: len(sketches)] * scale
        out_ref[:, n * tests.shape[0] : (n + 1) * tests.shape[0]] = found


def scores_of(sketches, own_tests, near_tests, scale):
    tests, kept = own_tests.shape
    count = len(sketches)
    return pl.pallas_call(
        functools.partial(score_kernel, scale=scale),
        out_shape=jax.ShapeDtypeStruct((count, tests * (1 + near_tests.shape[0])), jnp.float32),
        scratch_shapes=[pltpu.VMEM((16, kept), jnp.float32)],
        compiler_params=pltpu.CompilerParams(vmem_limit_bytes=32 * 1024 * 1024),
        name="scores",
    )(*sketches, own_tests, near_tests)


def on_device(gradients, sign_words, sub_index, test_sketch, *, mesh):
    feat_size, far_size, near_size = (mesh.shape[axis] for axis in ("feat", "far", "near"))
    local_features = gradients.shape[1]
    kept = sub_index.shape[0]
    tests = test_sketch.shape[0]
    high_dev = local_features // (NMID * NLOW)
    feature_scale = float(local_features * feat_size) ** (-0.5)
    score_scale = float(kept) ** (-0.5)
    place = lax.axis_index("feat").astype(jnp.int32).reshape(1)
    near_tests = jnp.stack([swapped(test_sketch, "near", near_size, s) for s in range(1, near_size)])
    shares = partial_sketch(gradients, sign_words, sub_index, place, high_dev, feature_scale)
    sketch = shares
    for s in range(1, feat_size):
        sketch = sketch + swapped(shares, "feat", feat_size, s)
    sketch = sketch.astype(jnp.bfloat16)
    sketches = [sketch] + [swapped(sketch, "far", far_size, s) for s in range(1, far_size)]
    scores = scores_of(sketches, test_sketch, near_tests, score_scale)
    scores = jnp.stack(
        [scores[:1]] + [swapped(scores[s : s + 1], "far", far_size, s) for s in range(1, far_size)]
    )
    scores = scores.reshape(far_size, near_size, tests)
    far, near = lax.axis_index("far"), lax.axis_index("near")
    for b in range(near_size.bit_length() - 1):
        split = scores.reshape(far_size, -1, 2, 1 << b, tests)
        scores = jnp.where(jnp.bitwise_and(near, 1 << b) != 0, split[:, :, ::-1], split)
    for b in range(far_size.bit_length() - 1):
        split = scores.reshape(-1, 2, 1 << b, near_size, tests)
        scores = jnp.where(jnp.bitwise_and(far, 1 << b) != 0, split[:, ::-1], split)
    return scores.reshape(1, -1)


def solution(mesh):
    feat_size, ex_size = mesh.shape["feat"], mesh.shape["ex"]
    far_size = min(4, ex_size)
    mesh = Mesh(mesh.devices.reshape(feat_size, far_size, ex_size // far_size), ("feat", "far", "near"))
    ex = ("far", "near")
    return jax.shard_map(
        functools.partial(on_device, mesh=mesh),
        mesh=mesh,
        in_specs=(P(ex, "feat"), P("feat"), P(), P(ex, None)),
        out_specs=P(ex, None),
        check_vma=False,
    )
```

```python
import functools

import jax
import jax.numpy as jnp
from jax import lax
from jax.experimental import pallas as pl
from jax.experimental.pallas import tpu as pltpu
from jax.sharding import Mesh, PartitionSpec as P

NMID = 256
NLOW = 256
TOP = 8
GROUP = 8
STEP = 4
SLOTS = 3
HALVED = TOP // 2
LANES = 128
PACK = 16
PAIR = 4


def odd_common_bits(left, right):
    return jnp.bitwise_and(lax.population_count(jnp.bitwise_and(left, right)), 1) == 1


def iota(shape, axis):
    return lax.broadcasted_iota(jnp.int32, shape, axis)


def sketch_kernel(
    place_ref, grads, words, sub_ref, out_ref,
    xbuf, wbuf, wpair, table, ybuf0, ybuf1, tbuf0, tbuf1, entries, weights, signs, acc, found_rows, sems, wsem,
    *, high_dev, scale,
):
    high_parts = out_ref.shape[0] * LANES // TOP // high_dev
    rest = NMID // TOP
    chunks = rest // GROUP
    steps = rest // STEP
    groups = high_dev // PACK
    points = entries.shape[2]
    pairs = HALVED * groups
    rounds = GROUP * TOP // PAIR
    turns = STEP * TOP // PAIR
    per_chunk = GROUP // STEP
    blocks = STEP * high_dev // PACK // turns
    half = LANES // 16
    ybuf = (ybuf0, ybuf1)
    tbuf = (tbuf0, tbuf1)

    def grad_copy(step, h):
        return pltpu.make_async_copy(
            grads.at[h, :, pl.ds(step * STEP, STEP)],
            xbuf.at[step % SLOTS, :, :, :, pl.ds(pl.multiple_of(h * NLOW, NLOW), NLOW)],
            sems.at[step % SLOTS],
        )

    def start_copies(step):
        @pl.loop(0, high_dev // 8)
        def _(n):
            for i in range(8):
                grad_copy(step, n * 8 + i).start()

    def wait_copies(step):
        slot = step % SLOTS
        pltpu.make_async_copy(xbuf.at[slot], xbuf.at[slot], sems.at[slot]).wait()

    per_high = NMID * NLOW // 16 // LANES
    word_copy = pltpu.make_async_copy(words, wbuf.at[:, :per_high], wsem)
    word_copy.start()
    start_copies(0)
    start_copies(1)

    out, given = iota(table.shape, 0), iota(table.shape, 1)
    table[...] = jnp.where(
        out // (high_dev // 2) == given % 2,
        jnp.where(odd_common_bits(out % (high_dev // 2), given // 2), -1.0, 1.0),
        0.0,
    ).astype(jnp.bfloat16)
    acc[...] = jnp.zeros_like(acc)
    lane = iota((groups, LANES), 1)
    for j in range(HALVED):
        spot = (lane // 2 % PACK) * TOP + 2 * j + lane % 2
        for part in range(points // LANES):
            line = jnp.zeros((groups, LANES), jnp.int32)
            for n in range(LANES // (2 * PACK)):
                hi = part * (LANES // (2 * PACK)) + n
                rows = sub_ref[hi * groups : (hi + 1) * groups, :]
                taken = jnp.take_along_axis(rows, spot, axis=1, mode="promise_in_bounds")
                line = jnp.where(lane // (2 * PACK) == n, taken, line)
            entries[j, :, part * LANES : (part + 1) * LANES] = line

    def build(e):
        entry = entries[e // groups, pl.ds(e % groups, 1), :]
        row = iota((24, points), 0)
        mask = jnp.where(
            row < 2 * GROUP,
            jnp.bitwise_or(jnp.left_shift(row % GROUP, 8), jnp.left_shift(row // GROUP, 13)),
            jnp.left_shift(row - 2 * GROUP, 11),
        )
        signs[e] = jnp.where(odd_common_bits(entry, mask), -1.0, 1.0)
        weights[e] = jnp.where(
            odd_common_bits(entry, iota((NLOW, points), 0)), -1.0, 1.0
        ).astype(jnp.bfloat16)

    word_copy.wait()
    lines = wbuf.reshape(high_dev * (per_high + 1), 1, LANES)

    @pl.loop(0, high_dev // 8)
    def _(n):
        for c in range(chunks):
            for pair in range(TOP // 2):
                one, two = (
                    lines[
                        pl.ds(n * 8 * (per_high + 1) + (2 * pair + which) * chunks + c, 8, per_high + 1), 0, :
                    ]
                    for which in range(2)
                )
                both = jnp.bitwise_or(one, jnp.left_shift(two, 16))
                for l_hi in range(2):
                    wpair[c, pair, pl.ds(n * 16 + l_hi, 8, 2), :] = both

    def prepare(step, u, part, parts):
        slot = step % SLOTS
        chunk = step * STEP // GROUP
        lane16 = iota((PACK, LANES), 1)
        bits = [jnp.left_shift(1, lane16 % 16), jnp.left_shift(1, lane16 % 16 + 16)]
        i = u * STEP // turns
        spot = (step % (GROUP // STEP) * STEP + i) * 16 + iota((PACK, LANES), 0) % 2 * half + lane16 // 16
        for n in range(part * blocks // parts, (part + 1) * blocks // parts):
            block = (u * blocks + n) % (high_dev // PACK)
            values = [[None, None] for _ in range(TOP)]
            for t in range(2):
                row = pl.multiple_of(t * high_dev + block * PACK, PACK)
                for pair in range(TOP // 2):
                    word = wpair[chunk, pair, pl.ds(row, PACK), :]
                    word = jnp.take_along_axis(word, spot, axis=1, mode="promise_in_bounds")
                    for which in range(2):
                        columns = pl.ds(pl.multiple_of(row * LANES, PACK * LANES), PACK * LANES)
                        value = xbuf[slot, 2 * pair + which, i, :, columns]
                        value = value.reshape(PACK, LANES).astype(jnp.float32)
                        values[2 * pair + which][t] = jnp.where(
                            jnp.bitwise_and(word, bits[which]) != 0, value, -value
                        )
            values = [[one + two, one - two] for one, two in values]
            for reach in (2, 4):
                nxt = list(values)
                for at in range(TOP):
                    if not at & reach:
                        nxt[at] = [values[at][t] + values[at + reach][t] for t in range(2)]
                        nxt[at + reach] = [values[at][t] - values[at + reach][t] for t in range(2)]
                values = nxt
            rows = pl.ds(pl.multiple_of(block * PACK, PACK), PACK)
            for top in range(TOP):
                for t in range(2):
                    ybuf[step % 2][top, i, rows, t * LANES : (t + 1) * LANES] = values[top][t].astype(
                        jnp.bfloat16
                    )

    def transform_high(step, u, n):
        top, i = u * PAIR % TOP + n, u * PAIR // TOP
        result = jnp.dot(table[...], ybuf[step % 2][top, i], preferred_element_type=jnp.float32)
        result = result.astype(jnp.bfloat16)
        chunk = step * STEP // GROUP
        row = step % (GROUP // STEP) * STEP + i
        lower = high_dev // 2
        for t in range(2):
            for l_hi in range(2):
                tbuf[chunk % 2][
                    top // 2,
                    n % 2 * GROUP + row,
                    t * lower : (t + 1) * lower,
                    l_hi * LANES : (l_hi + 1) * LANES,
                ] = result[l_hi * lower : (l_hi + 1) * lower, t * LANES : (t + 1) * LANES]

    def evaluate(chunk, e):
        j, g = e // groups, e % groups
        block = tbuf[chunk % 2][j, :, pl.ds(pl.multiple_of(g * PACK, PACK), PACK), :]
        found = jnp.dot(
            block.reshape(2 * GROUP * PACK, NLOW), weights[e], preferred_element_type=jnp.float32
        )
        total = found[:PACK] * signs[e, 0:1, :]
        for n in range(1, 2 * GROUP):
            total += found[n * PACK : (n + 1) * PACK] * signs[e, n : n + 1, :]
        acc[e] += total * signs[e, 2 * GROUP + chunk : 2 * GROUP + chunk + 1, :]

    def some_pairs(n, part, do):
        if pairs >= PAIR * rounds:
            for m in range(pairs // (PAIR * rounds)):
                do((n * PAIR + part) * (pairs // (PAIR * rounds)) + m)
        elif part % (PAIR * rounds // pairs) == 0:
            do((n * PAIR + part) // (PAIR * rounds // pairs))

    wait_copies(0)
    start_copies(2)

    @pl.loop(0, turns)
    def _(u):
        prepare(0, u, 0, 1)

    for step in range(steps):
        if step + 1 < steps:
            wait_copies(step + 1)

        @pl.loop(0, turns)
        def _(u):
            if step + SLOTS < steps:
                for n in range(high_dev // turns):
                    grad_copy(step + SLOTS, u * (high_dev // turns) + n).start()
            for part in range(PAIR):
                if step >= per_chunk:
                    some_pairs(
                        step % per_chunk * turns + u,
                        part,
                        functools.partial(evaluate, step // per_chunk - 1),
                    )
                else:
                    some_pairs(step * turns + u, part, build)
                transform_high(step, u, part)
                if step + 1 < steps:
                    prepare(step + 1, u, part, PAIR)

    @pl.loop(0, pairs)
    def _(e):
        evaluate(chunks - 1, e)
        own = iota((PACK, points), 1) // 2 % PACK == iota((PACK, points), 0)
        found_rows[e // groups, pl.ds(e % groups, 1), :] = jnp.sum(
            jnp.where(own, acc[e], 0.0), axis=0, keepdims=True
        )

    place = place_ref[0]
    for hi in range(high_parts):
        common = jnp.bitwise_and(place, hi)
        odd = jnp.bitwise_and(common ^ (common >> 1) ^ (common >> 2) ^ (common >> 3), 1)
        sign = jnp.where(odd == 1, -scale, scale)
        part, first = divmod(hi * 2 * PACK, LANES)
        spot = first + lane // TOP * 2 + lane % 2
        line = jnp.zeros((groups, LANES), jnp.float32)
        for j in range(HALVED):
            rows = found_rows[j, :, part * LANES : (part + 1) * LANES]
            taken = jnp.take_along_axis(rows, spot, axis=1, mode="promise_in_bounds")
            line = jnp.where(lane % TOP // 2 == j, taken, line)
        out_ref[hi * groups : (hi + 1) * groups, :] = line * sign


def partial_sketch(gradients, sign_words, sub_index, place, high_dev, scale):
    kept = sub_index.shape[0]
    rest = NMID // TOP
    groups = high_dev // PACK
    points = kept // (HALVED * groups)
    grads = gradients.reshape(high_dev, TOP, rest, 1, NLOW)
    words = sign_words.reshape(high_dev, -1, 1, LANES)
    return pl.pallas_call(
        functools.partial(sketch_kernel, high_dev=high_dev, scale=scale),
        out_shape=jax.ShapeDtypeStruct((kept // LANES, LANES), jnp.float32),
        in_specs=[
            pl.BlockSpec(memory_space=pltpu.SMEM),
            pl.BlockSpec(memory_space=pl.ANY),
            pl.BlockSpec(memory_space=pl.ANY),
            pl.BlockSpec(memory_space=pltpu.VMEM),
        ],
        out_specs=pl.BlockSpec(memory_space=pltpu.VMEM),
        scratch_shapes=[
            pltpu.VMEM((SLOTS, TOP, STEP, 1, high_dev * NLOW), jnp.bfloat16),
            pltpu.VMEM((high_dev, words.shape[1] + 1, 1, LANES), jnp.int32),
            pltpu.VMEM((rest // GROUP, TOP // 2, 2 * high_dev, LANES), jnp.int32),
            pltpu.VMEM((high_dev, high_dev), jnp.bfloat16),
            pltpu.VMEM((TOP, STEP, high_dev, NLOW), jnp.bfloat16),
            pltpu.VMEM((TOP, STEP, high_dev, NLOW), jnp.bfloat16),
            pltpu.VMEM((HALVED, 2 * GROUP, high_dev, NLOW), jnp.bfloat16),
            pltpu.VMEM((HALVED, 2 * GROUP, high_dev, NLOW), jnp.bfloat16),
            pltpu.VMEM((HALVED, groups, points), jnp.int32),
            pltpu.VMEM((HALVED * groups, NLOW, points), jnp.bfloat16),
            pltpu.VMEM((HALVED * groups, 24, points), jnp.float32),
            pltpu.VMEM((HALVED * groups, PACK, points), jnp.float32),
            pltpu.VMEM((HALVED, groups, points), jnp.float32),
            pltpu.SemaphoreType.DMA((SLOTS,)),
            pltpu.SemaphoreType.DMA,
        ],
        compiler_params=pltpu.CompilerParams(vmem_limit_bytes=65000 * 1024),
        cost_estimate=pl.CostEstimate(
            flops=4 * NLOW * high_dev * NMID * NLOW, bytes_accessed=4 * gradients.size, transcendentals=0
        ),
        name="sketch",
    )(place, grads, words, sub_index.reshape(kept // LANES, LANES))


def swapped(value, axis, size, bits):
    return lax.ppermute(value, axis, [(i, i ^ bits) for i in range(size)])


def score_kernel(*refs, scale, cuts):
    *sketches, own_tests, near_tests, out_ref, lines, held, sems = refs
    sources = [own_tests] + [near_tests.at[s] for s in range(near_tests.shape[0])]
    tests, kept = own_tests.shape
    wide = kept // cuts
    copies = [
        [
            pltpu.make_async_copy(
                source.at[:, cut * wide : (cut + 1) * wide],
                held.at[n * tests : (n + 1) * tests, cut * wide : (cut + 1) * wide],
                sems.at[n, cut],
            )
            for n, source in enumerate(sources)
        ]
        for cut in range(cuts)
    ]
    for cut in range(cuts):
        for copy in copies[cut]:
            copy.start()
    for n, sketch in enumerate(sketches):
        whole = sketch[...].astype(jnp.float32)
        for row in range(whole.shape[0]):
            lines[n : n + 1, row * LANES : (row + 1) * LANES] = whole[row : row + 1, :]
    left = lines[...].astype(jnp.bfloat16)
    total = jnp.zeros(out_ref.shape, jnp.float32)
    for cut in range(cuts):
        for copy in copies[cut]:
            copy.wait()
        columns = slice(cut * wide, (cut + 1) * wide)
        total += lax.dot_general(
            held[:, columns],
            left[:, columns],
            (((1,), (1,)), ((), ())),
            preferred_element_type=jnp.float32,
        )
    out_ref[...] = total * scale


def scores_of(sketches, own_tests, near_tests, scale):
    tests, kept = own_tests.shape
    places = 1 + near_tests.shape[0]
    cuts = 4
    found = pl.pallas_call(
        functools.partial(score_kernel, scale=scale, cuts=cuts),
        out_shape=jax.ShapeDtypeStruct((places * tests, PACK), jnp.float32),
        in_specs=[pl.BlockSpec(memory_space=pltpu.VMEM)] * len(sketches)
        + [pl.BlockSpec(memory_space=pl.ANY)] * 2,
        out_specs=pl.BlockSpec(memory_space=pltpu.VMEM),
        scratch_shapes=[
            pltpu.VMEM((PACK, kept), jnp.float32),
            pltpu.VMEM((places * tests, kept), jnp.bfloat16),
            pltpu.SemaphoreType.DMA((places, cuts)),
        ],
        compiler_params=pltpu.CompilerParams(vmem_limit_bytes=62 * 1024 * 1024),
        name="scores",
    )(*sketches, own_tests, near_tests)
    return found.T[: len(sketches)]


def on_device(gradients, sign_words, sub_index, test_sketch, *, mesh):
    feat_size, far_size, near_size = (mesh.shape[axis] for axis in ("feat", "far", "near"))
    local_features = gradients.shape[1]
    kept = sub_index.shape[0]
    tests = test_sketch.shape[0]
    high_dev = local_features // (NMID * NLOW)
    feature_scale = float(local_features * feat_size) ** (-0.5)
    score_scale = float(kept) ** (-0.5)
    place = lax.axis_index("feat").astype(jnp.int32).reshape(1)
    near_tests = jnp.stack([swapped(test_sketch, "near", near_size, s) for s in range(1, near_size)])
    shares = partial_sketch(gradients, sign_words, sub_index, place, high_dev, feature_scale)
    sketch = shares
    for s in range(1, feat_size):
        sketch = sketch + swapped(shares, "feat", feat_size, s)
    sketch = sketch.astype(jnp.bfloat16)
    sketches = [sketch] + [swapped(sketch, "far", far_size, s) for s in range(1, far_size)]
    scores = scores_of(sketches, test_sketch, near_tests, score_scale)
    scores = jnp.stack(
        [scores[:1]] + [swapped(scores[s : s + 1], "far", far_size, s) for s in range(1, far_size)]
    )
    scores = scores.reshape(far_size, near_size, tests)
    far, near = lax.axis_index("far"), lax.axis_index("near")
    for b in range(near_size.bit_length() - 1):
        split = scores.reshape(far_size, -1, 2, 1 << b, tests)
        scores = jnp.where(jnp.bitwise_and(near, 1 << b) != 0, split[:, :, ::-1], split)
    for b in range(far_size.bit_length() - 1):
        split = scores.reshape(-1, 2, 1 << b, near_size, tests)
        scores = jnp.where(jnp.bitwise_and(far, 1 << b) != 0, split[:, ::-1], split)
    return scores.reshape(1, -1)


def solution(mesh):
    feat_size, ex_size = mesh.shape["feat"], mesh.shape["ex"]
    far_size = min(4, ex_size)
    mesh = Mesh(mesh.devices.reshape(feat_size, far_size, ex_size // far_size), ("feat", "far", "near"))
    ex = ("far", "near")
    return jax.shard_map(
        functools.partial(on_device, mesh=mesh),
        mesh=mesh,
        in_specs=(P(ex, "feat"), P("feat"), P(), P(ex, None)),
        out_specs=P(ex, None),
        check_vma=False,
    )
```

```python
import functools

import jax
import jax.numpy as jnp
from jax import lax
from jax.experimental import pallas as pl
from jax.experimental.pallas import tpu as pltpu
from jax.sharding import Mesh, PartitionSpec as P

NMID = 256
NLOW = 256
TOP = 8
REST = NMID // TOP
TURN = 4
SLOTS = 3
LANES = 128
PACK = 16


def odd_common_bits(left, right):
    return jnp.bitwise_and(lax.population_count(jnp.bitwise_and(left, right)), 1) == 1


def iota(shape, axis):
    return lax.broadcasted_iota(jnp.int32, shape, axis)


def sketch_kernel(
    place_ref, grads, words, sub_ref, out_ref,
    xbuf, wbuf, wpair, low_table, high_table, signed0, signed1, first0, first1, spots, signs, acc, sems, wsem,
    *, high_dev, scale,
):
    high_parts = out_ref.shape[0] * LANES // TOP // high_dev
    groups = high_dev // PACK
    per_high = words.shape[1]
    turns = REST // TURN
    copies = high_dev // turns
    half = LANES // 16
    signed, first = (signed0, signed1), (first0, first1)

    def grad_copy(step, h):
        slot = lax.rem(step, SLOTS)
        return pltpu.make_async_copy(
            grads.at[h, step],
            xbuf.at[slot, :, :, pl.ds(pl.multiple_of(h * LANES, LANES), LANES)],
            sems.at[slot],
        )

    def start_copies(step):
        @pl.loop(0, high_dev // 8)
        def _(n):
            for i in range(8):
                grad_copy(step, n * 8 + i).start()

    def wait_copies(step):
        slot = lax.rem(step, SLOTS)
        pltpu.make_async_copy(xbuf.at[slot], xbuf.at[slot], sems.at[slot]).wait()

    word_copy = pltpu.make_async_copy(words, wbuf.at[:, :per_high], wsem)
    word_copy.start()
    start_copies(0)
    start_copies(1)

    for table in (low_table, high_table):
        table[...] = jnp.where(
            odd_common_bits(iota(table.shape, 0), iota(table.shape, 1)), -1.0, 1.0
        ).astype(jnp.bfloat16)
    acc[...] = jnp.zeros_like(acc)
    lane16 = iota((PACK, LANES), 1)
    row16 = iota((PACK, LANES), 0)

    @pl.loop(0, groups)
    def _(g):
        entry = jnp.zeros((PACK, LANES), jnp.int32)
        for hi in range(high_parts):
            line = jnp.broadcast_to(sub_ref[pl.ds(hi * groups + g, 1), :], (PACK, LANES))
            taken = jnp.take_along_axis(line, row16 * TOP + lane16 % TOP, axis=1, mode="promise_in_bounds")
            entry = jnp.where(lane16 // TOP == hi, taken, entry)
        rows = pl.ds(pl.multiple_of(g * PACK, PACK), PACK)
        spots[rows, :] = jnp.bitwise_and(entry, NLOW - 1)
        for mid in range(REST):
            signs[mid, rows, :] = jnp.where(odd_common_bits(entry, mid * NLOW), -1.0, 1.0)

    word_copy.wait()
    lines = wbuf.reshape(high_dev * (per_high + 1), 1, LANES)

    @pl.loop(0, high_dev // 8)
    def _(n):
        for pair in range(per_high // 2):
            one, two = (
                lines[pl.ds(n * 8 * (per_high + 1) + 2 * pair + which, 8, per_high + 1), 0, :]
                for which in range(2)
            )
            wpair[pair, pl.ds(pl.multiple_of(n * 8, 8), 8), :] = jnp.bitwise_or(
                one, jnp.left_shift(two, 16)
            )

    def prepare(n, parity):
        step, i = n // turns, lax.rem(n, turns)
        slot = lax.rem(step, SLOTS)
        bits = [jnp.left_shift(1, lane16 % 16), jnp.left_shift(1, lane16 % 16 + 16)]
        for block in range(groups):
            rows = slice(block * PACK, (block + 1) * PACK)
            columns = slice(block * PACK * LANES, (block + 1) * PACK * LANES)
            for pair in range(TURN // 2):
                packed = wpair[step * (TURN // 2) + pair, rows, :]
                for l_hi in range(2):
                    spot = i * 16 + l_hi * half + lane16 // 16
                    word = jnp.take_along_axis(packed, spot, axis=1, mode="promise_in_bounds")
                    for which in range(2):
                        c = 2 * pair + which
                        value = xbuf[slot, (c * turns + i) * 2 + l_hi, :, columns]
                        value = value.reshape(PACK, LANES).astype(jnp.float32)
                        value = jnp.where(jnp.bitwise_and(word, bits[which]) != 0, value, -value)
                        signed[parity][
                            c * high_dev + block * PACK : c * high_dev + (block + 1) * PACK,
                            l_hi * LANES : (l_hi + 1) * LANES,
                        ] = value.astype(jnp.bfloat16)

    def transform_low(parity):
        first[parity][...] = jnp.dot(
            signed[parity][...], low_table[...], preferred_element_type=jnp.float32
        ).astype(jnp.bfloat16)

    def transform_high(n, parity, c):
        step, i = n // turns, lax.rem(n, turns)
        found = jnp.dot(
            high_table[...],
            first[parity][c * high_dev : (c + 1) * high_dev, :],
            preferred_element_type=jnp.float32,
        )
        spot = spots[...]
        low = jnp.bitwise_and(spot, LANES - 1)
        zero = jnp.take_along_axis(found[:, :LANES], low, axis=1, mode="promise_in_bounds")
        one = jnp.take_along_axis(found[:, LANES:], low, axis=1, mode="promise_in_bounds")
        acc[step, c] += jnp.where(spot >= LANES, one, zero) * signs[c * turns + i]

    def turn(n, parity, with_prepare, with_low, with_copies):
        if with_prepare:

            @pl.when(lax.rem(n + 2, turns) == 0)
            def _():
                wait_copies((n + 2) // turns)

        if with_copies:
            for m in range(copies):
                grad_copy((n + 2) // turns + 2, lax.rem(n + 2, turns) * copies + m).start()
        for c in range(TURN):
            transform_high(n, parity, c)
        if with_low:
            transform_low(1 - parity)
        if with_prepare:
            prepare(n + 2, parity)

    wait_copies(0)
    for n in range(2):
        for m in range(copies):
            grad_copy(2, n * copies + m).start()
        prepare(n, n)
    transform_low(0)

    last = TOP * turns
    ends = last - 2 * turns - 2

    @pl.loop(0, ends // 2)
    def _(n):
        for parity in range(2):
            turn(2 * n + parity, parity, True, True, True)

    @pl.loop(ends // 2, last // 2 - 1)
    def _(n):
        for parity in range(2):
            turn(2 * n + parity, parity, True, True, False)

    turn(last - 2, 0, False, True, False)
    turn(last - 1, 1, False, False, False)

    place = place_ref[0]
    for g in range(groups):
        rows = slice(g * PACK, (g + 1) * PACK)
        total = jnp.zeros((PACK, LANES), jnp.float32)
        for step in range(TOP):
            part = acc[step, 0, rows, :]
            for c in range(1, TURN):
                part += acc[step, c, rows, :]
            total += jnp.where(odd_common_bits(lane16 % TOP, step), -part, part)
        for hi in range(high_parts):
            taken = jnp.take_along_axis(total, hi * TOP + lane16 % TOP, axis=1, mode="promise_in_bounds")
            line = jnp.where(lane16 // TOP == row16, taken, 0.0)
            common = jnp.bitwise_and(place, hi)
            odd = jnp.bitwise_and(common ^ (common >> 1) ^ (common >> 2) ^ (common >> 3), 1)
            sign = jnp.where(odd == 1, -scale, scale)
            out_ref[hi * groups + g : hi * groups + g + 1, :] = jnp.sum(line, axis=0, keepdims=True) * sign


def partial_sketch(gradients, sign_words, sub_index, place, high_dev, scale):
    kept = sub_index.shape[0]
    grads = gradients.reshape(high_dev, TOP, 2 * REST, 1, LANES)
    words = sign_words.reshape(high_dev, -1, 1, LANES)
    return pl.pallas_call(
        functools.partial(sketch_kernel, high_dev=high_dev, scale=scale),
        out_shape=jax.ShapeDtypeStruct((kept // LANES, LANES), jnp.float32),
        in_specs=[
            pl.BlockSpec(memory_space=pltpu.SMEM),
            pl.BlockSpec(memory_space=pl.ANY),
            pl.BlockSpec(memory_space=pl.ANY),
            pl.BlockSpec(memory_space=pltpu.VMEM),
        ],
        out_specs=pl.BlockSpec(memory_space=pltpu.VMEM),
        scratch_shapes=[
            pltpu.VMEM((SLOTS, 2 * REST, 1, high_dev * LANES), jnp.bfloat16),
            pltpu.VMEM((high_dev, words.shape[1] + 1, 1, LANES), jnp.int32),
            pltpu.VMEM((words.shape[1] // 2, high_dev, LANES), jnp.int32),
            pltpu.VMEM((NLOW, NLOW), jnp.bfloat16),
            pltpu.VMEM((high_dev, high_dev), jnp.bfloat16),
            pltpu.VMEM((TURN * high_dev, NLOW), jnp.bfloat16),
            pltpu.VMEM((TURN * high_dev, NLOW), jnp.bfloat16),
            pltpu.VMEM((TURN * high_dev, NLOW), jnp.bfloat16),
            pltpu.VMEM((TURN * high_dev, NLOW), jnp.bfloat16),
            pltpu.VMEM((high_dev, LANES), jnp.int32),
            pltpu.VMEM((REST, high_dev, LANES), jnp.float32),
            pltpu.VMEM((TOP, TURN, high_dev, LANES), jnp.float32),
            pltpu.SemaphoreType.DMA((SLOTS,)),
            pltpu.SemaphoreType.DMA,
        ],
        compiler_params=pltpu.CompilerParams(vmem_limit_bytes=60 * 1024 * 1024),
        cost_estimate=pl.CostEstimate(
            flops=4 * NLOW * high_dev * NMID * NLOW, bytes_accessed=4 * gradients.size, transcendentals=0
        ),
        name="sketch",
    )(place, grads, words, sub_index.reshape(kept // LANES, LANES))


def swapped(value, axis, size, bits):
    return lax.ppermute(value, axis, [(i, i ^ bits) for i in range(size)])


def score_kernel(*refs, scale):
    *sketches, own_tests, near_tests, out_ref, lines = refs
    for n, sketch in enumerate(sketches):
        whole = sketch[...].astype(jnp.float32)
        for row in range(whole.shape[0]):
            lines[n : n + 1, row * LANES : (row + 1) * LANES] = whole[row : row + 1, :]
    left = lines[...].astype(jnp.bfloat16)
    for n, tests in enumerate([own_tests] + [near_tests.at[s] for s in range(near_tests.shape[0])]):
        found = lax.dot_general(
            left, tests[...], (((1,), (1,)), ((), ())), preferred_element_type=jnp.float32
        )
        found = found[: len(sketches)] * scale
        out_ref[:, n * tests.shape[0] : (n + 1) * tests.shape[0]] = found


def scores_of(sketches, own_tests, near_tests, scale):
    tests, kept = own_tests.shape
    count = len(sketches)
    return pl.pallas_call(
        functools.partial(score_kernel, scale=scale),
        out_shape=jax.ShapeDtypeStruct((count, tests * (1 + near_tests.shape[0])), jnp.float32),
        scratch_shapes=[pltpu.VMEM((16, kept), jnp.float32)],
        compiler_params=pltpu.CompilerParams(vmem_limit_bytes=32 * 1024 * 1024),
        name="scores",
    )(*sketches, own_tests, near_tests)


def on_device(gradients, sign_words, sub_index, test_sketch, *, mesh):
    feat_size, far_size, near_size = (mesh.shape[axis] for axis in ("feat", "far", "near"))
    local_features = gradients.shape[1]
    kept = sub_index.shape[0]
    tests = test_sketch.shape[0]
    high_dev = local_features // (NMID * NLOW)
    feature_scale = float(local_features * feat_size) ** (-0.5)
    score_scale = float(kept) ** (-0.5)
    place = lax.axis_index("feat").astype(jnp.int32).reshape(1)
    near_tests = jnp.stack([swapped(test_sketch, "near", near_size, s) for s in range(1, near_size)])
    shares = partial_sketch(gradients, sign_words, sub_index, place, high_dev, feature_scale)
    sketch = shares
    for s in range(1, feat_size):
        sketch = sketch + swapped(shares, "feat", feat_size, s)
    sketch = sketch.astype(jnp.bfloat16)
    sketches = [sketch] + [swapped(sketch, "far", far_size, s) for s in range(1, far_size)]
    scores = scores_of(sketches, test_sketch, near_tests, score_scale)
    scores = jnp.stack(
        [scores[:1]] + [swapped(scores[s : s + 1], "far", far_size, s) for s in range(1, far_size)]
    )
    scores = scores.reshape(far_size, near_size, tests)
    far, near = lax.axis_index("far"), lax.axis_index("near")
    for b in range(near_size.bit_length() - 1):
        split = scores.reshape(far_size, -1, 2, 1 << b, tests)
        scores = jnp.where(jnp.bitwise_and(near, 1 << b) != 0, split[:, :, ::-1], split)
    for b in range(far_size.bit_length() - 1):
        split = scores.reshape(-1, 2, 1 << b, near_size, tests)
        scores = jnp.where(jnp.bitwise_and(far, 1 << b) != 0, split[:, ::-1], split)
    return scores.reshape(1, -1)


def solution(mesh):
    feat_size, ex_size = mesh.shape["feat"], mesh.shape["ex"]
    far_size = min(4, ex_size)
    mesh = Mesh(mesh.devices.reshape(feat_size, far_size, ex_size // far_size), ("feat", "far", "near"))
    ex = ("far", "near")
    return jax.shard_map(
        functools.partial(on_device, mesh=mesh),
        mesh=mesh,
        in_specs=(P(ex, "feat"), P("feat"), P(), P(ex, None)),
        out_specs=P(ex, None),
        check_vma=False,
    )
```

```python
import functools

import jax
import jax.numpy as jnp
from jax import lax
from jax.experimental import pallas as pl
from jax.experimental.pallas import tpu as pltpu
from jax.sharding import Mesh, PartitionSpec as P

NMID = 256
NLOW = 256
TOP = 8
GROUP = 8
STEP = 4
SLOTS = 2
ROWS = 2 * STEP
HALVED = TOP // 2
LANES = 128
PACK = 16
PAIR = 4


def odd_common_bits(left, right):
    return jnp.bitwise_and(lax.population_count(jnp.bitwise_and(left, right)), 1) == 1


def iota(shape, axis):
    return lax.broadcasted_iota(jnp.int32, shape, axis)


def sketch_kernel(
    place_ref, grads, words, sub_ref, out_ref,
    xbuf, wbuf, wpair, table, ybuf0, ybuf1, tbuf0, tbuf1, entries, weights, signs, acc, found_rows, sems, wsem,
    *, high_dev, scale,
):
    high_parts = out_ref.shape[0] * LANES // TOP // high_dev
    rest = NMID // TOP
    chunks = rest // GROUP
    steps = rest // STEP
    groups = high_dev // PACK
    points = entries.shape[2]
    pairs = HALVED * groups
    rounds = GROUP * TOP // PAIR
    highs = high_dev * PAIR // (STEP * TOP)
    stride = high_dev + 1
    ybuf = (ybuf0, ybuf1)
    tbuf = (tbuf0, tbuf1)

    def grad_copies(step, then):
        slot = step % SLOTS
        for top in range(TOP):
            copy = pltpu.make_async_copy(
                grads.at[:, top, step],
                xbuf.at[slot, :, :, top * ROWS * LANES : (top + 1) * ROWS * LANES],
                sems.at[slot, top],
            )
            then(copy)

    per_high = NMID * NLOW // 16 // LANES
    word_copy = pltpu.make_async_copy(words, wbuf.at[:, :per_high], wsem)
    word_copy.start()
    for step in range(SLOTS):
        grad_copies(step, lambda copy: copy.start())

    table[...] = jnp.where(
        odd_common_bits(iota(table.shape, 0), iota(table.shape, 1)), -1.0, 1.0
    ).astype(jnp.bfloat16)
    acc[...] = jnp.zeros_like(acc)
    lane = iota((groups, LANES), 1)
    for j in range(HALVED):
        spot = (lane // 2 % PACK) * TOP + 2 * j + lane % 2
        for part in range(points // LANES):
            line = jnp.zeros((groups, LANES), jnp.int32)
            for n in range(LANES // (2 * PACK)):
                hi = part * (LANES // (2 * PACK)) + n
                rows = sub_ref[hi * groups : (hi + 1) * groups, :]
                taken = jnp.take_along_axis(rows, spot, axis=1, mode="promise_in_bounds")
                line = jnp.where(lane // (2 * PACK) == n, taken, line)
            entries[j, :, part * LANES : (part + 1) * LANES] = line

    def build(e):
        entry = entries[e // groups, pl.ds(e % groups, 1), :]
        row = iota((24, points), 0)
        mask = jnp.where(
            row < 2 * GROUP,
            jnp.bitwise_or(jnp.left_shift(row % GROUP, 8), jnp.left_shift(row // GROUP, 13)),
            jnp.left_shift(row - 2 * GROUP, 11),
        )
        signs[e] = jnp.where(odd_common_bits(entry, mask), -1.0, 1.0)
        weights[e] = jnp.where(
            odd_common_bits(entry, iota((NLOW, points), 0)), -1.0, 1.0
        ).astype(jnp.bfloat16)

    word_copy.wait()
    lines = wbuf.reshape(high_dev * (per_high + 1), 1, LANES)
    lane8 = iota((8, LANES), 1)

    def spread(both):
        value = jnp.take_along_axis(both, lane8 % 16 * 8 + lane8 // 16, axis=1, mode="promise_in_bounds")
        for reach, keep in ((8, 0x00FF00FF), (4, 0x0F0F0F0F), (2, 0x33333333), (1, 0x55555555)):
            other = jnp.take_along_axis(value, jnp.bitwise_xor(lane8, reach), axis=1, mode="promise_in_bounds")
            value = jnp.where(
                jnp.bitwise_and(lane8, reach) == 0,
                jnp.bitwise_or(
                    jnp.bitwise_and(value, keep), jnp.left_shift(jnp.bitwise_and(other, keep), reach)
                ),
                jnp.bitwise_or(
                    jnp.bitwise_and(value, ~keep), jnp.bitwise_and(jnp.right_shift(other, reach), keep)
                ),
            )
        return value

    @pl.loop(0, high_dev // 8)
    def _(n):
        for c in range(chunks):
            for pair in range(TOP // 2):
                one, two = (
                    lines[
                        pl.ds(n * 8 * (per_high + 1) + (2 * pair + which) * chunks + c, 8, per_high + 1), 0, :
                    ]
                    for which in range(2)
                )
                wpair[c, pair, pl.ds(pl.multiple_of(n * 8, 8), 8), :] = spread(
                    jnp.bitwise_or(one, jnp.left_shift(two, 16))
                )

    def prepare(step, u, part, parts):
        slot = step % SLOTS
        chunk = step * STEP // GROUP
        row = step % (GROUP // STEP) * ROWS + iota((ROWS, LANES), 0)
        bits = [jnp.left_shift(1, row), jnp.left_shift(1, row + 16)]
        for n in range(part * highs // parts, (part + 1) * highs // parts):
            h = u * highs + n
            values = []
            for pair in range(TOP // 2):
                word = jnp.broadcast_to(wpair[chunk, pair, pl.ds(h, 1), :], (ROWS, LANES))
                two = xbuf[slot, h, :, 2 * pair * ROWS * LANES : 2 * (pair + 1) * ROWS * LANES]
                two = two.reshape(2 * ROWS, LANES).astype(jnp.float32)
                for which in range(2):
                    value = two[which * ROWS : (which + 1) * ROWS]
                    values.append(jnp.where(jnp.bitwise_and(word, bits[which]) != 0, value, -value))
            for reach in (2, 4):
                nxt = list(values)
                for at in range(TOP):
                    if not at & reach:
                        nxt[at] = values[at] + values[at + reach]
                        nxt[at + reach] = values[at] - values[at + reach]
                values = nxt
            for top in range(TOP):
                ybuf[step % 2][top, pl.ds(h, ROWS, stride), :] = values[top]

    def transform_high(step, u, n):
        top, i = u * PAIR % TOP + n, u * PAIR // TOP
        columns = [
            ybuf[step % 2][top, pl.ds((2 * i + l_hi) * stride, high_dev), :].astype(jnp.bfloat16)
            for l_hi in range(2)
        ]
        result = jnp.dot(
            table[...], jnp.concatenate(columns, axis=1), preferred_element_type=jnp.float32
        )
        chunk = step * STEP // GROUP
        row = step % (GROUP // STEP) * STEP + i
        tbuf[chunk % 2][top // 2, n % 2 * GROUP + row] = result.astype(jnp.bfloat16)

    def evaluate(chunk, e):
        j, g = e // groups, e % groups
        block = tbuf[chunk % 2][j, :, pl.ds(pl.multiple_of(g * PACK, PACK), PACK), :]
        found = jnp.dot(
            block.reshape(2 * GROUP * PACK, NLOW), weights[e], preferred_element_type=jnp.float32
        )
        total = found[:PACK] * signs[e, 0:1, :]
        for n in range(1, 2 * GROUP):
            total += found[n * PACK : (n + 1) * PACK] * signs[e, n : n + 1, :]
        acc[e] += total * signs[e, 2 * GROUP + chunk : 2 * GROUP + chunk + 1, :]

    def some_pairs(n, part, do):
        if pairs >= PAIR * rounds:
            for m in range(pairs // (PAIR * rounds)):
                do((n * PAIR + part) * (pairs // (PAIR * rounds)) + m)
        elif part % (PAIR * rounds // pairs) == 0:
            do((n * PAIR + part) // (PAIR * rounds // pairs))

    turns = STEP * TOP // PAIR
    per_chunk = GROUP // STEP

    grad_copies(0, lambda copy: copy.wait())

    @pl.loop(0, turns)
    def _(u):
        prepare(0, u, 0, 1)

    for step in range(steps):
        if step + SLOTS < steps:
            grad_copies(step + SLOTS, lambda copy: copy.start())
        if step + 1 < steps:
            grad_copies(step + 1, lambda copy: copy.wait())

        @pl.loop(0, turns)
        def _(u):
            for part in range(PAIR):
                if step >= per_chunk:
                    some_pairs(
                        step % per_chunk * turns + u,
                        part,
                        functools.partial(evaluate, step // per_chunk - 1),
                    )
                else:
                    some_pairs(step * turns + u, part, build)
                transform_high(step, u, part)
                if step + 1 < steps:
                    prepare(step + 1, u, part, PAIR)

    @pl.loop(0, pairs)
    def _(e):
        evaluate(chunks - 1, e)
        own = iota((PACK, points), 1) // 2 % PACK == iota((PACK, points), 0)
        found_rows[e // groups, pl.ds(e % groups, 1), :] = jnp.sum(
            jnp.where(own, acc[e], 0.0), axis=0, keepdims=True
        )

    place = place_ref[0]
    for hi in range(high_parts):
        common = jnp.bitwise_and(place, hi)
        odd = jnp.bitwise_and(common ^ (common >> 1) ^ (common >> 2) ^ (common >> 3), 1)
        sign = jnp.where(odd == 1, -scale, scale)
        part, first = divmod(hi * 2 * PACK, LANES)
        spot = first + lane // TOP * 2 + lane % 2
        line = jnp.zeros((groups, LANES), jnp.float32)
        for j in range(HALVED):
            rows = found_rows[j, :, part * LANES : (part + 1) * LANES]
            taken = jnp.take_along_axis(rows, spot, axis=1, mode="promise_in_bounds")
            line = jnp.where(lane % TOP // 2 == j, taken, line)
        out_ref[hi * groups : (hi + 1) * groups, :] = line * sign


def partial_sketch(gradients, sign_words, sub_index, place, high_dev, scale):
    kept = sub_index.shape[0]
    rest = NMID // TOP
    groups = high_dev // PACK
    points = kept // (HALVED * groups)
    grads = gradients.reshape(high_dev, TOP, rest // STEP, 1, ROWS * LANES)
    words = sign_words.reshape(high_dev, -1, 1, LANES)
    return pl.pallas_call(
        functools.partial(sketch_kernel, high_dev=high_dev, scale=scale),
        out_shape=jax.ShapeDtypeStruct((kept // LANES, LANES), jnp.float32),
        in_specs=[
            pl.BlockSpec(memory_space=pltpu.SMEM),
            pl.BlockSpec(memory_space=pl.ANY),
            pl.BlockSpec(memory_space=pl.ANY),
            pl.BlockSpec(memory_space=pltpu.VMEM),
        ],
        out_specs=pl.BlockSpec(memory_space=pltpu.VMEM),
        scratch_shapes=[
            pltpu.VMEM((SLOTS, high_dev, 1, TOP * ROWS * LANES), jnp.bfloat16),
            pltpu.VMEM((high_dev, words.shape[1] + 1, 1, LANES), jnp.int32),
            pltpu.VMEM((rest // GROUP, TOP // 2, high_dev, LANES), jnp.int32),
            pltpu.VMEM((high_dev, high_dev), jnp.bfloat16),
            pltpu.VMEM((TOP, ROWS * (high_dev + 1), LANES), jnp.float32),
            pltpu.VMEM((TOP, ROWS * (high_dev + 1), LANES), jnp.float32),
            pltpu.VMEM((HALVED, 2 * GROUP, high_dev, NLOW), jnp.bfloat16),
            pltpu.VMEM((HALVED, 2 * GROUP, high_dev, NLOW), jnp.bfloat16),
            pltpu.VMEM((HALVED, groups, points), jnp.int32),
            pltpu.VMEM((HALVED * groups, NLOW, points), jnp.bfloat16),
            pltpu.VMEM((HALVED * groups, 24, points), jnp.float32),
            pltpu.VMEM((HALVED * groups, PACK, points), jnp.float32),
            pltpu.VMEM((HALVED, groups, points), jnp.float32),
            pltpu.SemaphoreType.DMA((SLOTS, TOP)),
            pltpu.SemaphoreType.DMA,
        ],
        compiler_params=pltpu.CompilerParams(vmem_limit_bytes=63 * 1024 * 1024),
        cost_estimate=pl.CostEstimate(
            flops=4 * NLOW * high_dev * NMID * NLOW, bytes_accessed=4 * gradients.size, transcendentals=0
        ),
        name="sketch",
    )(place, grads, words, sub_index.reshape(kept // LANES, LANES))


def swapped(value, axis, size, bits):
    return lax.ppermute(value, axis, [(i, i ^ bits) for i in range(size)])


def score_kernel(*refs, scale):
    *sketches, own_tests, near_tests, out_ref, lines = refs
    for n, sketch in enumerate(sketches):
        whole = sketch[...].astype(jnp.float32)
        for row in range(whole.shape[0]):
            lines[n : n + 1, row * LANES : (row + 1) * LANES] = whole[row : row + 1, :]
    left = lines[...].astype(jnp.bfloat16)
    for n, tests in enumerate([own_tests] + [near_tests.at[s] for s in range(near_tests.shape[0])]):
        found = lax.dot_general(
            left, tests[...], (((1,), (1,)), ((), ())), preferred_element_type=jnp.float32
        )
        found = found[: len(sketches)] * scale
        out_ref[:, n * tests.shape[0] : (n + 1) * tests.shape[0]] = found


def scores_of(sketches, own_tests, near_tests, scale):
    tests, kept = own_tests.shape
    count = len(sketches)
    return pl.pallas_call(
        functools.partial(score_kernel, scale=scale),
        out_shape=jax.ShapeDtypeStruct((count, tests * (1 + near_tests.shape[0])), jnp.float32),
        scratch_shapes=[pltpu.VMEM((16, kept), jnp.float32)],
        compiler_params=pltpu.CompilerParams(vmem_limit_bytes=32 * 1024 * 1024),
        name="scores",
    )(*sketches, own_tests, near_tests)


def on_device(gradients, sign_words, sub_index, test_sketch, *, mesh):
    feat_size, far_size, near_size = (mesh.shape[axis] for axis in ("feat", "far", "near"))
    local_features = gradients.shape[1]
    kept = sub_index.shape[0]
    tests = test_sketch.shape[0]
    high_dev = local_features // (NMID * NLOW)
    feature_scale = float(local_features * feat_size) ** (-0.5)
    score_scale = float(kept) ** (-0.5)
    place = lax.axis_index("feat").astype(jnp.int32).reshape(1)
    near_tests = jnp.stack([swapped(test_sketch, "near", near_size, s) for s in range(1, near_size)])
    shares = partial_sketch(gradients, sign_words, sub_index, place, high_dev, feature_scale)
    sketch = shares
    for s in range(1, feat_size):
        sketch = sketch + swapped(shares, "feat", feat_size, s)
    sketch = sketch.astype(jnp.bfloat16)
    sketches = [sketch] + [swapped(sketch, "far", far_size, s) for s in range(1, far_size)]
    scores = scores_of(sketches, test_sketch, near_tests, score_scale)
    scores = jnp.stack(
        [scores[:1]] + [swapped(scores[s : s + 1], "far", far_size, s) for s in range(1, far_size)]
    )
    scores = scores.reshape(far_size, near_size, tests)
    far, near = lax.axis_index("far"), lax.axis_index("near")
    for b in range(near_size.bit_length() - 1):
        split = scores.reshape(far_size, -1, 2, 1 << b, tests)
        scores = jnp.where(jnp.bitwise_and(near, 1 << b) != 0, split[:, :, ::-1], split)
    for b in range(far_size.bit_length() - 1):
        split = scores.reshape(-1, 2, 1 << b, near_size, tests)
        scores = jnp.where(jnp.bitwise_and(far, 1 << b) != 0, split[:, ::-1], split)
    return scores.reshape(1, -1)


def solution(mesh):
    feat_size, ex_size = mesh.shape["feat"], mesh.shape["ex"]
    far_size = min(4, ex_size)
    mesh = Mesh(mesh.devices.reshape(feat_size, far_size, ex_size // far_size), ("feat", "far", "near"))
    ex = ("far", "near")
    return jax.shard_map(
        functools.partial(on_device, mesh=mesh),
        mesh=mesh,
        in_specs=(P(ex, "feat"), P("feat"), P(), P(ex, None)),
        out_specs=P(ex, None),
        check_vma=False,
    )
```

```python
import functools

import jax
import jax.numpy as jnp
from jax import lax
from jax.experimental import pallas as pl
from jax.experimental.pallas import tpu as pltpu
from jax.sharding import Mesh, PartitionSpec as P

NMID = 256
NLOW = 256
TOP = 8
GROUP = 8
STEP = 4
SLOTS = 2
ROWS = 2 * STEP
HALVED = TOP // 2
LANES = 128
PACK = 16
PAIR = 4


def odd_common_bits(left, right):
    return jnp.bitwise_and(lax.population_count(jnp.bitwise_and(left, right)), 1) == 1


def iota(shape, axis):
    return lax.broadcasted_iota(jnp.int32, shape, axis)


def sketch_kernel(
    place_ref, grads, words, sub_ref, out_ref,
    xbuf, wbuf, wpair, table, ybuf0, ybuf1, tbuf0, tbuf1, entries, weights, signs, acc, found_rows, sems, wsem,
    *, high_dev, scale,
):
    high_parts = out_ref.shape[0] * LANES // TOP // high_dev
    rest = NMID // TOP
    chunks = rest // GROUP
    steps = rest // STEP
    groups = high_dev // PACK
    points = entries.shape[2]
    pairs = HALVED * groups
    rounds = GROUP * TOP // PAIR
    highs = high_dev * PAIR // (STEP * TOP)
    stride = high_dev + 1
    ybuf = (ybuf0, ybuf1)
    tbuf = (tbuf0, tbuf1)

    def grad_copies(step, then):
        slot = step % SLOTS
        for top in range(TOP):
            copy = pltpu.make_async_copy(
                grads.at[:, top, step],
                xbuf.at[slot, :, :, top * ROWS * LANES : (top + 1) * ROWS * LANES],
                sems.at[slot, top],
            )
            then(copy)

    per_high = NMID * NLOW // 16 // LANES
    word_copy = pltpu.make_async_copy(words, wbuf.at[:, :per_high], wsem)
    word_copy.start()
    for step in range(SLOTS):
        grad_copies(step, lambda copy: copy.start())

    table[...] = jnp.where(
        odd_common_bits(iota(table.shape, 0), iota(table.shape, 1)), -1.0, 1.0
    ).astype(jnp.bfloat16)
    acc[...] = jnp.zeros_like(acc)
    lane = iota((groups, LANES), 1)
    for j in range(HALVED):
        spot = (lane // 2 % PACK) * TOP + 2 * j + lane % 2
        for part in range(points // LANES):
            line = jnp.zeros((groups, LANES), jnp.int32)
            for n in range(LANES // (2 * PACK)):
                hi = part * (LANES // (2 * PACK)) + n
                rows = sub_ref[hi * groups : (hi + 1) * groups, :]
                taken = jnp.take_along_axis(rows, spot, axis=1, mode="promise_in_bounds")
                line = jnp.where(lane // (2 * PACK) == n, taken, line)
            entries[j, :, part * LANES : (part + 1) * LANES] = line

    def build(e):
        entry = entries[e // groups, pl.ds(e % groups, 1), :]
        row = iota((24, points), 0)
        mask = jnp.where(
            row < 2 * GROUP,
            jnp.bitwise_or(jnp.left_shift(row % GROUP, 8), jnp.left_shift(row // GROUP, 13)),
            jnp.left_shift(row - 2 * GROUP, 11),
        )
        signs[e] = jnp.where(odd_common_bits(entry, mask), -1.0, 1.0)
        weights[e] = jnp.where(
            odd_common_bits(entry, iota((NLOW, points), 0)), -1.0, 1.0
        ).astype(jnp.bfloat16)

    word_copy.wait()
    lines = wbuf.reshape(high_dev * (per_high + 1), 1, LANES)
    lane8 = iota((8, LANES), 1)

    def spread(both):
        value = jnp.take_along_axis(both, lane8 % 16 * 8 + lane8 // 16, axis=1, mode="promise_in_bounds")
        for reach, keep in ((8, 0x00FF00FF), (4, 0x0F0F0F0F), (2, 0x33333333), (1, 0x55555555)):
            other = jnp.take_along_axis(value, jnp.bitwise_xor(lane8, reach), axis=1, mode="promise_in_bounds")
            value = jnp.where(
                jnp.bitwise_and(lane8, reach) == 0,
                jnp.bitwise_or(
                    jnp.bitwise_and(value, keep), jnp.left_shift(jnp.bitwise_and(other, keep), reach)
                ),
                jnp.bitwise_or(
                    jnp.bitwise_and(value, ~keep), jnp.bitwise_and(jnp.right_shift(other, reach), keep)
                ),
            )
        return value

    @pl.loop(0, high_dev // 8)
    def _(n):
        for c in range(chunks):
            for pair in range(TOP // 2):
                one, two = (
                    lines[
                        pl.ds(n * 8 * (per_high + 1) + (2 * pair + which) * chunks + c, 8, per_high + 1), 0, :
                    ]
                    for which in range(2)
                )
                wpair[c, pair, pl.ds(pl.multiple_of(n * 8, 8), 8), :] = spread(
                    jnp.bitwise_or(one, jnp.left_shift(two, 16))
                )

    def prepare(step, u, part, parts):
        slot = step % SLOTS
        chunk = step * STEP // GROUP
        row = step % (GROUP // STEP) * ROWS + iota((ROWS, LANES), 0)
        bits = [jnp.left_shift(1, row), jnp.left_shift(1, row + 16)]
        for n in range(part * highs // parts, (part + 1) * highs // parts):
            h = u * highs + n
            values = []
            for pair in range(TOP // 2):
                word = jnp.broadcast_to(wpair[chunk, pair, pl.ds(h, 1), :], (ROWS, LANES))
                two = xbuf[slot, h, :, 2 * pair * ROWS * LANES : 2 * (pair + 1) * ROWS * LANES]
                two = two.reshape(2 * ROWS, LANES).astype(jnp.float32)
                for which in range(2):
                    value = two[which * ROWS : (which + 1) * ROWS]
                    values.append(jnp.where(jnp.bitwise_and(word, bits[which]) != 0, value, -value))
            for reach in (2, 4):
                nxt = list(values)
                for at in range(TOP):
                    if not at & reach:
                        nxt[at] = values[at] + values[at + reach]
                        nxt[at + reach] = values[at] - values[at + reach]
                values = nxt
            for top in range(TOP):
                ybuf[step % 2][top, pl.ds(h, ROWS, stride), :] = values[top]

    def transform_high(step, u):
        first, i = u * PAIR % TOP, u * PAIR // TOP
        columns = [
            ybuf[step % 2][first + n, pl.ds((2 * i + l_hi) * stride, high_dev), :].astype(jnp.bfloat16)
            for n in range(PAIR)
            for l_hi in range(2)
        ]
        result = jnp.dot(
            table[...], jnp.concatenate(columns, axis=1), preferred_element_type=jnp.float32
        ).astype(jnp.bfloat16)
        chunk = step * STEP // GROUP
        row = step % (GROUP // STEP) * STEP + i
        for n in range(PAIR):
            top = first + n
            tbuf[chunk % 2][top // 2, n % 2 * GROUP + row] = result[:, n * NLOW : (n + 1) * NLOW]

    def evaluate(chunk, e):
        j, g = e // groups, e % groups
        block = tbuf[chunk % 2][j, :, pl.ds(pl.multiple_of(g * PACK, PACK), PACK), :]
        found = jnp.dot(
            block.reshape(2 * GROUP * PACK, NLOW), weights[e], preferred_element_type=jnp.float32
        )
        total = found[:PACK] * signs[e, 0:1, :]
        for n in range(1, 2 * GROUP):
            total += found[n * PACK : (n + 1) * PACK] * signs[e, n : n + 1, :]
        acc[e] += total * signs[e, 2 * GROUP + chunk : 2 * GROUP + chunk + 1, :]

    def some_pairs(n, part, do):
        if pairs >= PAIR * rounds:
            for m in range(pairs // (PAIR * rounds)):
                do((n * PAIR + part) * (pairs // (PAIR * rounds)) + m)
        elif part % (PAIR * rounds // pairs) == 0:
            do((n * PAIR + part) // (PAIR * rounds // pairs))

    turns = STEP * TOP // PAIR
    per_chunk = GROUP // STEP

    grad_copies(0, lambda copy: copy.wait())

    @pl.loop(0, turns)
    def _(u):
        prepare(0, u, 0, 1)

    for step in range(steps):
        if step + SLOTS < steps:
            grad_copies(step + SLOTS, lambda copy: copy.start())
        if step + 1 < steps:
            grad_copies(step + 1, lambda copy: copy.wait())

        @pl.loop(0, turns)
        def _(u):
            for part in range(PAIR):
                if step >= per_chunk:
                    some_pairs(
                        step % per_chunk * turns + u,
                        part,
                        functools.partial(evaluate, step // per_chunk - 1),
                    )
                else:
                    some_pairs(step * turns + u, part, build)
            transform_high(step, u)
            if step + 1 < steps:
                prepare(step + 1, u, 0, 1)

    @pl.loop(0, pairs)
    def _(e):
        evaluate(chunks - 1, e)
        own = iota((PACK, points), 1) // 2 % PACK == iota((PACK, points), 0)
        found_rows[e // groups, pl.ds(e % groups, 1), :] = jnp.sum(
            jnp.where(own, acc[e], 0.0), axis=0, keepdims=True
        )

    place = place_ref[0]
    for hi in range(high_parts):
        common = jnp.bitwise_and(place, hi)
        odd = jnp.bitwise_and(common ^ (common >> 1) ^ (common >> 2) ^ (common >> 3), 1)
        sign = jnp.where(odd == 1, -scale, scale)
        part, first = divmod(hi * 2 * PACK, LANES)
        spot = first + lane // TOP * 2 + lane % 2
        line = jnp.zeros((groups, LANES), jnp.float32)
        for j in range(HALVED):
            rows = found_rows[j, :, part * LANES : (part + 1) * LANES]
            taken = jnp.take_along_axis(rows, spot, axis=1, mode="promise_in_bounds")
            line = jnp.where(lane % TOP // 2 == j, taken, line)
        out_ref[hi * groups : (hi + 1) * groups, :] = line * sign


def partial_sketch(gradients, sign_words, sub_index, place, high_dev, scale):
    kept = sub_index.shape[0]
    rest = NMID // TOP
    groups = high_dev // PACK
    points = kept // (HALVED * groups)
    grads = gradients.reshape(high_dev, TOP, rest // STEP, 1, ROWS * LANES)
    words = sign_words.reshape(high_dev, -1, 1, LANES)
    return pl.pallas_call(
        functools.partial(sketch_kernel, high_dev=high_dev, scale=scale),
        out_shape=jax.ShapeDtypeStruct((kept // LANES, LANES), jnp.float32),
        in_specs=[
            pl.BlockSpec(memory_space=pltpu.SMEM),
            pl.BlockSpec(memory_space=pl.ANY),
            pl.BlockSpec(memory_space=pl.ANY),
            pl.BlockSpec(memory_space=pltpu.VMEM),
        ],
        out_specs=pl.BlockSpec(memory_space=pltpu.VMEM),
        scratch_shapes=[
            pltpu.VMEM((SLOTS, high_dev, 1, TOP * ROWS * LANES), jnp.bfloat16),
            pltpu.VMEM((high_dev, words.shape[1] + 1, 1, LANES), jnp.int32),
            pltpu.VMEM((rest // GROUP, TOP // 2, high_dev, LANES), jnp.int32),
            pltpu.VMEM((high_dev, high_dev), jnp.bfloat16),
            pltpu.VMEM((TOP, ROWS * (high_dev + 1), LANES), jnp.float32),
            pltpu.VMEM((TOP, ROWS * (high_dev + 1), LANES), jnp.float32),
            pltpu.VMEM((HALVED, 2 * GROUP, high_dev, NLOW), jnp.bfloat16),
            pltpu.VMEM((HALVED, 2 * GROUP, high_dev, NLOW), jnp.bfloat16),
            pltpu.VMEM((HALVED, groups, points), jnp.int32),
            pltpu.VMEM((HALVED * groups, NLOW, points), jnp.bfloat16),
            pltpu.VMEM((HALVED * groups, 24, points), jnp.float32),
            pltpu.VMEM((HALVED * groups, PACK, points), jnp.float32),
            pltpu.VMEM((HALVED, groups, points), jnp.float32),
            pltpu.SemaphoreType.DMA((SLOTS, TOP)),
            pltpu.SemaphoreType.DMA,
        ],
        compiler_params=pltpu.CompilerParams(vmem_limit_bytes=63 * 1024 * 1024),
        cost_estimate=pl.CostEstimate(
            flops=4 * NLOW * high_dev * NMID * NLOW, bytes_accessed=4 * gradients.size, transcendentals=0
        ),
        name="sketch",
    )(place, grads, words, sub_index.reshape(kept // LANES, LANES))


def swapped(value, axis, size, bits):
    return lax.ppermute(value, axis, [(i, i ^ bits) for i in range(size)])


def score_kernel(*refs, scale):
    *sketches, own_tests, near_tests, out_ref, lines = refs
    for n, sketch in enumerate(sketches):
        whole = sketch[...].astype(jnp.float32)
        for row in range(whole.shape[0]):
            lines[n : n + 1, row * LANES : (row + 1) * LANES] = whole[row : row + 1, :]
    left = lines[...].astype(jnp.bfloat16)
    for n, tests in enumerate([own_tests] + [near_tests.at[s] for s in range(near_tests.shape[0])]):
        found = lax.dot_general(
            left, tests[...], (((1,), (1,)), ((), ())), preferred_element_type=jnp.float32
        )
        found = found[: len(sketches)] * scale
        out_ref[:, n * tests.shape[0] : (n + 1) * tests.shape[0]] = found


def scores_of(sketches, own_tests, near_tests, scale):
    tests, kept = own_tests.shape
    count = len(sketches)
    return pl.pallas_call(
        functools.partial(score_kernel, scale=scale),
        out_shape=jax.ShapeDtypeStruct((count, tests * (1 + near_tests.shape[0])), jnp.float32),
        scratch_shapes=[pltpu.VMEM((16, kept), jnp.float32)],
        compiler_params=pltpu.CompilerParams(vmem_limit_bytes=32 * 1024 * 1024),
        name="scores",
    )(*sketches, own_tests, near_tests)


def on_device(gradients, sign_words, sub_index, test_sketch, *, mesh):
    feat_size, far_size, near_size = (mesh.shape[axis] for axis in ("feat", "far", "near"))
    local_features = gradients.shape[1]
    kept = sub_index.shape[0]
    tests = test_sketch.shape[0]
    high_dev = local_features // (NMID * NLOW)
    feature_scale = float(local_features * feat_size) ** (-0.5)
    score_scale = float(kept) ** (-0.5)
    place = lax.axis_index("feat").astype(jnp.int32).reshape(1)
    near_tests = jnp.stack([swapped(test_sketch, "near", near_size, s) for s in range(1, near_size)])
    shares = partial_sketch(gradients, sign_words, sub_index, place, high_dev, feature_scale)
    sketch = shares
    for s in range(1, feat_size):
        sketch = sketch + swapped(shares, "feat", feat_size, s)
    sketch = sketch.astype(jnp.bfloat16)
    sketches = [sketch] + [swapped(sketch, "far", far_size, s) for s in range(1, far_size)]
    scores = scores_of(sketches, test_sketch, near_tests, score_scale)
    scores = jnp.stack(
        [scores[:1]] + [swapped(scores[s : s + 1], "far", far_size, s) for s in range(1, far_size)]
    )
    scores = scores.reshape(far_size, near_size, tests)
    far, near = lax.axis_index("far"), lax.axis_index("near")
    for b in range(near_size.bit_length() - 1):
        split = scores.reshape(far_size, -1, 2, 1 << b, tests)
        scores = jnp.where(jnp.bitwise_and(near, 1 << b) != 0, split[:, :, ::-1], split)
    for b in range(far_size.bit_length() - 1):
        split = scores.reshape(-1, 2, 1 << b, near_size, tests)
        scores = jnp.where(jnp.bitwise_and(far, 1 << b) != 0, split[:, ::-1], split)
    return scores.reshape(1, -1)


def solution(mesh):
    feat_size, ex_size = mesh.shape["feat"], mesh.shape["ex"]
    far_size = min(4, ex_size)
    mesh = Mesh(mesh.devices.reshape(feat_size, far_size, ex_size // far_size), ("feat", "far", "near"))
    ex = ("far", "near")
    return jax.shard_map(
        functools.partial(on_device, mesh=mesh),
        mesh=mesh,
        in_specs=(P(ex, "feat"), P("feat"), P(), P(ex, None)),
        out_specs=P(ex, None),
        check_vma=False,
    )
```

```python
import functools

import jax
import jax.numpy as jnp
from jax import lax
from jax.experimental import pallas as pl
from jax.experimental.pallas import tpu as pltpu
from jax.sharding import Mesh, PartitionSpec as P

NMID = 256
NLOW = 256
TOP = 8
GROUP = 8
STEP = 4
SLOTS = 2
ROWS = 2 * STEP
HALVED = TOP // 2
LANES = 128
PACK = 16
PAIR = 4


def odd_common_bits(left, right):
    return jnp.bitwise_and(lax.population_count(jnp.bitwise_and(left, right)), 1) == 1


def iota(shape, axis):
    return lax.broadcasted_iota(jnp.int32, shape, axis)


def sketch_kernel(
    place_ref, grads, words, sub_ref, out_ref,
    xbuf, wbuf, wpair, table, ybuf0, ybuf1, tbuf0, tbuf1, entries, weights, signs, acc, found_rows, sems, wsem,
    *, high_dev, scale,
):
    high_parts = out_ref.shape[0] * LANES // TOP // high_dev
    rest = NMID // TOP
    chunks = rest // GROUP
    steps = rest // STEP
    groups = high_dev // PACK
    points = entries.shape[2]
    pairs = HALVED * groups
    rounds = GROUP * TOP // PAIR
    highs = high_dev * PAIR // (STEP * TOP)
    stride = high_dev + 1
    ybuf = (ybuf0, ybuf1)
    tbuf = (tbuf0, tbuf1)

    def grad_copies(step, then):
        slot = step % SLOTS
        for top in range(TOP):
            copy = pltpu.make_async_copy(
                grads.at[:, top, step],
                xbuf.at[slot, :, :, top * ROWS * LANES : (top + 1) * ROWS * LANES],
                sems.at[slot, top],
            )
            then(copy)

    per_high = NMID * NLOW // 16 // LANES
    word_copy = pltpu.make_async_copy(words, wbuf.at[:, :per_high], wsem)
    word_copy.start()
    for step in range(SLOTS):
        grad_copies(step, lambda copy: copy.start())

    table[...] = jnp.where(
        odd_common_bits(iota(table.shape, 0), iota(table.shape, 1)), -1.0, 1.0
    ).astype(jnp.bfloat16)
    acc[...] = jnp.zeros_like(acc)
    lane = iota((groups, LANES), 1)
    for j in range(HALVED):
        spot = (lane // 2 % PACK) * TOP + 2 * j + lane % 2
        for part in range(points // LANES):
            line = jnp.zeros((groups, LANES), jnp.int32)
            for n in range(LANES // (2 * PACK)):
                hi = part * (LANES // (2 * PACK)) + n
                rows = sub_ref[hi * groups : (hi + 1) * groups, :]
                taken = jnp.take_along_axis(rows, spot, axis=1, mode="promise_in_bounds")
                line = jnp.where(lane // (2 * PACK) == n, taken, line)
            entries[j, :, part * LANES : (part + 1) * LANES] = line

    def build(e):
        entry = entries[e // groups, pl.ds(e % groups, 1), :]
        row = iota((24, points), 0)
        mask = jnp.where(
            row < 2 * GROUP,
            jnp.bitwise_or(jnp.left_shift(row % GROUP, 8), jnp.left_shift(row // GROUP, 13)),
            jnp.left_shift(row - 2 * GROUP, 11),
        )
        signs[e] = jnp.where(odd_common_bits(entry, mask), -1.0, 1.0)
        weights[e] = jnp.where(
            odd_common_bits(entry, iota((NLOW, points), 0)), -1.0, 1.0
        ).astype(jnp.bfloat16)

    word_copy.wait()
    lines = wbuf.reshape(high_dev * (per_high + 1), 1, LANES)
    lane8 = iota((8, LANES), 1)

    def spread(both):
        value = jnp.take_along_axis(both, lane8 % 16 * 8 + lane8 // 16, axis=1, mode="promise_in_bounds")
        for reach, keep in ((8, 0x00FF00FF), (4, 0x0F0F0F0F), (2, 0x33333333), (1, 0x55555555)):
            other = jnp.take_along_axis(value, jnp.bitwise_xor(lane8, reach), axis=1, mode="promise_in_bounds")
            value = jnp.where(
                jnp.bitwise_and(lane8, reach) == 0,
                jnp.bitwise_or(
                    jnp.bitwise_and(value, keep), jnp.left_shift(jnp.bitwise_and(other, keep), reach)
                ),
                jnp.bitwise_or(
                    jnp.bitwise_and(value, ~keep), jnp.bitwise_and(jnp.right_shift(other, reach), keep)
                ),
            )
        return value

    def spread_words(c, n):
        for pair in range(TOP // 2):
            one, two = (
                lines[
                    pl.ds(n * 8 * (per_high + 1) + (2 * pair + which) * chunks + c, 8, per_high + 1), 0, :
                ]
                for which in range(2)
            )
            wpair[c, pair, pl.ds(pl.multiple_of(n * 8, 8), 8), :] = spread(
                jnp.bitwise_or(one, jnp.left_shift(two, 16))
            )

    @pl.loop(0, high_dev // 32)
    def _(n):
        for m in range(4):
            spread_words(0, 4 * n + m)

    def prepare(step, u, part, parts):
        slot = step % SLOTS
        chunk = step * STEP // GROUP
        row = step % (GROUP // STEP) * ROWS + iota((ROWS, LANES), 0)
        bits = [jnp.left_shift(1, row), jnp.left_shift(1, row + 16)]
        for n in range(part * highs // parts, (part + 1) * highs // parts):
            h = u * highs + n
            values = []
            for pair in range(TOP // 2):
                word = jnp.broadcast_to(wpair[chunk, pair, pl.ds(h, 1), :], (ROWS, LANES))
                two = xbuf[slot, h, :, 2 * pair * ROWS * LANES : 2 * (pair + 1) * ROWS * LANES]
                two = two.reshape(2 * ROWS, LANES).astype(jnp.float32)
                for which in range(2):
                    value = two[which * ROWS : (which + 1) * ROWS]
                    values.append(jnp.where(jnp.bitwise_and(word, bits[which]) != 0, value, -value))
            for reach in (2, 4):
                nxt = list(values)
                for at in range(TOP):
                    if not at & reach:
                        nxt[at] = values[at] + values[at + reach]
                        nxt[at + reach] = values[at] - values[at + reach]
                values = nxt
            for top in range(TOP):
                ybuf[step % 2][top, pl.ds(h, ROWS, stride), :] = values[top]

    def transform_high(step, u):
        first, i = u * PAIR % TOP, u * PAIR // TOP
        columns = [
            ybuf[step % 2][first + n, pl.ds((2 * i + l_hi) * stride, high_dev), :].astype(jnp.bfloat16)
            for n in range(PAIR)
            for l_hi in range(2)
        ]
        result = jnp.dot(
            table[...], jnp.concatenate(columns, axis=1), preferred_element_type=jnp.float32
        ).astype(jnp.bfloat16)
        chunk = step * STEP // GROUP
        row = step % (GROUP // STEP) * STEP + i
        for n in range(PAIR):
            top = first + n
            tbuf[chunk % 2][top // 2, n % 2 * GROUP + row] = result[:, n * NLOW : (n + 1) * NLOW]

    def evaluate(chunk, e):
        j, g = e // groups, e % groups
        block = tbuf[chunk % 2][j, :, pl.ds(pl.multiple_of(g * PACK, PACK), PACK), :]
        found = jnp.dot(
            block.reshape(2 * GROUP * PACK, NLOW), weights[e], preferred_element_type=jnp.float32
        )
        total = found[:PACK] * signs[e, 0:1, :]
        for n in range(1, 2 * GROUP):
            total += found[n * PACK : (n + 1) * PACK] * signs[e, n : n + 1, :]
        acc[e] += total * signs[e, 2 * GROUP + chunk : 2 * GROUP + chunk + 1, :]

    def some_pairs(n, part, do):
        if pairs >= PAIR * rounds:
            for m in range(pairs // (PAIR * rounds)):
                do((n * PAIR + part) * (pairs // (PAIR * rounds)) + m)
        elif part % (PAIR * rounds // pairs) == 0:
            do((n * PAIR + part) // (PAIR * rounds // pairs))

    turns = STEP * TOP // PAIR
    per_chunk = GROUP // STEP

    grad_copies(0, lambda copy: copy.wait())

    @pl.loop(0, turns)
    def _(u):
        prepare(0, u, 0, 1)

    for step in range(steps):
        if step + SLOTS < steps:
            grad_copies(step + SLOTS, lambda copy: copy.start())
        if step + 1 < steps:
            grad_copies(step + 1, lambda copy: copy.wait())

        @pl.loop(0, turns)
        def _(u):
            later, part, parts = {0: (1, 0, 1), 1: (2, 0, 2), 2: (2, 1, 2), 3: (3, 0, 2), 4: (3, 1, 2)}.get(
                step, (chunks, 0, 1)
            )
            if later < chunks:
                count = high_dev // 8 // parts // turns
                for m in range(count):
                    spread_words(later, (part * turns + u) * count + m)
            for part in range(PAIR):
                if step >= per_chunk:
                    some_pairs(
                        step % per_chunk * turns + u,
                        part,
                        functools.partial(evaluate, step // per_chunk - 1),
                    )
                else:
                    some_pairs(step * turns + u, part, build)
            transform_high(step, u)
            if step + 1 < steps:
                prepare(step + 1, u, 0, 1)

    @pl.loop(0, pairs)
    def _(e):
        evaluate(chunks - 1, e)
        own = iota((PACK, points), 1) // 2 % PACK == iota((PACK, points), 0)
        found_rows[e // groups, pl.ds(e % groups, 1), :] = jnp.sum(
            jnp.where(own, acc[e], 0.0), axis=0, keepdims=True
        )

    place = place_ref[0]
    for hi in range(high_parts):
        common = jnp.bitwise_and(place, hi)
        odd = jnp.bitwise_and(common ^ (common >> 1) ^ (common >> 2) ^ (common >> 3), 1)
        sign = jnp.where(odd == 1, -scale, scale)
        part, first = divmod(hi * 2 * PACK, LANES)
        spot = first + lane // TOP * 2 + lane % 2
        line = jnp.zeros((groups, LANES), jnp.float32)
        for j in range(HALVED):
            rows = found_rows[j, :, part * LANES : (part + 1) * LANES]
            taken = jnp.take_along_axis(rows, spot, axis=1, mode="promise_in_bounds")
            line = jnp.where(lane % TOP // 2 == j, taken, line)
        out_ref[hi * groups : (hi + 1) * groups, :] = line * sign


def partial_sketch(gradients, sign_words, sub_index, place, high_dev, scale):
    kept = sub_index.shape[0]
    rest = NMID // TOP
    groups = high_dev // PACK
    points = kept // (HALVED * groups)
    grads = gradients.reshape(high_dev, TOP, rest // STEP, 1, ROWS * LANES)
    words = sign_words.reshape(high_dev, -1, 1, LANES)
    return pl.pallas_call(
        functools.partial(sketch_kernel, high_dev=high_dev, scale=scale),
        out_shape=jax.ShapeDtypeStruct((kept // LANES, LANES), jnp.float32),
        in_specs=[
            pl.BlockSpec(memory_space=pltpu.SMEM),
            pl.BlockSpec(memory_space=pl.ANY),
            pl.BlockSpec(memory_space=pl.ANY),
            pl.BlockSpec(memory_space=pltpu.VMEM),
        ],
        out_specs=pl.BlockSpec(memory_space=pltpu.VMEM),
        scratch_shapes=[
            pltpu.VMEM((SLOTS, high_dev, 1, TOP * ROWS * LANES), jnp.bfloat16),
            pltpu.VMEM((high_dev, words.shape[1] + 1, 1, LANES), jnp.int32),
            pltpu.VMEM((rest // GROUP, TOP // 2, high_dev, LANES), jnp.int32),
            pltpu.VMEM((high_dev, high_dev), jnp.bfloat16),
            pltpu.VMEM((TOP, ROWS * (high_dev + 1), LANES), jnp.float32),
            pltpu.VMEM((TOP, ROWS * (high_dev + 1), LANES), jnp.float32),
            pltpu.VMEM((HALVED, 2 * GROUP, high_dev, NLOW), jnp.bfloat16),
            pltpu.VMEM((HALVED, 2 * GROUP, high_dev, NLOW), jnp.bfloat16),
            pltpu.VMEM((HALVED, groups, points), jnp.int32),
            pltpu.VMEM((HALVED * groups, NLOW, points), jnp.bfloat16),
            pltpu.VMEM((HALVED * groups, 24, points), jnp.float32),
            pltpu.VMEM((HALVED * groups, PACK, points), jnp.float32),
            pltpu.VMEM((HALVED, groups, points), jnp.float32),
            pltpu.SemaphoreType.DMA((SLOTS, TOP)),
            pltpu.SemaphoreType.DMA,
        ],
        compiler_params=pltpu.CompilerParams(vmem_limit_bytes=63 * 1024 * 1024),
        cost_estimate=pl.CostEstimate(
            flops=4 * NLOW * high_dev * NMID * NLOW, bytes_accessed=4 * gradients.size, transcendentals=0
        ),
        name="sketch",
    )(place, grads, words, sub_index.reshape(kept // LANES, LANES))


def swapped(value, axis, size, bits):
    return lax.ppermute(value, axis, [(i, i ^ bits) for i in range(size)])


def score_kernel(*refs, scale):
    *sketches, own_tests, near_tests, out_ref, lines = refs
    for n, sketch in enumerate(sketches):
        whole = sketch[...].astype(jnp.float32)
        for row in range(whole.shape[0]):
            lines[n : n + 1, row * LANES : (row + 1) * LANES] = whole[row : row + 1, :]
    left = lines[...].astype(jnp.bfloat16)
    for n, tests in enumerate([own_tests] + [near_tests.at[s] for s in range(near_tests.shape[0])]):
        found = lax.dot_general(
            left, tests[...], (((1,), (1,)), ((), ())), preferred_element_type=jnp.float32
        )
        found = found[: len(sketches)] * scale
        out_ref[:, n * tests.shape[0] : (n + 1) * tests.shape[0]] = found


def scores_of(sketches, own_tests, near_tests, scale):
    tests, kept = own_tests.shape
    count = len(sketches)
    return pl.pallas_call(
        functools.partial(score_kernel, scale=scale),
        out_shape=jax.ShapeDtypeStruct((count, tests * (1 + near_tests.shape[0])), jnp.float32),
        scratch_shapes=[pltpu.VMEM((16, kept), jnp.float32)],
        compiler_params=pltpu.CompilerParams(vmem_limit_bytes=32 * 1024 * 1024),
        name="scores",
    )(*sketches, own_tests, near_tests)


def on_device(gradients, sign_words, sub_index, test_sketch, *, mesh):
    feat_size, far_size, near_size = (mesh.shape[axis] for axis in ("feat", "far", "near"))
    local_features = gradients.shape[1]
    kept = sub_index.shape[0]
    tests = test_sketch.shape[0]
    high_dev = local_features // (NMID * NLOW)
    feature_scale = float(local_features * feat_size) ** (-0.5)
    score_scale = float(kept) ** (-0.5)
    place = lax.axis_index("feat").astype(jnp.int32).reshape(1)
    near_tests = jnp.stack([swapped(test_sketch, "near", near_size, s) for s in range(1, near_size)])
    shares = partial_sketch(gradients, sign_words, sub_index, place, high_dev, feature_scale)
    sketch = shares
    for s in range(1, feat_size):
        sketch = sketch + swapped(shares, "feat", feat_size, s)
    sketch = sketch.astype(jnp.bfloat16)
    sketches = [sketch] + [swapped(sketch, "far", far_size, s) for s in range(1, far_size)]
    scores = scores_of(sketches, test_sketch, near_tests, score_scale)
    scores = jnp.stack(
        [scores[:1]] + [swapped(scores[s : s + 1], "far", far_size, s) for s in range(1, far_size)]
    )
    scores = scores.reshape(far_size, near_size, tests)
    far, near = lax.axis_index("far"), lax.axis_index("near")
    for b in range(near_size.bit_length() - 1):
        split = scores.reshape(far_size, -1, 2, 1 << b, tests)
        scores = jnp.where(jnp.bitwise_and(near, 1 << b) != 0, split[:, :, ::-1], split)
    for b in range(far_size.bit_length() - 1):
        split = scores.reshape(-1, 2, 1 << b, near_size, tests)
        scores = jnp.where(jnp.bitwise_and(far, 1 << b) != 0, split[:, ::-1], split)
    return scores.reshape(1, -1)


def solution(mesh):
    feat_size, ex_size = mesh.shape["feat"], mesh.shape["ex"]
    far_size = min(4, ex_size)
    mesh = Mesh(mesh.devices.reshape(feat_size, far_size, ex_size // far_size), ("feat", "far", "near"))
    ex = ("far", "near")
    return jax.shard_map(
        functools.partial(on_device, mesh=mesh),
        mesh=mesh,
        in_specs=(P(ex, "feat"), P("feat"), P(), P(ex, None)),
        out_specs=P(ex, None),
        check_vma=False,
    )
```

```python
import functools

import jax
import jax.numpy as jnp
from jax import lax
from jax.experimental import pallas as pl
from jax.experimental.pallas import tpu as pltpu
from jax.sharding import Mesh, PartitionSpec as P

NMID = 256
NLOW = 256
TOP = 8
GROUP = 8
STEP = 4
SLOTS = 2
ROWS = 2 * STEP
HALVED = TOP // 2
LANES = 128
PACK = 16
PAIR = 4


def odd_common_bits(left, right):
    return jnp.bitwise_and(lax.population_count(jnp.bitwise_and(left, right)), 1) == 1


def iota(shape, axis):
    return lax.broadcasted_iota(jnp.int32, shape, axis)


def sketch_kernel(
    place_ref, grads, words, sub_ref, out_ref,
    xbuf, wbuf, wpair, table, ybuf0, ybuf1, tbuf0, tbuf1, entries, weights, signs, acc, found_rows, sems, wsem,
    *, high_dev, scale,
):
    high_parts = out_ref.shape[0] * LANES // TOP // high_dev
    rest = NMID // TOP
    chunks = rest // GROUP
    steps = rest // STEP
    groups = high_dev // PACK
    points = entries.shape[2]
    pairs = HALVED * groups
    rounds = GROUP * TOP // PAIR
    highs = high_dev * PAIR // (STEP * TOP)
    stride = high_dev + 1
    ybuf = (ybuf0, ybuf1)
    tbuf = (tbuf0, tbuf1)

    def grad_copies(step, then):
        slot = step % SLOTS
        for top in range(TOP):
            copy = pltpu.make_async_copy(
                grads.at[:, top, step],
                xbuf.at[slot, :, :, top * ROWS * LANES : (top + 1) * ROWS * LANES],
                sems.at[slot, top],
            )
            then(copy)

    per_high = NMID * NLOW // 16 // LANES
    word_copy = pltpu.make_async_copy(words, wbuf, wsem)
    word_copy.start()
    for step in range(SLOTS):
        grad_copies(step, lambda copy: copy.start())

    table[...] = jnp.where(
        odd_common_bits(iota(table.shape, 0), iota(table.shape, 1)), -1.0, 1.0
    ).astype(jnp.bfloat16)
    acc[...] = jnp.zeros_like(acc)
    lane = iota((groups, LANES), 1)
    for j in range(HALVED):
        spot = (lane // 2 % PACK) * TOP + 2 * j + lane % 2
        for part in range(points // LANES):
            line = jnp.zeros((groups, LANES), jnp.int32)
            for n in range(LANES // (2 * PACK)):
                hi = part * (LANES // (2 * PACK)) + n
                rows = sub_ref[hi * groups : (hi + 1) * groups, :]
                taken = jnp.take_along_axis(rows, spot, axis=1, mode="promise_in_bounds")
                line = jnp.where(lane // (2 * PACK) == n, taken, line)
            entries[j, :, part * LANES : (part + 1) * LANES] = line

    def build(e):
        entry = entries[e // groups, pl.ds(e % groups, 1), :]
        row = iota((24, points), 0)
        mask = jnp.where(
            row < 2 * GROUP,
            jnp.bitwise_or(jnp.left_shift(row % GROUP, 8), jnp.left_shift(row // GROUP, 13)),
            jnp.left_shift(row - 2 * GROUP, 11),
        )
        signs[e] = jnp.where(odd_common_bits(entry, mask), -1.0, 1.0)
        weights[e] = jnp.where(
            odd_common_bits(entry, iota((NLOW, points), 0)), -1.0, 1.0
        ).astype(jnp.bfloat16)

    word_copy.wait()

    def pair_words(c, n):
        for pair in range(TOP // 2):
            one, two = (
                wbuf[pl.ds(n * 8 * per_high + (2 * pair + which) * chunks + c, 8, per_high), :]
                for which in range(2)
            )
            wpair[c, pair, pl.ds(pl.multiple_of(n * 8, 8), 8), :] = jnp.bitwise_or(
                one, jnp.left_shift(two, 16)
            )

    @pl.loop(0, high_dev // 32)
    def _(n):
        for m in range(4):
            pair_words(0, 4 * n + m)

    def prepare(step, u, part, parts):
        slot = step % SLOTS
        chunk = step * STEP // GROUP
        lane8 = iota((ROWS, LANES), 1)
        bits = [jnp.left_shift(1, lane8 % 16), jnp.left_shift(1, lane8 % 16 + 16)]
        spot = step % (GROUP // STEP) * (16 * STEP) + iota((ROWS, LANES), 0) * 8 + lane8 // 16
        for n in range(part * highs // parts, (part + 1) * highs // parts):
            h = u * highs + n
            values = []
            for pair in range(TOP // 2):
                word = jnp.broadcast_to(wpair[chunk, pair, pl.ds(h, 1), :], (ROWS, LANES))
                word = jnp.take_along_axis(word, spot, axis=1, mode="promise_in_bounds")
                two = xbuf[slot, h, :, 2 * pair * ROWS * LANES : 2 * (pair + 1) * ROWS * LANES]
                two = two.reshape(2 * ROWS, LANES).astype(jnp.float32)
                for which in range(2):
                    value = two[which * ROWS : (which + 1) * ROWS]
                    values.append(jnp.where(jnp.bitwise_and(word, bits[which]) != 0, value, -value))
            for reach in (2, 4):
                nxt = list(values)
                for at in range(TOP):
                    if not at & reach:
                        nxt[at] = values[at] + values[at + reach]
                        nxt[at + reach] = values[at] - values[at + reach]
                values = nxt
            for top in range(TOP):
                ybuf[step % 2][top, pl.ds(h, ROWS, stride), :] = values[top]

    def transform_high(step, u):
        first, i = u * PAIR % TOP, u * PAIR // TOP
        columns = [
            ybuf[step % 2][first + n, pl.ds((2 * i + l_hi) * stride, high_dev), :].astype(jnp.bfloat16)
            for n in range(PAIR)
            for l_hi in range(2)
        ]
        result = jnp.dot(
            table[...], jnp.concatenate(columns, axis=1), preferred_element_type=jnp.float32
        ).astype(jnp.bfloat16)
        chunk = step * STEP // GROUP
        row = step % (GROUP // STEP) * STEP + i
        for n in range(PAIR):
            top = first + n
            tbuf[chunk % 2][top // 2, n % 2 * GROUP + row] = result[:, n * NLOW : (n + 1) * NLOW]

    def evaluate(chunk, e):
        j, g = e // groups, e % groups
        block = tbuf[chunk % 2][j, :, pl.ds(pl.multiple_of(g * PACK, PACK), PACK), :]
        found = jnp.dot(
            block.reshape(2 * GROUP * PACK, NLOW), weights[e], preferred_element_type=jnp.float32
        )
        total = found[:PACK] * signs[e, 0:1, :]
        for n in range(1, 2 * GROUP):
            total += found[n * PACK : (n + 1) * PACK] * signs[e, n : n + 1, :]
        acc[e] += total * signs[e, 2 * GROUP + chunk : 2 * GROUP + chunk + 1, :]

    def some_pairs(n, part, do):
        if pairs >= PAIR * rounds:
            for m in range(pairs // (PAIR * rounds)):
                do((n * PAIR + part) * (pairs // (PAIR * rounds)) + m)
        elif part % (PAIR * rounds // pairs) == 0:
            do((n * PAIR + part) // (PAIR * rounds // pairs))

    turns = STEP * TOP // PAIR
    per_chunk = GROUP // STEP

    grad_copies(0, lambda copy: copy.wait())

    @pl.loop(0, turns)
    def _(u):
        prepare(0, u, 0, 1)

    for step in range(steps):
        if step + SLOTS < steps:
            grad_copies(step + SLOTS, lambda copy: copy.start())
        if step + 1 < steps:
            grad_copies(step + 1, lambda copy: copy.wait())

        @pl.loop(0, turns)
        def _(u):
            later, part, parts = {0: (1, 0, 1), 1: (2, 0, 2), 2: (2, 1, 2), 3: (3, 0, 2), 4: (3, 1, 2)}.get(
                step, (chunks, 0, 1)
            )
            if later < chunks:
                count = high_dev // 8 // parts // turns
                for m in range(count):
                    pair_words(later, (part * turns + u) * count + m)
            for part in range(PAIR):
                if step >= per_chunk:
                    some_pairs(
                        step % per_chunk * turns + u,
                        part,
                        functools.partial(evaluate, step // per_chunk - 1),
                    )
                else:
                    some_pairs(step * turns + u, part, build)
            transform_high(step, u)
            if step + 1 < steps:
                prepare(step + 1, u, 0, 1)

    @pl.loop(0, pairs)
    def _(e):
        evaluate(chunks - 1, e)
        own = iota((PACK, points), 1) // 2 % PACK == iota((PACK, points), 0)
        found_rows[e // groups, pl.ds(e % groups, 1), :] = jnp.sum(
            jnp.where(own, acc[e], 0.0), axis=0, keepdims=True
        )

    place = place_ref[0]
    for hi in range(high_parts):
        common = jnp.bitwise_and(place, hi)
        odd = jnp.bitwise_and(common ^ (common >> 1) ^ (common >> 2) ^ (common >> 3), 1)
        sign = jnp.where(odd == 1, -scale, scale)
        part, first = divmod(hi * 2 * PACK, LANES)
        spot = first + lane // TOP * 2 + lane % 2
        line = jnp.zeros((groups, LANES), jnp.float32)
        for j in range(HALVED):
            rows = found_rows[j, :, part * LANES : (part + 1) * LANES]
            taken = jnp.take_along_axis(rows, spot, axis=1, mode="promise_in_bounds")
            line = jnp.where(lane % TOP // 2 == j, taken, line)
        out_ref[hi * groups : (hi + 1) * groups, :] = line * sign


def partial_sketch(gradients, sign_words, sub_index, place, high_dev, scale):
    kept = sub_index.shape[0]
    rest = NMID // TOP
    groups = high_dev // PACK
    points = kept // (HALVED * groups)
    grads = gradients.reshape(high_dev, TOP, rest // STEP, 1, ROWS * LANES)
    words = sign_words.reshape(-1, LANES)
    return pl.pallas_call(
        functools.partial(sketch_kernel, high_dev=high_dev, scale=scale),
        out_shape=jax.ShapeDtypeStruct((kept // LANES, LANES), jnp.float32),
        in_specs=[
            pl.BlockSpec(memory_space=pltpu.SMEM),
            pl.BlockSpec(memory_space=pl.ANY),
            pl.BlockSpec(memory_space=pl.ANY),
            pl.BlockSpec(memory_space=pltpu.VMEM),
        ],
        out_specs=pl.BlockSpec(memory_space=pltpu.VMEM),
        scratch_shapes=[
            pltpu.VMEM((SLOTS, high_dev, 1, TOP * ROWS * LANES), jnp.bfloat16),
            pltpu.VMEM(words.shape, jnp.int32),
            pltpu.VMEM((rest // GROUP, TOP // 2, high_dev, LANES), jnp.int32),
            pltpu.VMEM((high_dev, high_dev), jnp.bfloat16),
            pltpu.VMEM((TOP, ROWS * (high_dev + 1), LANES), jnp.float32),
            pltpu.VMEM((TOP, ROWS * (high_dev + 1), LANES), jnp.float32),
            pltpu.VMEM((HALVED, 2 * GROUP, high_dev, NLOW), jnp.bfloat16),
            pltpu.VMEM((HALVED, 2 * GROUP, high_dev, NLOW), jnp.bfloat16),
            pltpu.VMEM((HALVED, groups, points), jnp.int32),
            pltpu.VMEM((HALVED * groups, NLOW, points), jnp.bfloat16),
            pltpu.VMEM((HALVED * groups, 24, points), jnp.float32),
            pltpu.VMEM((HALVED * groups, PACK, points), jnp.float32),
            pltpu.VMEM((HALVED, groups, points), jnp.float32),
            pltpu.SemaphoreType.DMA((SLOTS, TOP)),
            pltpu.SemaphoreType.DMA,
        ],
        compiler_params=pltpu.CompilerParams(vmem_limit_bytes=63 * 1024 * 1024),
        cost_estimate=pl.CostEstimate(
            flops=4 * NLOW * high_dev * NMID * NLOW, bytes_accessed=4 * gradients.size, transcendentals=0
        ),
        name="sketch",
    )(place, grads, words, sub_index.reshape(kept // LANES, LANES))


def swapped(value, axis, size, bits):
    return lax.ppermute(value, axis, [(i, i ^ bits) for i in range(size)])


def score_kernel(*refs, scale):
    *sketches, own_tests, near_tests, out_ref, lines = refs
    for n, sketch in enumerate(sketches):
        whole = sketch[...].astype(jnp.float32)
        for row in range(whole.shape[0]):
            lines[n : n + 1, row * LANES : (row + 1) * LANES] = whole[row : row + 1, :]
    left = lines[...].astype(jnp.bfloat16)
    for n, tests in enumerate([own_tests] + [near_tests.at[s] for s in range(near_tests.shape[0])]):
        found = lax.dot_general(
            left, tests[...], (((1,), (1,)), ((), ())), preferred_element_type=jnp.float32
        )
        found = found[: len(sketches)] * scale
        out_ref[:, n * tests.shape[0] : (n + 1) * tests.shape[0]] = found


def scores_of(sketches, own_tests, near_tests, scale):
    tests, kept = own_tests.shape
    count = len(sketches)
    return pl.pallas_call(
        functools.partial(score_kernel, scale=scale),
        out_shape=jax.ShapeDtypeStruct((count, tests * (1 + near_tests.shape[0])), jnp.float32),
        scratch_shapes=[pltpu.VMEM((16, kept), jnp.float32)],
        compiler_params=pltpu.CompilerParams(vmem_limit_bytes=32 * 1024 * 1024),
        name="scores",
    )(*sketches, own_tests, near_tests)


def on_device(gradients, sign_words, sub_index, test_sketch, *, mesh):
    feat_size, far_size, near_size = (mesh.shape[axis] for axis in ("feat", "far", "near"))
    local_features = gradients.shape[1]
    kept = sub_index.shape[0]
    tests = test_sketch.shape[0]
    high_dev = local_features // (NMID * NLOW)
    feature_scale = float(local_features * feat_size) ** (-0.5)
    score_scale = float(kept) ** (-0.5)
    place = lax.axis_index("feat").astype(jnp.int32).reshape(1)
    near_tests = jnp.stack([swapped(test_sketch, "near", near_size, s) for s in range(1, near_size)])
    shares = partial_sketch(gradients, sign_words, sub_index, place, high_dev, feature_scale)
    sketch = shares
    for s in range(1, feat_size):
        sketch = sketch + swapped(shares, "feat", feat_size, s)
    sketch = sketch.astype(jnp.bfloat16)
    sketches = [sketch] + [swapped(sketch, "far", far_size, s) for s in range(1, far_size)]
    scores = scores_of(sketches, test_sketch, near_tests, score_scale)
    scores = jnp.stack(
        [scores[:1]] + [swapped(scores[s : s + 1], "far", far_size, s) for s in range(1, far_size)]
    )
    scores = scores.reshape(far_size, near_size, tests)
    far, near = lax.axis_index("far"), lax.axis_index("near")
    for b in range(near_size.bit_length() - 1):
        split = scores.reshape(far_size, -1, 2, 1 << b, tests)
        scores = jnp.where(jnp.bitwise_and(near, 1 << b) != 0, split[:, :, ::-1], split)
    for b in range(far_size.bit_length() - 1):
        split = scores.reshape(-1, 2, 1 << b, near_size, tests)
        scores = jnp.where(jnp.bitwise_and(far, 1 << b) != 0, split[:, ::-1], split)
    return scores.reshape(1, -1)


def solution(mesh):
    feat_size, ex_size = mesh.shape["feat"], mesh.shape["ex"]
    far_size = min(4, ex_size)
    mesh = Mesh(mesh.devices.reshape(feat_size, far_size, ex_size // far_size), ("feat", "far", "near"))
    ex = ("far", "near")
    return jax.shard_map(
        functools.partial(on_device, mesh=mesh),
        mesh=mesh,
        in_specs=(P(ex, "feat"), P("feat"), P(), P(ex, None)),
        out_specs=P(ex, None),
        check_vma=False,
    )
```

```python
import functools

import jax
import jax.numpy as jnp
from jax import lax
from jax.experimental import pallas as pl
from jax.experimental.pallas import tpu as pltpu
from jax.sharding import Mesh, PartitionSpec as P

NMID = 256
NLOW = 256
TOP = 8
GROUP = 8
STEP = 4
SLOTS = 2
CUTS = 4
ROWS = 2 * STEP
HALVED = TOP // 2
LANES = 128
PACK = 16
PAIR = 4


def odd_common_bits(left, right):
    return jnp.bitwise_and(lax.population_count(jnp.bitwise_and(left, right)), 1) == 1


def iota(shape, axis):
    return lax.broadcasted_iota(jnp.int32, shape, axis)


def sketch_kernel(
    place_ref, grads, words, sub_ref, out_ref,
    xbuf, wbuf, wpair, table, ybuf0, ybuf1, tbuf0, tbuf1, entries, weights, signs, acc, found_rows, sems, wsem,
    *, high_dev, scale,
):
    high_parts = out_ref.shape[0] * LANES // TOP // high_dev
    rest = NMID // TOP
    chunks = rest // GROUP
    steps = rest // STEP
    groups = high_dev // PACK
    points = entries.shape[2]
    pairs = HALVED * groups
    rounds = GROUP * TOP // PAIR
    highs = high_dev * PAIR // (STEP * TOP)
    stride = high_dev + 1
    ybuf = (ybuf0, ybuf1)
    tbuf = (tbuf0, tbuf1)

    def grad_copies(step, start):
        slot = step % SLOTS
        part = high_dev // CUTS
        for cut in range(CUTS):
            for top in range(TOP):
                copy = pltpu.make_async_copy(
                    grads.at[cut * part : (cut + 1) * part, top, step],
                    xbuf.at[
                        slot,
                        cut * part : (cut + 1) * part,
                        :,
                        top * ROWS * LANES : (top + 1) * ROWS * LANES,
                    ],
                    sems.at[slot, cut, top],
                )
                if start:
                    copy.start(priority=top % 2)
                else:
                    copy.wait()

    per_high = NMID * NLOW // 16 // LANES
    word_copy = pltpu.make_async_copy(words, wbuf, wsem)
    word_copy.start()
    for step in range(SLOTS):
        grad_copies(step, True)

    table[...] = jnp.where(
        odd_common_bits(iota(table.shape, 0), iota(table.shape, 1)), -1.0, 1.0
    ).astype(jnp.bfloat16)
    acc[...] = jnp.zeros_like(acc)
    lane = iota((groups, LANES), 1)
    for j in range(HALVED):
        spot = (lane // 2 % PACK) * TOP + 2 * j + lane % 2
        for part in range(points // LANES):
            line = jnp.zeros((groups, LANES), jnp.int32)
            for n in range(LANES // (2 * PACK)):
                hi = part * (LANES // (2 * PACK)) + n
                rows = sub_ref[hi * groups : (hi + 1) * groups, :]
                taken = jnp.take_along_axis(rows, spot, axis=1, mode="promise_in_bounds")
                line = jnp.where(lane // (2 * PACK) == n, taken, line)
            entries[j, :, part * LANES : (part + 1) * LANES] = line

    def build(e):
        entry = entries[e // groups, pl.ds(e % groups, 1), :]
        row = iota((24, points), 0)
        mask = jnp.where(
            row < 2 * GROUP,
            jnp.bitwise_or(jnp.left_shift(row % GROUP, 8), jnp.left_shift(row // GROUP, 13)),
            jnp.left_shift(row - 2 * GROUP, 11),
        )
        signs[e] = jnp.where(odd_common_bits(entry, mask), -1.0, 1.0)
        weights[e] = jnp.where(
            odd_common_bits(entry, iota((NLOW, points), 0)), -1.0, 1.0
        ).astype(jnp.bfloat16)

    word_copy.wait()

    def pair_words(c, n):
        for pair in range(TOP // 2):
            one, two = (
                wbuf[pl.ds(n * 8 * per_high + (2 * pair + which) * chunks + c, 8, per_high), :]
                for which in range(2)
            )
            wpair[c, pair, pl.ds(pl.multiple_of(n * 8, 8), 8), :] = jnp.bitwise_or(
                one, jnp.left_shift(two, 16)
            )

    @pl.loop(0, high_dev // 32)
    def _(n):
        for m in range(4):
            pair_words(0, 4 * n + m)

    def prepare(step, u, part, parts):
        slot = step % SLOTS
        chunk = step * STEP // GROUP
        lane8 = iota((ROWS, LANES), 1)
        bits = [jnp.left_shift(1, lane8 % 16), jnp.left_shift(1, lane8 % 16 + 16)]
        spot = step % (GROUP // STEP) * (16 * STEP) + iota((ROWS, LANES), 0) * 8 + lane8 // 16
        for n in range(part * highs // parts, (part + 1) * highs // parts):
            h = u * highs + n
            values = []
            for pair in range(TOP // 2):
                word = jnp.broadcast_to(wpair[chunk, pair, pl.ds(h, 1), :], (ROWS, LANES))
                word = jnp.take_along_axis(word, spot, axis=1, mode="promise_in_bounds")
                two = xbuf[slot, h, :, 2 * pair * ROWS * LANES : 2 * (pair + 1) * ROWS * LANES]
                two = two.reshape(2 * ROWS, LANES).astype(jnp.float32)
                for which in range(2):
                    value = two[which * ROWS : (which + 1) * ROWS]
                    values.append(jnp.where(jnp.bitwise_and(word, bits[which]) != 0, value, -value))
            for reach in (2, 4):
                nxt = list(values)
                for at in range(TOP):
                    if not at & reach:
                        nxt[at] = values[at] + values[at + reach]
                        nxt[at + reach] = values[at] - values[at + reach]
                values = nxt
            for top in range(TOP):
                ybuf[step % 2][top, pl.ds(h, ROWS, stride), :] = values[top]

    def transform_high(step, u):
        first, i = u * PAIR % TOP, u * PAIR // TOP
        columns = [
            ybuf[step % 2][first + n, pl.ds((2 * i + l_hi) * stride, high_dev), :].astype(jnp.bfloat16)
            for n in range(PAIR)
            for l_hi in range(2)
        ]
        result = jnp.dot(
            table[...], jnp.concatenate(columns, axis=1), preferred_element_type=jnp.float32
        ).astype(jnp.bfloat16)
        chunk = step * STEP // GROUP
        row = step % (GROUP // STEP) * STEP + i
        for n in range(PAIR):
            top = first + n
            tbuf[chunk % 2][top // 2, n % 2 * GROUP + row] = result[:, n * NLOW : (n + 1) * NLOW]

    def evaluate(chunk, e):
        j, g = e // groups, e % groups
        block = tbuf[chunk % 2][j, :, pl.ds(pl.multiple_of(g * PACK, PACK), PACK), :]
        found = jnp.dot(
            block.reshape(2 * GROUP * PACK, NLOW), weights[e], preferred_element_type=jnp.float32
        )
        total = found[:PACK] * signs[e, 0:1, :]
        for n in range(1, 2 * GROUP):
            total += found[n * PACK : (n + 1) * PACK] * signs[e, n : n + 1, :]
        acc[e] += total * signs[e, 2 * GROUP + chunk : 2 * GROUP + chunk + 1, :]

    def some_pairs(n, part, do):
        if pairs >= PAIR * rounds:
            for m in range(pairs // (PAIR * rounds)):
                do((n * PAIR + part) * (pairs // (PAIR * rounds)) + m)
        elif part % (PAIR * rounds // pairs) == 0:
            do((n * PAIR + part) // (PAIR * rounds // pairs))

    turns = STEP * TOP // PAIR
    per_chunk = GROUP // STEP

    grad_copies(0, False)

    @pl.loop(0, turns)
    def _(u):
        prepare(0, u, 0, 1)

    for step in range(steps):
        if step + SLOTS < steps:
            grad_copies(step + SLOTS, True)
        if step + 1 < steps:
            grad_copies(step + 1, False)

        @pl.loop(0, turns)
        def _(u):
            later, part, parts = {0: (1, 0, 1), 1: (2, 0, 2), 2: (2, 1, 2), 3: (3, 0, 2), 4: (3, 1, 2)}.get(
                step, (chunks, 0, 1)
            )
            if later < chunks:
                count = high_dev // 8 // parts // turns
                for m in range(count):
                    pair_words(later, (part * turns + u) * count + m)
            for part in range(PAIR):
                if step >= per_chunk:
                    some_pairs(
                        step % per_chunk * turns + u,
                        part,
                        functools.partial(evaluate, step // per_chunk - 1),
                    )
                else:
                    some_pairs(step * turns + u, part, build)
            transform_high(step, u)
            if step + 1 < steps:
                prepare(step + 1, u, 0, 1)

    @pl.loop(0, pairs)
    def _(e):
        evaluate(chunks - 1, e)
        own = iota((PACK, points), 1) // 2 % PACK == iota((PACK, points), 0)
        found_rows[e // groups, pl.ds(e % groups, 1), :] = jnp.sum(
            jnp.where(own, acc[e], 0.0), axis=0, keepdims=True
        )

    place = place_ref[0]
    for hi in range(high_parts):
        common = jnp.bitwise_and(place, hi)
        odd = jnp.bitwise_and(common ^ (common >> 1) ^ (common >> 2) ^ (common >> 3), 1)
        sign = jnp.where(odd == 1, -scale, scale)
        part, first = divmod(hi * 2 * PACK, LANES)
        spot = first + lane // TOP * 2 + lane % 2
        line = jnp.zeros((groups, LANES), jnp.float32)
        for j in range(HALVED):
            rows = found_rows[j, :, part * LANES : (part + 1) * LANES]
            taken = jnp.take_along_axis(rows, spot, axis=1, mode="promise_in_bounds")
            line = jnp.where(lane % TOP // 2 == j, taken, line)
        out_ref[hi * groups : (hi + 1) * groups, :] = line * sign


def partial_sketch(gradients, sign_words, sub_index, place, high_dev, scale):
    kept = sub_index.shape[0]
    rest = NMID // TOP
    groups = high_dev // PACK
    points = kept // (HALVED * groups)
    grads = gradients.reshape(high_dev, TOP, rest // STEP, 1, ROWS * LANES)
    words = sign_words.reshape(-1, LANES)
    return pl.pallas_call(
        functools.partial(sketch_kernel, high_dev=high_dev, scale=scale),
        out_shape=jax.ShapeDtypeStruct((kept // LANES, LANES), jnp.float32),
        in_specs=[
            pl.BlockSpec(memory_space=pltpu.SMEM),
            pl.BlockSpec(memory_space=pl.ANY),
            pl.BlockSpec(memory_space=pl.ANY),
            pl.BlockSpec(memory_space=pltpu.VMEM),
        ],
        out_specs=pl.BlockSpec(memory_space=pltpu.VMEM),
        scratch_shapes=[
            pltpu.VMEM((SLOTS, high_dev, 1, TOP * ROWS * LANES), jnp.bfloat16),
            pltpu.VMEM(words.shape, jnp.int32),
            pltpu.VMEM((rest // GROUP, TOP // 2, high_dev, LANES), jnp.int32),
            pltpu.VMEM((high_dev, high_dev), jnp.bfloat16),
            pltpu.VMEM((TOP, ROWS * (high_dev + 1), LANES), jnp.float32),
            pltpu.VMEM((TOP, ROWS * (high_dev + 1), LANES), jnp.float32),
            pltpu.VMEM((HALVED, 2 * GROUP, high_dev, NLOW), jnp.bfloat16),
            pltpu.VMEM((HALVED, 2 * GROUP, high_dev, NLOW), jnp.bfloat16),
            pltpu.VMEM((HALVED, groups, points), jnp.int32),
            pltpu.VMEM((HALVED * groups, NLOW, points), jnp.bfloat16),
            pltpu.VMEM((HALVED * groups, 24, points), jnp.float32),
            pltpu.VMEM((HALVED * groups, PACK, points), jnp.float32),
            pltpu.VMEM((HALVED, groups, points), jnp.float32),
            pltpu.SemaphoreType.DMA((SLOTS, CUTS, TOP)),
            pltpu.SemaphoreType.DMA,
        ],
        compiler_params=pltpu.CompilerParams(vmem_limit_bytes=63 * 1024 * 1024),
        cost_estimate=pl.CostEstimate(
            flops=4 * NLOW * high_dev * NMID * NLOW, bytes_accessed=4 * gradients.size, transcendentals=0
        ),
        name="sketch",
    )(place, grads, words, sub_index.reshape(kept // LANES, LANES))


def swapped(value, axis, size, bits):
    return lax.ppermute(value, axis, [(i, i ^ bits) for i in range(size)])


def score_kernel(*refs, scale):
    *sketches, own_tests, near_tests, out_ref, lines = refs
    for n, sketch in enumerate(sketches):
        whole = sketch[...].astype(jnp.float32)
        for row in range(whole.shape[0]):
            lines[n : n + 1, row * LANES : (row + 1) * LANES] = whole[row : row + 1, :]
    left = lines[...].astype(jnp.bfloat16)
    for n, tests in enumerate([own_tests] + [near_tests.at[s] for s in range(near_tests.shape[0])]):
        found = lax.dot_general(
            left, tests[...], (((1,), (1,)), ((), ())), preferred_element_type=jnp.float32
        )
        found = found[: len(sketches)] * scale
        out_ref[:, n * tests.shape[0] : (n + 1) * tests.shape[0]] = found


def scores_of(sketches, own_tests, near_tests, scale):
    tests, kept = own_tests.shape
    count = len(sketches)
    return pl.pallas_call(
        functools.partial(score_kernel, scale=scale),
        out_shape=jax.ShapeDtypeStruct((count, tests * (1 + near_tests.shape[0])), jnp.float32),
        scratch_shapes=[pltpu.VMEM((16, kept), jnp.float32)],
        compiler_params=pltpu.CompilerParams(vmem_limit_bytes=32 * 1024 * 1024),
        name="scores",
    )(*sketches, own_tests, near_tests)


def on_device(gradients, sign_words, sub_index, test_sketch, *, mesh):
    feat_size, far_size, near_size = (mesh.shape[axis] for axis in ("feat", "far", "near"))
    local_features = gradients.shape[1]
    kept = sub_index.shape[0]
    tests = test_sketch.shape[0]
    high_dev = local_features // (NMID * NLOW)
    feature_scale = float(local_features * feat_size) ** (-0.5)
    score_scale = float(kept) ** (-0.5)
    place = lax.axis_index("feat").astype(jnp.int32).reshape(1)
    near_tests = jnp.stack([swapped(test_sketch, "near", near_size, s) for s in range(1, near_size)])
    shares = partial_sketch(gradients, sign_words, sub_index, place, high_dev, feature_scale)
    sketch = shares
    for s in range(1, feat_size):
        sketch = sketch + swapped(shares, "feat", feat_size, s)
    sketch = sketch.astype(jnp.bfloat16)
    sketches = [sketch] + [swapped(sketch, "far", far_size, s) for s in range(1, far_size)]
    scores = scores_of(sketches, test_sketch, near_tests, score_scale)
    scores = jnp.stack(
        [scores[:1]] + [swapped(scores[s : s + 1], "far", far_size, s) for s in range(1, far_size)]
    )
    scores = scores.reshape(far_size, near_size, tests)
    far, near = lax.axis_index("far"), lax.axis_index("near")
    for b in range(near_size.bit_length() - 1):
        split = scores.reshape(far_size, -1, 2, 1 << b, tests)
        scores = jnp.where(jnp.bitwise_and(near, 1 << b) != 0, split[:, :, ::-1], split)
    for b in range(far_size.bit_length() - 1):
        split = scores.reshape(-1, 2, 1 << b, near_size, tests)
        scores = jnp.where(jnp.bitwise_and(far, 1 << b) != 0, split[:, ::-1], split)
    return scores.reshape(1, -1)


def solution(mesh):
    feat_size, ex_size = mesh.shape["feat"], mesh.shape["ex"]
    far_size = min(4, ex_size)
    mesh = Mesh(mesh.devices.reshape(feat_size, far_size, ex_size // far_size), ("feat", "far", "near"))
    ex = ("far", "near")
    return jax.shard_map(
        functools.partial(on_device, mesh=mesh),
        mesh=mesh,
        in_specs=(P(ex, "feat"), P("feat"), P(), P(ex, None)),
        out_specs=P(ex, None),
        check_vma=False,
    )
```
